256 devices in a mesh: lat: 8 (over z_hi, y), lon: 32 (over z_lo, x, core).
Axes of the slice: x: 4, y: 4, z: 8 (z_hi: 2, z_lo: 4; z = z_hi * 4 + z_lo), core: 2. Of those that a mesh axis runs over, the one named last changes fastest.
Arguments:
- latent_field: bfloat16 [96, 1536, 512], P('lat', 'lon'), may hold values from -6 to 6
- surface: int32 [96, 1536], P('lat', 'lon'), may hold values from 0 to 2
- surface_table: float32 [3, 512], replicated, may hold values from -3 to 3
- shifts: int32 [2], replicated, may hold values from 1 to 11, as said below
- gain_attn_one: float32 [512], replicated, may hold values from 0.5 to 1.5
- inward_one: bfloat16 [512, 1536], replicated, may hold values from -5 to 5
- outward_one: bfloat16 [512, 512], replicated, may hold values from -0.25 to 0.25
- gain_ffn: float32 [512], replicated, may hold values from 0.5 to 1.5
- ffn_up: bfloat16 [512, 2048], replicated, may hold values from -0.25 to 0.25
- ffn_down: bfloat16 [2048, 512], replicated, may hold values from -0.125 to 0.125
- gain_merge: float32 [2048], replicated, may hold values from 0.5 to 1.5
- merge_proj: bfloat16 [2048, 1024], P('lat', 'lon'), may hold values from -0.125 to 0.125
- gain_two: float32 [1024], replicated, may hold values from 0.5 to 1.5
- inward_two: bfloat16 [1024, 3072], P('lat', 'lon'), may hold values from -5 to 5
- outward_two: bfloat16 [1024, 1024], P('lat', 'lon'), may hold values from -0.1875 to 0.1875
Outputs:
- level_one: bfloat16 [96, 1536, 512], P('lat', 'lon')
- level_two: bfloat16 [48, 768, 1024], P('lat', 'lon')
The draws below stay inside these ranges and needn't reach their ends.
Inputs may be any that keep to these rules, and one draw needn't show every extreme that they name: shifts[0] lies in 1 to 5; shifts[1] is 11. `surface`: 0 sea, 1 land, 2 sea ice.
All inputs are finite; a program needn't handle non-finite values.
Results may differ from the reference program's by a relative error of at most 0.015.
Values may be sent and summed in bfloat16 or wider, within the bound.
No kernel may reach another device: no remote copies, remote signals or barrier semaphores. Data moves between devices by JAX's collectives and lax.ppermute only.
A program may use at most 128 MiB of HBM per device.

```python
import jax
import jax.numpy as jnp
from jax import lax

D1 = 512
D2 = 1024
FF1 = 2048
HEADS1 = 8
HEADS2 = 16
WH = 6
WW = 12
NLAT = 96
NLON = 1536


def draw_shifts(key, part):
    key = jax.random.fold_in(key, 7)
    lat_part = jax.random.randint(key, (1,), 1, WH)
    lon_part = jnp.full((1,), WW - 1, jnp.int32)
    return jnp.concatenate([lat_part.astype(jnp.int32), lon_part]).astype(jnp.int32)


def drawn_weight(key, row_count, col_count):
    values = jax.random.normal(key, (row_count, col_count), jnp.float32)
    return jnp.clip(values, -4.0, 4.0) * row_count ** (-0.5)


def draw_inward_one(key, part):
    key = jax.random.fold_in(key, 11)
    return drawn_weight(key, D1, 3 * D1).astype(jnp.bfloat16)


def draw_inward_two(key, part):
    key = jax.random.fold_in(key, 13)
    return drawn_weight(key, D2, 3 * D2).astype(jnp.bfloat16)


def with_ends(values, stream_key, least, high):
    extent = values.shape
    spot = [jax.random.randint(jax.random.fold_in(stream_key, axis), (), 0, extent[axis]) for axis in range(len(extent))]
    values = values.at[tuple(spot)].set(least)
    longest = extent.index(max(extent))
    spot[longest] = (spot[longest] + 1) % extent[longest]
    return values.at[tuple(spot)].set(high)


def steps_of(key, extent, cuts, smallest, largest):
    level, own = 1.0, jax.random.fold_in(key, 6)
    for position, blocks in cuts:
        draws = jnp.exp(jax.random.uniform(jax.random.fold_in(own, position), (blocks,), jnp.float32, smallest / len(cuts), largest / len(cuts)))
        level = level * jnp.repeat(draws, extent[position] // blocks).reshape([-1 if axis == position else 1 for axis in range(len(extent))])
    return level


def bell_draw(rng, extent, spread, bound, shards=(), held_as=jnp.bfloat16):
    entries = jax.random.normal(rng, extent, jnp.float32) * spread
    if len(shards) > 0:
        entries = steps_of(rng, extent, shards, -0.22, 0.18) * entries
    return jnp.clip(entries, min=-bound, max=bound).astype(held_as)


def setup_inputs(seed: int = 0) -> dict:
    splits = jax.random.split(jax.random.key(seed), 16)
    return {
        "latent_field": bell_draw(splits[0], (NLAT, NLON, D1), 1.0, 6.0, ((0, 8), (1, 32))),
        "surface": with_ends(jax.random.randint(splits[1], (NLAT, NLON), 0, 3), jax.random.fold_in(splits[1], 1), 0, 2).astype(jnp.int32),
        "surface_table": bell_draw(splits[2], (3, D1), 0.5, 3.0, (), jnp.float32),
        "shifts": draw_shifts(jax.random.fold_in(splits[15], 71), 0),
        "gain_attn_one": jnp.clip(1.0 + 0.1 * jax.random.normal(splits[4], (D1,), jnp.float32), 0.5, 1.5),
        "inward_one": draw_inward_one(jax.random.fold_in(splits[15], 71), 0),
        "outward_one": bell_draw(splits[6], (D1, D1), D1 ** -0.5, 0.25),
        "gain_ffn": jnp.clip(1.0 + 0.1 * jax.random.normal(splits[7], (D1,), jnp.float32), 0.5, 1.5),
        "ffn_up": bell_draw(splits[8], (D1, FF1), D1 ** -0.5, 0.25),
        "ffn_down": bell_draw(splits[9], (FF1, D1), FF1 ** -0.5, 0.125),
        "gain_merge": jnp.clip(1.0 + 0.1 * jax.random.normal(splits[10], (4 * D1,), jnp.float32), 0.5, 1.5),
        "merge_proj": bell_draw(splits[11], (4 * D1, D2), (4 * D1) ** -0.5, 0.125, ((0, 8), (1, 32))),
        "gain_two": jnp.clip(1.0 + 0.1 * jax.random.normal(splits[12], (D2,), jnp.float32), 0.5, 1.5),
        "inward_two": draw_inward_two(jax.random.fold_in(splits[15], 71), 0),
        "outward_two": bell_draw(splits[14], (D2, D2), D2 ** -0.5, 0.1875, ((0, 8), (1, 32))),
    }


EPS = 1e-05

def matmul(first_op, second_op):
    return jnp.dot(first_op, second_op, preferred_element_type=jnp.float32)

def normed(hidden_in, gain_vec):
    centre = lax.optimization_barrier(jnp.mean(hidden_in, axis=-1, keepdims=True))
    centred = hidden_in - centre
    variance = lax.optimization_barrier(jnp.mean(centred * centred, axis=-1, keepdims=True))
    return centred * lax.rsqrt(variance + EPS) * gain_vec

def by_rows(function, *arrays):
    grouped = tuple((array.reshape((array.shape[0] // WH, WH) + array.shape[1:]) for array in arrays))
    outcome = lax.map(lambda portion: function(*portion), grouped)
    return outcome.reshape((outcome.shape[0] * WH,) + outcome.shape[2:])

def attend(queries, key_val, inside, head_count):
    row_count, col_count, feature = queries.shape
    head_size = feature // head_count
    band_rows = row_count // WH
    band_cols = col_count // WW

    def windows(tensor):
        tensor = tensor.reshape(band_rows, WH, band_cols, WW, head_count, head_size)
        return tensor.transpose(0, 2, 4, 1, 3, 5).reshape(band_rows, band_cols, head_count, WH * WW, head_size).astype(jnp.float32)
    query_win = windows(queries)
    key_win = windows(key_val[..., :feature])
    value_win = windows(key_val[..., feature:])
    key_mask = jnp.broadcast_to(inside.reshape(band_rows, WH, 1), (band_rows, WH, WW)).reshape(band_rows, WH * WW)
    key_mask = key_mask[:, None, None, None, :]
    scores = jnp.einsum('abhqd,abhkd->abhqk', query_win, key_win) * head_size ** (-0.5)
    scores = jnp.where(key_mask, scores, -1000000000.0)
    row_max = lax.optimization_barrier(jnp.max(scores, axis=-1, keepdims=True))
    weights_exp = jnp.exp(scores - row_max)
    weights_bf = (weights_exp / lax.optimization_barrier(jnp.sum(weights_exp, axis=-1, keepdims=True))).astype(jnp.bfloat16)
    outcome = jnp.einsum('abhqk,abhkd->abhqd', weights_bf.astype(jnp.float32), value_win).astype(jnp.bfloat16)
    outcome = outcome.reshape(band_rows, band_cols, head_count, WH, WW, head_size)
    return outcome.transpose(0, 3, 1, 4, 2, 5).reshape(row_count, col_count, feature)

def shifted_attention(packed, shifts, head_count):
    lat_cells, lon_cells, packed_width = packed.shape
    feature = packed_width // 3
    lat_shift = shifts[0]
    lon_shift = shifts[1]
    anchor = jnp.int32(0)
    rolled = jnp.roll(packed, -lon_shift, axis=1)
    padded = jnp.pad(rolled, ((WH, WH), (0, 0), (0, 0)))
    win_rows = lat_cells + WH
    band = lax.dynamic_slice(padded, (lat_shift, anchor, anchor), (win_rows, lon_cells, packed_width))
    band_count = win_rows // WH
    band = band.reshape(band_count, WH, lon_cells, packed_width)

    def per_band(window_row):
        one_band = lax.dynamic_index_in_dim(band, window_row, 0, keepdims=False)
        ext_row = lat_shift + window_row * WH + jnp.arange(WH, dtype=jnp.int32)
        inside = (ext_row >= WH) & (ext_row < WH + lat_cells)
        return attend(one_band[..., :feature], one_band[..., feature:], inside, head_count)
    outcome = lax.map(per_band, jnp.arange(band_count, dtype=jnp.int32))
    outcome = outcome.reshape(win_rows, lon_cells, feature)
    own_part = lax.dynamic_slice(outcome, (WH - lat_shift, anchor, anchor), (lat_cells, lon_cells, feature))
    return jnp.roll(own_part, lon_shift, axis=1)

def attention_level(residual, gain_vec, inward, outward, shifts, head_count):
    packed = by_rows(lambda portion: matmul(normed(portion, gain_vec).astype(jnp.bfloat16), inward).astype(jnp.bfloat16), residual)
    attended = shifted_attention(packed, shifts, head_count)
    return by_rows(lambda resid_part, attn_part: resid_part + matmul(attn_part, outward), residual, attended)

def pair_up(grid):
    lat_cells, lon_cells, feature = grid.shape
    grid = grid.reshape(lat_cells // 2, 2, lon_cells // 2, 2, feature)
    return grid.transpose(0, 2, 3, 1, 4).reshape(lat_cells // 2, lon_cells // 2, 4 * feature)

def reference(latent_field, surface, surface_table, shifts, gain_attn_one, inward_one, outward_one, gain_ffn, ffn_up, ffn_down, gain_merge, merge_proj, gain_two, inward_two, outward_two):
    residual = latent_field.astype(jnp.float32) + surface_table[surface]
    residual = attention_level(residual, gain_attn_one, inward_one, outward_one, shifts, HEADS1)

    def feed(portion):
        hidden = jax.nn.gelu(matmul(normed(portion, gain_ffn).astype(jnp.bfloat16), ffn_up)).astype(jnp.bfloat16)
        return (portion + matmul(hidden, ffn_down)).astype(jnp.bfloat16)
    level_one = by_rows(feed, residual)
    merged = pair_up(level_one)

    def squeeze(portion):
        return matmul(normed(portion.astype(jnp.float32), gain_merge).astype(jnp.bfloat16), merge_proj).astype(jnp.bfloat16)
    reduced = by_rows(squeeze, merged)
    level_two = attention_level(reduced.astype(jnp.float32), gain_two, inward_two, outward_two, shifts, HEADS2).astype(jnp.bfloat16)
    return (level_one, level_two)
```

```python
import jax
import jax.numpy as jnp
from jax import lax
from jax.experimental import pallas as pl
from jax.experimental.pallas import tpu as pltpu
from jax.sharding import PartitionSpec as P

EPS = 1e-05
BF = jnp.bfloat16
F32 = jnp.float32
AXES = ("lat", "lon")
VMEM = pl.BlockSpec(memory_space=pltpu.VMEM)
SMEM = pl.BlockSpec(memory_space=pltpu.SMEM)
ANY = pl.BlockSpec(memory_space=pl.ANY)
LIMIT = 56 * 1024 * 1024

PLACES = [(x, y, z, c) for z in range(8) for y in range(4) for x in range(4) for c in range(2)]


def number(x, y, z, c):
    x, y, z, c = x % 4, y % 4, z % 8, c % 2
    return ((z // 4) * 4 + y) * 32 + ((z % 4) * 4 + x) * 2 + c


def move(array, dx=0, dy=0, dz=0, dc=0):
    pairs = [
        (number(x, y, z, c), number(x + dx, y + dy, z + dz, c + dc)) for x, y, z, c in PLACES
    ]
    return lax.ppermute(array, AXES, pairs)


def to_cell(array, dlat, dlon):
    pairs = [
        (i * 32 + j, ((i + dlat) % 8) * 32 + (j + dlon) % 32) for i in range(8) for j in range(32)
    ]
    return lax.ppermute(array, AXES, pairs)


def after(value, *others):
    return lax.optimization_barrier((value,) + others)[0]


def pack_kernel(merge_ref, inward_ref, outward_ref, out_ref):
    out_ref[0:32] = merge_ref[:, :128]
    out_ref[32:64] = merge_ref[:, 128:]
    out_ref[64:96] = outward_ref[...]
    out_ref[96:192] = inward_ref[...]


def pack(merge, inward, outward):
    return pl.pallas_call(
        pack_kernel,
        out_shape=jax.ShapeDtypeStruct((192, 128), BF),
        in_specs=[VMEM] * 3,
        out_specs=VMEM,
        name="pack",
    )(merge.T, inward.T, outward.T)


def assemble_z_kernel(place_ref, *refs):
    pieces, (first_ref, second_ref, sem) = refs[:8], refs[8:]
    z = place_ref[2]
    copies = []
    for step, piece in enumerate(pieces):
        to = lax.rem(z + step, 8)
        for rows, out in ((slice(0, 96), first_ref), (slice(96, 192), second_ref)):
            copies.append(pltpu.make_async_copy(piece.at[rows], out.at[to], sem.at[len(copies)]))
    for copy in copies:
        copy.start()
    for copy in copies:
        copy.wait()


def assemble_z(place, *pieces):
    return pl.pallas_call(
        assemble_z_kernel,
        out_shape=[jax.ShapeDtypeStruct((8, 96, 128), BF)] * 2,
        in_specs=[SMEM] + [ANY] * 8,
        out_specs=[VMEM] * 2,
        scratch_shapes=[pltpu.SemaphoreType.DMA((16,))],
        name="assemble_z",
    )(place, *pieces)


def assemble_kernel(place_ref, *refs):
    out_first, out_second, sem = refs[10:]
    copies = []
    for part in range(2):
        at = place_ref[1 - part]
        for piece, step, lo, hi in zip(
            refs[part * 5 : part * 5 + 5], (0, 3, 1, 2, 2), (0, 0, 0, 0, 4), (8, 8, 8, 4, 8)
        ):
            index = lax.rem(at + step, 4)
            target = out_second.at[lo:hi, index] if part else out_first.at[index, lo:hi]
            copies.append(pltpu.make_async_copy(piece, target, sem.at[len(copies)]))
    for copy in copies:
        copy.start()
    for copy in copies:
        copy.wait()


def assemble(place, first, second):
    return pl.pallas_call(
        assemble_kernel,
        out_shape=[
            jax.ShapeDtypeStruct((4, 8, 96, 128), BF),
            jax.ShapeDtypeStruct((8, 4, 96, 128), BF),
        ],
        in_specs=[SMEM] + [ANY] * 10,
        out_specs=[VMEM] * 2,
        scratch_shapes=[pltpu.SemaphoreType.DMA((10,))],
        name="assemble",
    )(place, *first, *second)


def normed(hidden, gain):
    centre = jnp.mean(hidden, axis=-1, keepdims=True)
    centred = hidden - centre
    variance = jnp.mean(centred * centred, axis=-1, keepdims=True)
    return centred * lax.rsqrt(variance + EPS) * gain


def dot(a, b):
    return jnp.dot(a, b, preferred_element_type=F32)


def dot_nt(a, b):
    return lax.dot_general(a, b, (((1,), (1,)), ((), ())), preferred_element_type=F32)


def window_mask(split, edge):
    def code(axis):
        token = lax.broadcasted_iota(jnp.int32, (144, 144), axis)
        row = (token * 2731) >> 16
        col = token - 24 * row
        return jnp.where(col >= 12, 1, 0) + jnp.where(row >= split, 2, 0) * edge

    return code(0) == code(1)


def attend_pair(queries, keys, values, mask):
    low = lax.broadcasted_iota(jnp.int32, (144, 128), 1) < 64
    zero = jnp.zeros_like(queries)
    both = jnp.concatenate([jnp.where(low, queries, zero), jnp.where(low, zero, queries)], axis=0)
    scores = jnp.where(mask, dot_nt(both, keys), -1e9)
    weights = jnp.exp(scores - jnp.max(scores, axis=-1, keepdims=True))
    total = jnp.sum(weights, axis=-1, keepdims=True)
    mixed = dot(weights.astype(BF), values) * (1.0 / total)
    return jnp.where(low, mixed[:144], mixed[144:])


def fill(ext, above_ref, own_ref, below_ref):
    for row in range(3):
        ext[row] = above_ref[row]
        ext[15 + row] = below_ref[row]
    for row in range(12):
        ext[3 + row] = own_ref[row]


def level_one_kernel(
    place_ref,
    above_ref,
    x_ref,
    below_ref,
    col_ref,
    cls_ref,
    table_ref,
    gain1_ref,
    gain2_ref,
    inward_hbm,
    outward_hbm,
    up_hbm,
    down_hbm,
    out_ref,
    inward,
    outward,
    up,
    down,
    rim,
    residual,
    attended,
    ext,
    sem,
):
    copies = [
        pltpu.make_async_copy(source, target, sem.at[index])
        for index, (source, target) in enumerate(
            ((inward_hbm, inward), (outward_hbm, outward), (up_hbm, up), (down_hbm, down))
        )
    ]
    for copy in copies:
        copy.start()
    lat, shift = place_ref[4], place_ref[5]
    split = jnp.where(shift > 0, 6 - shift, -shift)
    fill(ext, above_ref, x_ref, below_ref)
    for band in range(2):
        for row in range(6):
            frame = band * 6 + row
            rim[row, 8:56] = ext[3 + shift + frame].astype(F32)
            rim[row, 7:8] = col_ref[frame : frame + 1].astype(F32)
            cls = cls_ref[:, frame : frame + 1]
            embedded = jnp.where(
                cls == 0.0, table_ref[0:1], jnp.where(cls == 1.0, table_ref[1:2], table_ref[2:3])
            )
            residual[row * 48 : (row + 1) * 48] = rim[row, 7:55] + embedded
        normal = normed(residual[...], gain1_ref[...]).astype(BF)
        if band == 1:
            edge = jnp.where((lat == 7) & (shift > 0), 1, 0)
        else:
            edge = jnp.where((lat == 0) & (shift < 0), 1, 0)
        mask = window_mask(split, edge)
        mask = jnp.concatenate([mask, mask], axis=0)
        if band == 0:
            copies[0].wait()
        for quarter in range(2):
            at = quarter * 256
            parts = [
                dot(normal, inward[:, part * 512 + at : part * 512 + at + 256]).reshape(6, 48, 256)
                for part in range(3)
            ]
            for pair in range(2):
                lanes = slice(pair * 128, pair * 128 + 128)
                for block in range(2):
                    cols = slice(block * 24, block * 24 + 24)
                    queries, keys, values = (
                        part[:, cols, lanes].reshape(144, 128).astype(BF) for part in parts
                    )
                    mixed = attend_pair(queries * BF(0.125), keys, values, mask)
                    attended[:, cols, at + pair * 128 : at + pair * 128 + 128] = mixed.reshape(
                        6, 24, 128
                    )
        if band == 0:
            copies[1].wait()
        mid = residual[...] + dot(attended[...].reshape(288, 512).astype(BF), outward[...])
        residual[...] = mid
        normal = normed(mid, gain2_ref[...]).astype(BF)
        if band == 0:
            copies[2].wait()
            copies[3].wait()
        for chunk in range(4):
            part = slice(chunk * 512, chunk * 512 + 512)
            hidden = jax.nn.gelu(dot(normal, up[:, part])).astype(BF)
            residual[...] += dot(hidden, down[part])
        out_ref[band * 6 : band * 6 + 6] = residual[...].astype(BF).reshape(6, 48, 512)


def level_one(place, above, x, below, col, cls, table, gain1, gain2, inward, outward, up, down):
    return pl.pallas_call(
        level_one_kernel,
        out_shape=jax.ShapeDtypeStruct((12, 48, 512), BF),
        in_specs=[SMEM] + [VMEM] * 8 + [ANY] * 4,
        out_specs=VMEM,
        scratch_shapes=[
            pltpu.VMEM((512, 1536), BF),
            pltpu.VMEM((512, 512), BF),
            pltpu.VMEM((512, 2048), BF),
            pltpu.VMEM((2048, 512), BF),
            pltpu.VMEM((6, 56, 512), F32),
            pltpu.VMEM((288, 512), F32),
            pltpu.VMEM((6, 48, 512), F32),
            pltpu.VMEM((18, 48, 512), BF),
            pltpu.SemaphoreType.DMA((4,)),
        ],
        compiler_params=pltpu.CompilerParams(vmem_limit_bytes=LIMIT),
        cost_estimate=pl.CostEstimate(
            flops=4_000_000_000, bytes_accessed=8_000_000, transcendentals=3_000_000
        ),
        name="level_one",
    )(place, above, x, below, col, cls, table, gain1, gain2, inward, outward, up, down)


def level_two_kernel(place_ref, above_ref, f_ref, below_ref, col_ref, gain1_ref, gain2_ref, *refs):
    first, second = refs[0:10], refs[10:20]
    out_ref, merge, outward, inward, rim, merged, total, packed, attended, ext, sem = refs[20:]
    x, y, core = place_ref[0], place_ref[1], place_ref[3]
    lat, shift = place_ref[4], place_ref[5]
    waits = {"merge": [], "inward": [], "outward": []}
    count = 0
    jobs = []
    for piece in range(10):
        step = (0, 3, 1, 2, 2)[piece % 5]
        lo, hi = ((0, 4), (0, 4), (0, 4), (0, 2), (2, 4))[piece % 5]
        to_x = lax.rem(x + step, 4)
        to_c = core if piece < 5 else 1 - core
        to = to_x * 2 + to_c
        for section in range(3):
            rows = slice(section * 32, section * 32 + 32)
            target = (merge.at[0], merge.at[1], outward)[section]
            jobs.append(
                (
                    "outward" if section == 2 else "merge",
                    first[piece].at[:, :, rows],
                    target.at[lo:hi, :, to],
                )
            )
        lo, hi = ((0, 8), (0, 8), (0, 8), (0, 4), (4, 8))[piece % 5]
        to_y = lax.rem(y + step, 4)
        jobs.append(("inward", second[piece], inward.at[to_y, lo:hi, :, to_c]))
    for kind in ("merge", "inward", "outward"):
        for job, source, target in jobs:
            if job == kind:
                copy = pltpu.make_async_copy(source, target, sem.at[count])
                copy.start()
                waits[kind].append(copy)
                count += 1

    fill(ext, above_ref, f_ref, below_ref)
    for row in range(12):
        values = ext[3 + shift + row].astype(F32)
        left = col_ref[row : row + 1].astype(F32)
        for quarter in range(4):
            lanes = slice(quarter * 128, quarter * 128 + 128)
            rim[quarter, row, 8:56] = values[:, lanes]
            rim[quarter, row, 7:8] = left[:, lanes]
    for row in range(6):
        for part in range(4):
            for quarter in range(4):
                at = part * 512 + quarter * 128
                merged[row * 24 : row * 24 + 24, at : at + 128] = rim[
                    quarter, 2 * row + part % 2, pl.ds(7 + part // 2, 24, stride=2), :
                ]
    normal = normed(merged[...], gain1_ref[...]).astype(BF)
    for copy in waits["merge"]:
        copy.wait()
    reduced = None
    for z_hi in range(2):
        for y_at in range(4):
            block = jnp.concatenate(
                [
                    merge[half, y_at, z_hi * 4 : z_hi * 4 + 4].reshape(1024, 128)
                    for half in range(2)
                ],
                axis=1,
            )
            at = (z_hi * 4 + y_at) * 256
            part = dot_nt(normal[:, at : at + 256], block)
            reduced = part if reduced is None else reduced + part
    reduced = reduced.astype(BF).astype(F32)
    total[...] = reduced
    normal = normed(reduced, gain2_ref[...]).astype(BF)
    for copy in waits["inward"]:
        copy.wait()
    for third in range(3):
        for z_hi in range(2):
            for y_at in range(0, 4, 2):
                block = jnp.concatenate(
                    [
                        inward[y_at + half, z_hi * 4 : z_hi * 4 + 4].reshape(3072, 128)[
                            third * 1024 : third * 1024 + 1024
                        ]
                        for half in range(2)
                    ],
                    axis=1,
                )
                at = (z_hi * 4 + y_at) * 128
                part = dot_nt(normal[:, at : at + 256], block)
                if z_hi + y_at == 0:
                    sums = part
                else:
                    sums = sums + part
        if third == 0:
            sums = sums * 0.125
        packed[:, third * 1024 : third * 1024 + 1024] = sums.astype(BF)

    split = jnp.where(shift > 0, 6 - shift, -shift)
    edge = jnp.where(((lat == 7) & (shift > 0)) | ((lat == 0) & (shift < 0)), 1, 0)
    mask = window_mask(split, edge)
    mask = jnp.concatenate([mask, mask], axis=0)
    for pair in range(8):
        at = pair * 128
        mixed = attend_pair(
            packed[:, at : at + 128],
            packed[:, 1024 + at : 1024 + at + 128],
            packed[:, 2048 + at : 2048 + at + 128],
            mask,
        )
        attended[:, at : at + 128] = mixed.astype(BF)
    for copy in waits["outward"]:
        copy.wait()
    sums = total[...]
    for z_hi in range(2):
        for y_at in range(0, 4, 2):
            block = jnp.concatenate(
                [
                    outward[y_at + half, z_hi * 4 : z_hi * 4 + 4].reshape(1024, 128)
                    for half in range(2)
                ],
                axis=1,
            )
            at = (z_hi * 4 + y_at) * 128
            sums = sums + dot_nt(attended[:, at : at + 256], block)
    total[...] = sums
    for row in range(6):
        out_ref[row] = total[row * 24 : row * 24 + 24].astype(BF)


def level_two(place, above, f, below, col, gain1, gain2, first, second):
    return pl.pallas_call(
        level_two_kernel,
        out_shape=jax.ShapeDtypeStruct((6, 24, 1024), BF),
        in_specs=[SMEM] + [VMEM] * 6 + [ANY] * 20,
        out_specs=VMEM,
        scratch_shapes=[
            pltpu.VMEM((2, 4, 8, 8, 32, 128), BF),
            pltpu.VMEM((4, 8, 8, 32, 128), BF),
            pltpu.VMEM((4, 8, 4, 2, 96, 128), BF),
            pltpu.VMEM((4, 12, 56, 128), F32),
            pltpu.VMEM((144, 2048), F32),
            pltpu.VMEM((144, 1024), F32),
            pltpu.VMEM((144, 3072), BF),
            pltpu.VMEM((144, 1024), BF),
            pltpu.VMEM((18, 48, 512), BF),
            pltpu.SemaphoreType.DMA((40,)),
        ],
        compiler_params=pltpu.CompilerParams(vmem_limit_bytes=LIMIT),
        cost_estimate=pl.CostEstimate(
            flops=2_000_000_000, bytes_accessed=14_000_000, transcendentals=1_000_000
        ),
        name="level_two",
    )(place, above, f, below, col, gain1, gain2, *first, *second)


def edges(grid):
    return to_cell(grid[-3:], 1, 0), to_cell(grid[:3], -1, 0)


def column(above, grid, below, index, direction):
    part = jnp.concatenate([part[:, index] for part in (above, grid, below)], axis=0)
    return to_cell(part, 0, direction)


def moved_rows(col, start):
    return lax.dynamic_slice_in_dim(col, start, 12, 0)


def moved_back(shift, above, grid, below, col):
    whole = jnp.concatenate([above, grid, below], axis=0)
    count = grid.shape[0]
    whole = lax.dynamic_slice_in_dim(whole, 3 - shift, count, 0)
    col = lax.dynamic_slice_in_dim(col, 3 - shift, count, 0)
    return jnp.concatenate([whole[:, 1:], col[:, None]], axis=1)


def line(*values):
    values = jnp.concatenate([value.reshape(-1) for value in values])
    return jnp.pad(values, (0, 512 - values.shape[0])).reshape(1, 512)


def shards(
    latent,
    surface,
    table,
    shifts,
    gain_one,
    inward_one,
    outward_one,
    gain_ffn,
    ffn_up,
    ffn_down,
    gain_merge,
    merge_proj,
    gain_two,
    inward_two,
    outward_two,
):
    lat, lon = lax.axis_index("lat"), lax.axis_index("lon")
    shift = jnp.where(shifts[0] <= 3, shifts[0], shifts[0] - 6)
    place = jnp.stack(
        [(lon // 2) % 4, lat % 4, (lat // 4) * 4 + lon // 8, lon % 2, lat, shift]
    ).astype(jnp.int32)

    shard = pack(merge_proj, inward_two, outward_two)
    around = [move(shard, dz=-step) for step in (4, 3, 5, 2, 6, 1, 7)]
    around = [shard] + [around[at] for at in (5, 3, 1, 0, 2, 4, 6)]

    classes = surface.astype(BF)
    left = to_cell(jnp.concatenate([latent[:, -1], line(classes[:, -1])]), 0, 1)
    left_cls = left[12, :12]

    first, second = assemble_z(place, *around)

    first_left, second_left = move(first, dy=1), move(second, dx=1)
    first_right, second_right = move(first, dy=-1), move(second, dx=-1)

    def message(part):
        values = jnp.concatenate(
            [latent[part].reshape(-1, 512), left[:12][part], line(classes[part], left_cls[part])]
        )
        return after(values, first)

    above = to_cell(message(slice(9, 12)), 1, 0)
    below = to_cell(message(slice(0, 3)), -1, 0)

    first, second = assemble(
        place,
        (
            first, first_left, first_right,
            move(first_left[:4], dy=1), move(first_right[4:], dy=-1),
        ),
        (
            second, second_left, second_right,
            move(second_left[:4], dx=1), move(second_right[4:], dx=-1),
        ),
    )
    first_left, second_left = move(first, dx=1), move(second, dy=1)
    first_right, second_right = move(first, dx=-1), move(second, dy=-1)
    firsts = [
        first, first_left, first_right,
        move(first_left[:2], dx=1), move(first_right[2:], dx=-1),
    ]
    seconds = [
        second, second_left, second_right,
        move(second_left[:4], dy=1), move(second_right[4:], dy=-1),
    ]
    firsts = firsts + [move(piece, dc=1) for piece in firsts]
    seconds = seconds + [move(piece, dc=1) for piece in seconds]

    cls = jnp.concatenate(
        [above[147, :144].reshape(3, 48), classes, below[147, :144].reshape(3, 48)]
    )
    left_cls = jnp.concatenate([above[147, 144:147], left_cls, below[147, 144:147]])
    cls = jnp.concatenate([left_cls[:, None], cls[:, :-1]], axis=1)
    cls = jnp.pad(moved_rows(cls, 3 + shift).astype(F32).T, ((0, 0), (0, 4)))
    left = moved_rows(jnp.concatenate([above[144:147], left[:12], below[144:147]]), 3 + shift)
    left = after(left, first, second)
    frame = level_one(
        place, above[:144].reshape(3, 48, 512), latent, below[:144].reshape(3, 48, 512),
        left, cls, table, gain_one.reshape(1, -1), gain_ffn.reshape(1, -1),
        inward_one, outward_one, ffn_up, ffn_down,
    )

    above, below = edges(frame)
    left = moved_rows(column(above, frame, below, 47, 1), 3 + shift)
    ends = (firsts[3], firsts[4], seconds[3], seconds[4])
    right = column(after(above, *ends), frame, below, 0, -1)
    out_one = moved_back(shift, above, frame, below, right)
    frame = level_two(
        place, above, frame, below, left,
        gain_merge.reshape(1, -1), gain_two.reshape(1, -1), firsts, seconds,
    )
    above, below = edges(frame)
    right = column(above, frame, below, 0, -1)
    return out_one, moved_back(shift, above, frame, below, right)


def solution(mesh):
    placed = (
        P("lat", "lon", None),
        P("lat", "lon"),
        P(),
        P(),
        P(),
        P(),
        P(),
        P(),
        P(),
        P(),
        P(),
        P("lat", "lon"),
        P(),
        P("lat", "lon"),
        P("lat", "lon"),
    )
    return jax.shard_map(
        shards,
        mesh=mesh,
        in_specs=placed,
        out_specs=(P("lat", "lon", None), P("lat", "lon", None)),
        check_vma=False,
    )
```

```python
import jax
import jax.numpy as jnp
from jax import lax
from jax.experimental import pallas as pl
from jax.experimental.pallas import tpu as pltpu
from jax.sharding import PartitionSpec as P

EPS = 1e-05
BF = jnp.bfloat16
F32 = jnp.float32
AXES = ("lat", "lon")
VMEM = pl.BlockSpec(memory_space=pltpu.VMEM)
SMEM = pl.BlockSpec(memory_space=pltpu.SMEM)
ANY = pl.BlockSpec(memory_space=pl.ANY)
MIB = 1024 * 1024

PLACES = [(x, y, z, c) for z in range(8) for y in range(4) for x in range(4) for c in range(2)]


def number(x, y, z, c):
    x, y, z, c = x % 4, y % 4, z % 8, c % 2
    return ((z // 4) * 4 + y) * 32 + ((z % 4) * 4 + x) * 2 + c


def move(array, steps):
    pairs = []
    for x, y, z, c in PLACES:
        dx, dy, dz, dc = steps[c]
        pairs.append((number(x, y, z, c), number(x + dx, y + dy, z + dz, c + dc)))
    return lax.ppermute(array, AXES, pairs)


def along_z(array, step):
    return move(array, ((0, 0, step, 0),) * 2)


def to_core(array):
    return move(array, ((0, 0, 0, 1),) * 2)


def along(array, last, step):
    by_x, by_y = (step, 0, 0, 0), (0, step, 0, 0)
    return move(array, (by_x, by_y) if last else (by_y, by_x))


def to_cell(array, dlat, dlon):
    pairs = [
        (i * 32 + j, ((i + dlat) % 8) * 32 + (j + dlon) % 32) for i in range(8) for j in range(32)
    ]
    return lax.ppermute(array, AXES, pairs)


def after(value, *others):
    return lax.optimization_barrier((value,) + others)[0]


def pack_kernel(place_ref, merge_ref, inward_ref, outward_ref, keep_ref, send_ref):
    def store(first, second):
        first[0:32] = merge_ref[:, :128]
        first[32:64] = merge_ref[:, 128:]
        first[64:96] = outward_ref[...]
        second[...] = inward_ref[...]

    @pl.when(place_ref[3] == 0)
    def _():
        store(keep_ref, send_ref)

    @pl.when(place_ref[3] == 1)
    def _():
        store(send_ref, keep_ref)


def pack(place, merge, inward, outward):
    return pl.pallas_call(
        pack_kernel,
        out_shape=[jax.ShapeDtypeStruct((96, 128), BF)] * 2,
        in_specs=[SMEM] + [VMEM] * 3,
        out_specs=[VMEM] * 2,
        compiler_params=pltpu.CompilerParams(vmem_limit_bytes=6 * MIB),
        name="pack",
    )(place, merge.T, inward.T, outward.T)


def assemble_z_kernel(place_ref, *refs):
    pieces, (out_ref, sem) = refs[:8], refs[8:]
    z, core = place_ref[2], place_ref[3]
    copies = []
    for step, piece in enumerate(pieces):
        to = lax.rem(z + step, 8)
        for other in range(2):
            target = out_ref.at[to, lax.rem(core + other, 2)]
            copies.append(pltpu.make_async_copy(piece.at[other], target, sem.at[len(copies)]))
    for copy in copies:
        copy.start()
    for copy in copies:
        copy.wait()


def assemble_z(place, *pieces):
    return pl.pallas_call(
        assemble_z_kernel,
        out_shape=jax.ShapeDtypeStruct((8, 2, 96, 128), BF),
        in_specs=[SMEM] + [ANY] * 8,
        out_specs=VMEM,
        scratch_shapes=[pltpu.SemaphoreType.DMA((16,))],
        compiler_params=pltpu.CompilerParams(vmem_limit_bytes=6 * MIB),
        name="assemble_z",
    )(place, *pieces)


def assemble_kernel(place_ref, own, left, right, half0, half1, out_ref, sem):
    at = place_ref[6]
    copies = [
        pltpu.make_async_copy(piece, out_ref.at[lax.rem(at + step, 4), lo:hi], sem.at[index])
        for index, (piece, step, lo, hi) in enumerate(
            ((own, 0, 0, 8), (left, 3, 0, 8), (right, 1, 0, 8), (half0, 2, 0, 4), (half1, 2, 4, 8))
        )
    ]
    for copy in copies:
        copy.start()
    for copy in copies:
        copy.wait()


def assemble(place, *pieces):
    return pl.pallas_call(
        assemble_kernel,
        out_shape=jax.ShapeDtypeStruct((4, 8, 2, 96, 128), BF),
        in_specs=[SMEM] + [ANY] * 5,
        out_specs=VMEM,
        scratch_shapes=[pltpu.SemaphoreType.DMA((5,))],
        compiler_params=pltpu.CompilerParams(vmem_limit_bytes=6 * MIB),
        name="assemble",
    )(place, *pieces)


def normed(hidden, gain):
    centre = jnp.mean(hidden, axis=-1, keepdims=True)
    centred = hidden - centre
    variance = jnp.mean(centred * centred, axis=-1, keepdims=True)
    return centred * lax.rsqrt(variance + EPS) * gain


def dot(a, b):
    return jnp.dot(a, b, preferred_element_type=F32)


def dot_nt(a, b):
    return lax.dot_general(a, b, (((1,), (1,)), ((), ())), preferred_element_type=F32)


def window_mask(split, edge):
    def code(axis):
        token = lax.broadcasted_iota(jnp.int32, (144, 144), axis)
        row = (token * 2731) >> 16
        col = token - 24 * row
        return jnp.where(col >= 12, 1, 0) + jnp.where(row >= split, 2, 0) * edge

    return code(0) == code(1)


def attend_pair(queries, keys, values, mask):
    low = lax.broadcasted_iota(jnp.int32, (144, 128), 1) < 64
    zero = jnp.zeros_like(queries)
    both = jnp.concatenate([jnp.where(low, queries, zero), jnp.where(low, zero, queries)], axis=0)
    scores = jnp.where(mask, dot_nt(both, keys), -1e9)
    weights = jnp.exp(scores - jnp.max(scores, axis=-1, keepdims=True))
    total = jnp.sum(weights, axis=-1, keepdims=True)
    mixed = dot(weights.astype(BF), values) * (1.0 / total)
    return jnp.where(low, mixed[:144], mixed[144:])


def level_one_kernel(
    place_ref,
    above_ref,
    x_ref,
    below_ref,
    col_ref,
    cls_ref,
    table_ref,
    gain1_ref,
    gain2_ref,
    inward_hbm,
    outward_hbm,
    up_hbm,
    down_hbm,
    out_ref,
    top_ref,
    bottom_ref,
    first_ref,
    last_ref,
    inward,
    outward,
    up,
    down,
    rim,
    residual,
    attended,
    ext,
    cols,
    sem,
):
    copies = [
        pltpu.make_async_copy(source, target, sem.at[index])
        for index, (source, target) in enumerate(
            ((inward_hbm, inward), (outward_hbm, outward), (up_hbm, up), (down_hbm, down))
        )
    ]
    for copy in copies:
        copy.start()
    lat, shift = place_ref[4], place_ref[5]
    split = jnp.where(shift > 0, 6 - shift, -shift)
    for row in range(3):
        ext[row] = above_ref[row * 48 : row * 48 + 48]
        ext[15 + row] = below_ref[row * 48 : row * 48 + 48]
        cols[row] = above_ref[144 + row : 145 + row].astype(F32)
        cols[15 + row] = below_ref[144 + row : 145 + row].astype(F32)
    for row in range(12):
        ext[3 + row] = x_ref[row]
        cols[3 + row] = col_ref[row : row + 1].astype(F32)
    for band in range(2):
        for row in range(6):
            frame = band * 6 + row
            rim[row, 8:56] = ext[3 + shift + frame].astype(F32)
            rim[row, 7:8] = cols[3 + shift + frame]
            cls = cls_ref[:, frame : frame + 1]
            embedded = jnp.where(
                cls == 0.0, table_ref[0:1], jnp.where(cls == 1.0, table_ref[1:2], table_ref[2:3])
            )
            residual[row * 48 : (row + 1) * 48] = rim[row, 7:55] + embedded
        normal = normed(residual[...], gain1_ref[...]).astype(BF)
        if band == 1:
            edge = jnp.where((lat == 7) & (shift > 0), 1, 0)
        else:
            edge = jnp.where((lat == 0) & (shift < 0), 1, 0)
        mask = window_mask(split, edge)
        mask = jnp.concatenate([mask, mask], axis=0)
        if band == 0:
            copies[0].wait()
        for quarter in range(2):
            at = quarter * 256
            parts = [
                dot(normal, inward[:, part * 512 + at : part * 512 + at + 256]).reshape(6, 48, 256)
                for part in range(3)
            ]
            for pair in range(2):
                lanes = slice(pair * 128, pair * 128 + 128)
                for block in range(2):
                    span = slice(block * 24, block * 24 + 24)
                    queries, keys, values = (
                        part[:, span, lanes].reshape(144, 128).astype(BF) for part in parts
                    )
                    mixed = attend_pair(queries * BF(0.125), keys, values, mask)
                    attended[:, span, at + pair * 128 : at + pair * 128 + 128] = mixed.reshape(
                        6, 24, 128
                    )
        if band == 0:
            copies[1].wait()
        mid = residual[...] + dot(attended[...].reshape(288, 512).astype(BF), outward[...])
        residual[...] = mid
        normal = normed(mid, gain2_ref[...]).astype(BF)
        if band == 0:
            copies[2].wait()
            copies[3].wait()
        for chunk in range(4):
            part = slice(chunk * 512, chunk * 512 + 512)
            hidden = jax.nn.gelu(dot(normal, up[:, part])).astype(BF)
            residual[...] += dot(hidden, down[part])
        result = residual[...].astype(BF).reshape(6, 48, 512)
        out_ref[band * 6 : band * 6 + 6] = result
        if band == 0:
            top_ref[...] = result[:3]
        else:
            bottom_ref[...] = result[3:]
        for row in range(6):
            first_ref[band * 6 + row] = residual[row * 48 : row * 48 + 1].astype(BF)
            last_ref[band * 6 + row] = residual[row * 48 + 47 : row * 48 + 48].astype(BF)


def level_one(place, above, x, below, col, cls, table, gain1, gain2, inward, outward, up, down):
    return pl.pallas_call(
        level_one_kernel,
        out_shape=[
            jax.ShapeDtypeStruct((12, 48, 512), BF),
            jax.ShapeDtypeStruct((3, 48, 512), BF),
            jax.ShapeDtypeStruct((3, 48, 512), BF),
            jax.ShapeDtypeStruct((12, 1, 512), BF),
            jax.ShapeDtypeStruct((12, 1, 512), BF),
        ],
        in_specs=[SMEM] + [VMEM] * 8 + [ANY] * 4,
        out_specs=[VMEM] * 5,
        scratch_shapes=[
            pltpu.VMEM((512, 1536), BF),
            pltpu.VMEM((512, 512), BF),
            pltpu.VMEM((512, 2048), BF),
            pltpu.VMEM((2048, 512), BF),
            pltpu.VMEM((6, 56, 512), F32),
            pltpu.VMEM((288, 512), F32),
            pltpu.VMEM((6, 48, 512), F32),
            pltpu.VMEM((18, 48, 512), BF),
            pltpu.VMEM((18, 1, 512), F32),
            pltpu.SemaphoreType.DMA((4,)),
        ],
        compiler_params=pltpu.CompilerParams(vmem_limit_bytes=24 * MIB),
        cost_estimate=pl.CostEstimate(
            flops=13_000_000_000, bytes_accessed=8_000_000, transcendentals=3_000_000
        ),
        name="level_one",
    )(place, above, x, below, col, cls, table, gain1, gain2, inward, outward, up, down)


def level_two_kernel(place_ref, above_ref, f_ref, below_ref, col_ref, gain1_ref, gain2_ref, *refs):
    mine, others = refs[0:5], refs[5:10]
    (out_ref, top_ref, bottom_ref, first_ref) = refs[10:14]
    merge, outward, inward, rim, merged, total, packed, attended, ext, sem = refs[14:]
    x, y, core = place_ref[0], place_ref[1], place_ref[3]
    lat, shift = place_ref[4], place_ref[5]

    def jobs(first, second):
        lists = {"merge": [], "inward": [], "outward": []}
        count = 0
        for piece, step, lo, hi in zip(
            range(5), (0, 3, 1, 2, 2), (0, 0, 0, 0, 2), (4, 4, 4, 2, 4)
        ):
            to_x, to_y = lax.rem(x + step, 4), lax.rem(y + step, 4)
            for section in range(3):
                rows = slice(section * 32, section * 32 + 32)
                target = (merge.at[0], merge.at[1], outward)[section]
                lists["outward" if section == 2 else "merge"].append(
                    pltpu.make_async_copy(
                        first[piece].at[:, :, :, rows],
                        target.at[lo:hi, :, to_x],
                        sem.at[count],
                    )
                )
                count += 1
            for column in range(lo, hi):
                lists["inward"].append(
                    pltpu.make_async_copy(
                        second[piece].at[column - lo], inward.at[to_y, :, column], sem.at[count]
                    )
                )
                count += 1
        return lists

    @pl.when(core == 0)
    def _():
        for copies in jobs(mine, others).values():
            for copy in copies:
                copy.start()

    @pl.when(core == 1)
    def _():
        for copies in jobs(others, mine).values():
            for copy in copies:
                copy.start()

    waits = jobs(mine, others)
    for row in range(3):
        ext[row] = above_ref[row]
        ext[15 + row] = below_ref[row]
    for row in range(12):
        ext[3 + row] = f_ref[row]
    for row in range(12):
        values = ext[3 + shift + row].astype(F32)
        left = col_ref[3 + shift + row].astype(F32)
        for quarter in range(4):
            lanes = slice(quarter * 128, quarter * 128 + 128)
            rim[quarter, row, 8:56] = values[:, lanes]
            rim[quarter, row, 7:8] = left[:, lanes]
    for row in range(6):
        for part in range(4):
            for quarter in range(4):
                at = part * 512 + quarter * 128
                merged[row * 24 : row * 24 + 24, at : at + 128] = rim[
                    quarter, 2 * row + part % 2, pl.ds(7 + part // 2, 24, stride=2), :
                ]
    normal = normed(merged[...], gain1_ref[...]).astype(BF)
    for copy in waits["merge"]:
        copy.wait()
    reduced = None
    for z_hi in range(2):
        for y_at in range(4):
            block = jnp.concatenate(
                [
                    merge[half, y_at, z_hi * 4 : z_hi * 4 + 4].reshape(1024, 128)
                    for half in range(2)
                ],
                axis=1,
            )
            at = (z_hi * 4 + y_at) * 256
            part = dot_nt(normal[:, at : at + 256], block)
            reduced = part if reduced is None else reduced + part
    reduced = reduced.astype(BF).astype(F32)
    total[...] = reduced
    normal = normed(reduced, gain2_ref[...]).astype(BF)
    for copy in waits["inward"]:
        copy.wait()
    for third in range(3):
        for z_hi in range(2):
            for y_at in range(0, 4, 2):
                block = jnp.concatenate(
                    [
                        inward[y_at + half, z_hi * 4 : z_hi * 4 + 4].reshape(3072, 128)[
                            third * 1024 : third * 1024 + 1024
                        ]
                        for half in range(2)
                    ],
                    axis=1,
                )
                at = (z_hi * 4 + y_at) * 128
                part = dot_nt(normal[:, at : at + 256], block)
                if z_hi + y_at == 0:
                    sums = part
                else:
                    sums = sums + part
        if third == 0:
            sums = sums * 0.125
        packed[:, third * 1024 : third * 1024 + 1024] = sums.astype(BF)

    split = jnp.where(shift > 0, 6 - shift, -shift)
    edge = jnp.where(((lat == 7) & (shift > 0)) | ((lat == 0) & (shift < 0)), 1, 0)
    mask = window_mask(split, edge)
    mask = jnp.concatenate([mask, mask], axis=0)
    for pair in range(8):
        at = pair * 128
        mixed = attend_pair(
            packed[:, at : at + 128],
            packed[:, 1024 + at : 1024 + at + 128],
            packed[:, 2048 + at : 2048 + at + 128],
            mask,
        )
        attended[:, at : at + 128] = mixed.astype(BF)
    for copy in waits["outward"]:
        copy.wait()
    sums = total[...]
    for z_hi in range(2):
        for y_at in range(0, 4, 2):
            block = jnp.concatenate(
                [
                    outward[y_at + half, z_hi * 4 : z_hi * 4 + 4].reshape(1024, 128)
                    for half in range(2)
                ],
                axis=1,
            )
            at = (z_hi * 4 + y_at) * 128
            sums = sums + dot_nt(attended[:, at : at + 256], block)
    total[...] = sums
    for row in range(6):
        result = total[row * 24 : row * 24 + 24].astype(BF)
        out_ref[row] = result
        if row < 3:
            top_ref[row] = result
        else:
            bottom_ref[row - 3] = result
        first_ref[row] = total[row * 24 : row * 24 + 1].astype(BF)


def level_two(place, above, f, below, col, gain1, gain2, mine, others):
    return pl.pallas_call(
        level_two_kernel,
        out_shape=[
            jax.ShapeDtypeStruct((6, 24, 1024), BF),
            jax.ShapeDtypeStruct((3, 24, 1024), BF),
            jax.ShapeDtypeStruct((3, 24, 1024), BF),
            jax.ShapeDtypeStruct((6, 1, 1024), BF),
        ],
        in_specs=[SMEM] + [VMEM] * 6 + [ANY] * 10,
        out_specs=[VMEM] * 4,
        scratch_shapes=[
            pltpu.VMEM((2, 4, 8, 4, 2, 32, 128), BF),
            pltpu.VMEM((4, 8, 4, 2, 32, 128), BF),
            pltpu.VMEM((4, 8, 4, 2, 96, 128), BF),
            pltpu.VMEM((4, 12, 56, 128), F32),
            pltpu.VMEM((144, 2048), F32),
            pltpu.VMEM((144, 1024), F32),
            pltpu.VMEM((144, 3072), BF),
            pltpu.VMEM((144, 1024), BF),
            pltpu.VMEM((18, 48, 512), BF),
            pltpu.SemaphoreType.DMA((31,)),
        ],
        compiler_params=pltpu.CompilerParams(vmem_limit_bytes=32 * MIB),
        cost_estimate=pl.CostEstimate(
            flops=11_000_000_000, bytes_accessed=14_000_000, transcendentals=1_000_000
        ),
        name="level_two",
    )(place, above, f, below, col, gain1, gain2, *mine, *others)


def edges(top, bottom):
    return to_cell(bottom, 1, 0), to_cell(top, -1, 0)


def column(above, col, below, index, direction):
    part = jnp.concatenate([above[:, index], col, below[:, index]], axis=0)
    return to_cell(part, 0, direction)


def moved_rows(col, start):
    return lax.dynamic_slice_in_dim(col, start, 12, 0)


def moved_back(shift, above, grid, below, col):
    whole = jnp.concatenate([above, grid, below], axis=0)
    count = grid.shape[0]
    whole = lax.dynamic_slice_in_dim(whole, 3 - shift, count, 0)
    col = lax.dynamic_slice_in_dim(col, 3 - shift, count, 0)
    return jnp.concatenate([whole[:, 1:], col], axis=1)


def line(*values):
    values = jnp.concatenate([value.reshape(-1) for value in values])
    return jnp.pad(values, (0, 512 - values.shape[0])).reshape(1, 512)


def shards(
    latent,
    surface,
    table,
    shifts,
    gain_one,
    inward_one,
    outward_one,
    gain_ffn,
    ffn_up,
    ffn_down,
    gain_merge,
    merge_proj,
    gain_two,
    inward_two,
    outward_two,
):
    lat, lon = lax.axis_index("lat"), lax.axis_index("lon")
    shift = jnp.where(shifts[0] <= 3, shifts[0], shifts[0] - 6)
    x, y, z, core = (lon // 2) % 4, lat % 4, (lat // 4) * 4 + lon // 8, lon % 2
    place = jnp.stack([x, y, z, core, lat, shift, jnp.where(core == 0, y, x)]).astype(jnp.int32)

    keep, send = pack(place, merge_proj, inward_two, outward_two)
    shard = jnp.stack([keep, to_core(send)])
    around = [along_z(shard, -step) for step in (4, 3, 5, 2, 6, 1, 7)]
    around = [shard] + [around[at] for at in (5, 3, 1, 0, 2, 4, 6)]

    classes = surface.astype(BF)
    left = to_cell(jnp.concatenate([latent[:, -1], line(classes[:, -1])]), 0, 1)
    left_cls = left[12, :12]

    block = assemble_z(place, *around)

    from_left, from_right = along(block, False, 1), along(block, False, -1)

    def message(part):
        values = jnp.concatenate(
            [latent[part].reshape(-1, 512), left[:12][part], line(classes[part], left_cls[part])]
        )
        return after(values, around[1], around[7])

    above = to_cell(message(slice(9, 12)), 1, 0)
    below = to_cell(message(slice(0, 3)), -1, 0)

    block = assemble(
        place, block, from_left, from_right,
        along(from_left[:4], False, 1), along(from_right[4:], False, -1),
    )
    from_left, from_right = along(block, True, 1), along(block, True, -1)
    mine = [
        block, from_left, from_right,
        along(from_left[:2], True, 1), along(from_right[2:], True, -1),
    ]
    others = [to_core(piece) for piece in mine[:3]]

    cls = jnp.concatenate(
        [above[147, :144].reshape(3, 48), classes, below[147, :144].reshape(3, 48)]
    )
    left_cls = jnp.concatenate([above[147, 144:147], left_cls, below[147, 144:147]])
    cls = jnp.concatenate([left_cls[:, None], cls[:, :-1]], axis=1)
    cls = jnp.pad(moved_rows(cls, 3 + shift).astype(F32).T, ((0, 0), (0, 4)))
    frame, top, bottom, first, last = level_one(
        place, above, latent, below, after(left, block), cls, table,
        gain_one.reshape(1, -1), gain_ffn.reshape(1, -1),
        inward_one, outward_one, ffn_up, ffn_down,
    )

    above, below = edges(top, bottom)
    left = column(after(above, *mine[1:3])[:, :, None], last, below[:, :, None], 47, 1)
    others += [to_core(after(piece, left)) for piece in mine[3:]]
    right = column(after(above, *others)[:, :, None], first, below[:, :, None], 0, -1)
    out_one = moved_back(shift, above, frame, below, right)
    frame, top, bottom, first = level_two(
        place, above, frame, below, left,
        gain_merge.reshape(1, -1), gain_two.reshape(1, -1), mine, others,
    )
    above, below = edges(top, bottom)
    right = jnp.concatenate(
        [to_cell(first[3:], 1, -1), to_cell(first, 0, -1), to_cell(first[:3], -1, -1)]
    )
    return out_one, moved_back(shift, above, frame, below, right)


def solution(mesh):
    placed = (
        P("lat", "lon", None),
        P("lat", "lon"),
        P(),
        P(),
        P(),
        P(),
        P(),
        P(),
        P(),
        P(),
        P(),
        P("lat", "lon"),
        P(),
        P("lat", "lon"),
        P("lat", "lon"),
    )
    return jax.shard_map(
        shards,
        mesh=mesh,
        in_specs=placed,
        out_specs=(P("lat", "lon", None), P("lat", "lon", None)),
        check_vma=False,
    )
```

```python
import jax
import jax.numpy as jnp
from jax import lax
from jax.experimental import pallas as pl
from jax.experimental.pallas import tpu as pltpu
from jax.sharding import PartitionSpec as P

EPS = 1e-05
BF = jnp.bfloat16
F32 = jnp.float32
AXES = ("lat", "lon")
VMEM = pl.BlockSpec(memory_space=pltpu.VMEM)
SMEM = pl.BlockSpec(memory_space=pltpu.SMEM)
ANY = pl.BlockSpec(memory_space=pl.ANY)
HBM = pl.BlockSpec(memory_space=pltpu.HBM)
MIB = 1024 * 1024

PLACES = [(x, y, z, c) for z in range(8) for y in range(4) for x in range(4) for c in range(2)]


def number(x, y, z, c):
    x, y, z, c = x % 4, y % 4, z % 8, c % 2
    return ((z // 4) * 4 + y) * 32 + ((z % 4) * 4 + x) * 2 + c


def move(array, steps):
    pairs = []
    for x, y, z, c in PLACES:
        dx, dy, dz, dc = steps[c]
        pairs.append((number(x, y, z, c), number(x + dx, y + dy, z + dz, c + dc)))
    return lax.ppermute(array, AXES, pairs)


def along_z(array, step):
    return move(array, ((0, 0, step, 0),) * 2)


def to_core(array):
    return move(array, ((0, 0, 0, 1),) * 2)


def along(array, last, step):
    by_x, by_y = (step, 0, 0, 0), (0, step, 0, 0)
    return move(array, (by_x, by_y) if last else (by_y, by_x))


def to_cell(array, dlat, dlon):
    pairs = [
        (i * 32 + j, ((i + dlat) % 8) * 32 + (j + dlon) % 32) for i in range(8) for j in range(32)
    ]
    return lax.ppermute(array, AXES, pairs)


def after(value, *others):
    return lax.optimization_barrier((value,) + others)[0]


def pack_kernel(place_ref, merge_ref, inward_ref, outward_ref, keep_ref, send_ref, sem):
    def copies(first, second):
        parts = (
            (merge_ref.at[:, 0:128], first.at[0:32]),
            (merge_ref.at[:, 128:256], first.at[32:64]),
            (outward_ref, first.at[64:96]),
            (inward_ref, second),
        )
        return [
            pltpu.make_async_copy(source, target, sem.at[index])
            for index, (source, target) in enumerate(parts)
        ]

    @pl.when(place_ref[3] == 0)
    def _():
        for copy in copies(keep_ref, send_ref):
            copy.start()

    @pl.when(place_ref[3] == 1)
    def _():
        for copy in copies(send_ref, keep_ref):
            copy.start()

    for copy in copies(keep_ref, send_ref):
        copy.wait()


def pack(place, merge, inward, outward):
    return pl.pallas_call(
        pack_kernel,
        out_shape=[jax.ShapeDtypeStruct((96, 128), BF)] * 2,
        in_specs=[SMEM] + [HBM] * 3,
        out_specs=[VMEM] * 2,
        scratch_shapes=[pltpu.SemaphoreType.DMA((4,))],
        compiler_params=pltpu.CompilerParams(vmem_limit_bytes=56 * MIB),
        name="pack",
    )(place, merge.T, inward.T, outward.T)


def assemble_z_kernel(place_ref, low_ref, near_ref, high_ref, out_ref, sem):
    z, core = place_ref[2], place_ref[3]
    copies = []
    for step in range(8):
        ref, first = ((low_ref, 0), (near_ref, 3), (high_ref, 6))[step // 3]
        to = lax.rem(z + 4 + step, 8)
        for other in range(2):
            target = out_ref.at[to, lax.rem(core + other, 2)]
            copies.append(
                pltpu.make_async_copy(ref.at[step - first, other], target, sem.at[len(copies)])
            )
    for copy in copies:
        copy.start()
    for copy in copies:
        copy.wait()


def assemble_z(place, low, near, high):
    return pl.pallas_call(
        assemble_z_kernel,
        out_shape=jax.ShapeDtypeStruct((8, 2, 96, 128), BF),
        in_specs=[SMEM] + [ANY] * 3,
        out_specs=VMEM,
        scratch_shapes=[pltpu.SemaphoreType.DMA((16,))],
        compiler_params=pltpu.CompilerParams(vmem_limit_bytes=6 * MIB),
        name="assemble_z",
    )(place, low, near, high)


def assemble_kernel(place_ref, own, left, right, half0, half1, out_ref, sem):
    at = place_ref[6]
    copies = [
        pltpu.make_async_copy(piece, out_ref.at[lax.rem(at + step, 4), lo:hi], sem.at[index])
        for index, (piece, step, lo, hi) in enumerate(
            ((own, 0, 0, 8), (left, 3, 0, 8), (right, 1, 0, 8), (half0, 2, 0, 4), (half1, 2, 4, 8))
        )
    ]
    for copy in copies:
        copy.start()
    for copy in copies:
        copy.wait()


def assemble(place, *pieces):
    return pl.pallas_call(
        assemble_kernel,
        out_shape=jax.ShapeDtypeStruct((4, 8, 2, 96, 128), BF),
        in_specs=[SMEM] + [ANY] * 5,
        out_specs=VMEM,
        scratch_shapes=[pltpu.SemaphoreType.DMA((5,))],
        compiler_params=pltpu.CompilerParams(vmem_limit_bytes=6 * MIB),
        name="assemble",
    )(place, *pieces)


def normed(hidden, gain):
    centre = jnp.mean(hidden, axis=-1, keepdims=True)
    centred = hidden - centre
    variance = jnp.mean(centred * centred, axis=-1, keepdims=True)
    return centred * lax.rsqrt(variance + EPS) * gain


def dot(a, b):
    return jnp.dot(a, b, preferred_element_type=F32)


def dot_nt(a, b):
    return lax.dot_general(a, b, (((1,), (1,)), ((), ())), preferred_element_type=F32)


def window_mask(split, edge):
    def code(axis):
        token = lax.broadcasted_iota(jnp.int32, (144, 144), axis)
        row = (token * 2731) >> 16
        col = token - 24 * row
        return jnp.where(col >= 12, 1, 0) + jnp.where(row >= split, 2, 0) * edge

    return code(0) == code(1)


def attend_pair(queries, keys, values, mask):
    low = lax.broadcasted_iota(jnp.int32, (144, 128), 1) < 64
    zero = jnp.zeros_like(queries)
    both = jnp.concatenate([jnp.where(low, queries, zero), jnp.where(low, zero, queries)], axis=0)
    scores = jnp.where(mask, dot_nt(both, keys), -1e9)
    weights = jnp.exp(scores - jnp.max(scores, axis=-1, keepdims=True))
    total = jnp.sum(weights, axis=-1, keepdims=True)
    mixed = dot(weights.astype(BF), values) * (1.0 / total)
    return jnp.where(low, mixed[:144], mixed[144:])


def level_one_kernel(
    place_ref,
    above_ref,
    x_ref,
    below_ref,
    col_ref,
    cls_ref,
    table_ref,
    gain1_ref,
    gain2_ref,
    inward_hbm,
    outward_hbm,
    up_hbm,
    down_hbm,
    out_ref,
    top_ref,
    bottom_ref,
    first_ref,
    last_ref,
    inward,
    outward,
    up,
    down,
    rim,
    residual,
    attended,
    ext,
    cols,
    sem,
):
    copies = [
        pltpu.make_async_copy(source, target, sem.at[index])
        for index, (source, target) in enumerate(
            ((inward_hbm, inward), (outward_hbm, outward), (up_hbm, up), (down_hbm, down))
        )
    ]
    for copy in copies:
        copy.start()
    lat, shift = place_ref[4], place_ref[5]
    split = jnp.where(shift > 0, 6 - shift, -shift)
    for row in range(3):
        ext[row] = above_ref[row * 48 : row * 48 + 48]
        ext[15 + row] = below_ref[row * 48 : row * 48 + 48]
    for row in range(12):
        ext[3 + row] = x_ref[row]
    for row in range(18):
        cols[row] = col_ref[row : row + 1].astype(F32)
    for band in range(2):
        for row in range(6):
            frame = band * 6 + row
            rim[row, 8:56] = ext[3 + shift + frame].astype(F32)
            rim[row, 7:8] = cols[3 + shift + frame]
            cls = cls_ref[:, frame : frame + 1]
            embedded = jnp.where(
                cls == 0.0, table_ref[0:1], jnp.where(cls == 1.0, table_ref[1:2], table_ref[2:3])
            )
            residual[row * 48 : (row + 1) * 48] = rim[row, 7:55] + embedded
        normal = normed(residual[...], gain1_ref[...]).astype(BF)
        if band == 1:
            edge = jnp.where((lat == 7) & (shift > 0), 1, 0)
        else:
            edge = jnp.where((lat == 0) & (shift < 0), 1, 0)
        mask = window_mask(split, edge)
        mask = jnp.concatenate([mask, mask], axis=0)
        if band == 0:
            copies[0].wait()
        for quarter in range(2):
            at = quarter * 256
            parts = [
                dot(normal, inward[:, part * 512 + at : part * 512 + at + 256]).reshape(6, 48, 256)
                for part in range(3)
            ]
            for pair in range(2):
                lanes = slice(pair * 128, pair * 128 + 128)
                for block in range(2):
                    span = slice(block * 24, block * 24 + 24)
                    queries, keys, values = (
                        part[:, span, lanes].reshape(144, 128).astype(BF) for part in parts
                    )
                    mixed = attend_pair(queries * BF(0.125), keys, values, mask)
                    attended[:, span, at + pair * 128 : at + pair * 128 + 128] = mixed.reshape(
                        6, 24, 128
                    )
        if band == 0:
            copies[1].wait()
        mid = residual[...] + dot(attended[...].reshape(288, 512).astype(BF), outward[...])
        residual[...] = mid
        normal = normed(mid, gain2_ref[...]).astype(BF)
        if band == 0:
            copies[2].wait()
            copies[3].wait()
        for chunk in range(4):
            part = slice(chunk * 512, chunk * 512 + 512)
            hidden = jax.nn.gelu(dot(normal, up[:, part])).astype(BF)
            residual[...] += dot(hidden, down[part])
        result = residual[...].astype(BF).reshape(6, 48, 512)
        out_ref[band * 6 : band * 6 + 6] = result
        if band == 0:
            top_ref[...] = result[:3]
        else:
            bottom_ref[...] = result[3:]
        for row in range(6):
            first_ref[band * 6 + row] = residual[row * 48 : row * 48 + 1].astype(BF)
            last_ref[band * 6 + row] = residual[row * 48 + 47 : row * 48 + 48].astype(BF)


def level_one(place, above, x, below, col, cls, table, gain1, gain2, inward, outward, up, down):
    return pl.pallas_call(
        level_one_kernel,
        out_shape=[
            jax.ShapeDtypeStruct((12, 48, 512), BF),
            jax.ShapeDtypeStruct((3, 48, 512), BF),
            jax.ShapeDtypeStruct((3, 48, 512), BF),
            jax.ShapeDtypeStruct((12, 1, 512), BF),
            jax.ShapeDtypeStruct((12, 1, 512), BF),
        ],
        in_specs=[SMEM] + [VMEM] * 8 + [HBM] * 4,
        out_specs=[VMEM] * 5,
        scratch_shapes=[
            pltpu.VMEM((512, 1536), BF),
            pltpu.VMEM((512, 512), BF),
            pltpu.VMEM((512, 2048), BF),
            pltpu.VMEM((2048, 512), BF),
            pltpu.VMEM((6, 56, 512), F32),
            pltpu.VMEM((288, 512), F32),
            pltpu.VMEM((6, 48, 512), F32),
            pltpu.VMEM((18, 48, 512), BF),
            pltpu.VMEM((18, 1, 512), F32),
            pltpu.SemaphoreType.DMA((4,)),
        ],
        compiler_params=pltpu.CompilerParams(vmem_limit_bytes=24 * MIB),
        cost_estimate=pl.CostEstimate(
            flops=13_000_000_000, bytes_accessed=8_000_000, transcendentals=3_000_000
        ),
        name="level_one",
    )(place, above, x, below, col, cls, table, gain1, gain2, inward, outward, up, down)


def level_two_kernel(place_ref, above_ref, f_ref, below_ref, col_ref, gain1_ref, gain2_ref, *refs):
    mine, others = refs[0:5], refs[5:10]
    (out_ref, top_ref, bottom_ref, first_ref) = refs[10:14]
    merge, outward, inward, rim, merged, total, packed, attended, ext, sem = refs[14:]
    x, y, core = place_ref[0], place_ref[1], place_ref[3]
    lat, shift = place_ref[4], place_ref[5]

    def jobs(first, second):
        lists = {"merge": [], "inward": [], "outward": []}
        count = 0
        for piece, step, lo, hi in zip(
            range(5), (0, 3, 1, 2, 2), (0, 0, 0, 0, 2), (4, 4, 4, 2, 4)
        ):
            to_x, to_y = lax.rem(x + step, 4), lax.rem(y + step, 4)
            for section in range(3):
                rows = slice(section * 32, section * 32 + 32)
                target = (merge.at[0], merge.at[1], outward)[section]
                lists["outward" if section == 2 else "merge"].append(
                    pltpu.make_async_copy(
                        first[piece].at[:, :, :, rows],
                        target.at[lo:hi, :, to_x],
                        sem.at[count],
                    )
                )
                count += 1
            for column in range(lo, hi):
                lists["inward"].append(
                    pltpu.make_async_copy(
                        second[piece].at[column - lo], inward.at[to_y, :, column], sem.at[count]
                    )
                )
                count += 1
        return lists

    @pl.when(core == 0)
    def _():
        for copies in jobs(mine, others).values():
            for copy in copies:
                copy.start()

    @pl.when(core == 1)
    def _():
        for copies in jobs(others, mine).values():
            for copy in copies:
                copy.start()

    waits = jobs(mine, others)
    for row in range(3):
        ext[row] = above_ref[row]
        ext[15 + row] = below_ref[row]
    for row in range(12):
        ext[3 + row] = f_ref[row]
    for row in range(12):
        values = ext[3 + shift + row].astype(F32)
        left = col_ref[3 + shift + row].astype(F32)
        for quarter in range(4):
            lanes = slice(quarter * 128, quarter * 128 + 128)
            rim[quarter, row, 8:56] = values[:, lanes]
            rim[quarter, row, 7:8] = left[:, lanes]
    for row in range(6):
        for part in range(4):
            for quarter in range(4):
                at = part * 512 + quarter * 128
                merged[row * 24 : row * 24 + 24, at : at + 128] = rim[
                    quarter, 2 * row + part % 2, pl.ds(7 + part // 2, 24, stride=2), :
                ]
    normal = normed(merged[...], gain1_ref[...]).astype(BF)
    for copy in waits["merge"]:
        copy.wait()
    reduced = None
    for z_hi in range(2):
        for y_at in range(4):
            block = jnp.concatenate(
                [
                    merge[half, y_at, z_hi * 4 : z_hi * 4 + 4].reshape(1024, 128)
                    for half in range(2)
                ],
                axis=1,
            )
            at = (z_hi * 4 + y_at) * 256
            part = dot_nt(normal[:, at : at + 256], block)
            reduced = part if reduced is None else reduced + part
    reduced = reduced.astype(BF).astype(F32)
    total[...] = reduced
    normal = normed(reduced, gain2_ref[...]).astype(BF)
    for copy in waits["inward"]:
        copy.wait()
    for third in range(3):
        for z_hi in range(2):
            for y_at in range(0, 4, 2):
                block = jnp.concatenate(
                    [
                        inward[y_at + half, z_hi * 4 : z_hi * 4 + 4].reshape(3072, 128)[
                            third * 1024 : third * 1024 + 1024
                        ]
                        for half in range(2)
                    ],
                    axis=1,
                )
                at = (z_hi * 4 + y_at) * 128
                part = dot_nt(normal[:, at : at + 256], block)
                if z_hi + y_at == 0:
                    sums = part
                else:
                    sums = sums + part
        if third == 0:
            sums = sums * 0.125
        packed[:, third * 1024 : third * 1024 + 1024] = sums.astype(BF)

    split = jnp.where(shift > 0, 6 - shift, -shift)
    edge = jnp.where(((lat == 7) & (shift > 0)) | ((lat == 0) & (shift < 0)), 1, 0)
    mask = window_mask(split, edge)
    mask = jnp.concatenate([mask, mask], axis=0)
    for pair in range(8):
        at = pair * 128
        mixed = attend_pair(
            packed[:, at : at + 128],
            packed[:, 1024 + at : 1024 + at + 128],
            packed[:, 2048 + at : 2048 + at + 128],
            mask,
        )
        attended[:, at : at + 128] = mixed.astype(BF)
    for copy in waits["outward"]:
        copy.wait()
    sums = total[...]
    for z_hi in range(2):
        for y_at in range(0, 4, 2):
            block = jnp.concatenate(
                [
                    outward[y_at + half, z_hi * 4 : z_hi * 4 + 4].reshape(1024, 128)
                    for half in range(2)
                ],
                axis=1,
            )
            at = (z_hi * 4 + y_at) * 128
            sums = sums + dot_nt(attended[:, at : at + 256], block)
    total[...] = sums
    for row in range(6):
        result = total[row * 24 : row * 24 + 24].astype(BF)
        out_ref[row] = result
        if row < 3:
            top_ref[row] = result
        else:
            bottom_ref[row - 3] = result
        first_ref[row] = total[row * 24 : row * 24 + 1].astype(BF)


def level_two(place, above, f, below, col, gain1, gain2, mine, others):
    return pl.pallas_call(
        level_two_kernel,
        out_shape=[
            jax.ShapeDtypeStruct((6, 24, 1024), BF),
            jax.ShapeDtypeStruct((3, 24, 1024), BF),
            jax.ShapeDtypeStruct((3, 24, 1024), BF),
            jax.ShapeDtypeStruct((6, 1, 1024), BF),
        ],
        in_specs=[SMEM] + [VMEM] * 6 + [ANY] * 10,
        out_specs=[VMEM] * 4,
        scratch_shapes=[
            pltpu.VMEM((2, 4, 8, 4, 2, 32, 128), BF),
            pltpu.VMEM((4, 8, 4, 2, 32, 128), BF),
            pltpu.VMEM((4, 8, 4, 2, 96, 128), BF),
            pltpu.VMEM((4, 12, 56, 128), F32),
            pltpu.VMEM((144, 2048), F32),
            pltpu.VMEM((144, 1024), F32),
            pltpu.VMEM((144, 3072), BF),
            pltpu.VMEM((144, 1024), BF),
            pltpu.VMEM((18, 48, 512), BF),
            pltpu.SemaphoreType.DMA((31,)),
        ],
        compiler_params=pltpu.CompilerParams(vmem_limit_bytes=32 * MIB),
        cost_estimate=pl.CostEstimate(
            flops=11_000_000_000, bytes_accessed=14_000_000, transcendentals=1_000_000
        ),
        name="level_two",
    )(place, above, f, below, col, gain1, gain2, *mine, *others)


def edges(top, bottom):
    return to_cell(bottom, 1, 0), to_cell(top, -1, 0)


def column(above, col, below, index, direction):
    part = jnp.concatenate([above[:, index], col, below[:, index]], axis=0)
    return to_cell(part, 0, direction)


def moved_rows(col, start):
    return lax.dynamic_slice_in_dim(col, start, 12, 0)


def moved_back(shift, above, grid, below, col):
    whole = jnp.concatenate([above, grid, below], axis=0)
    count = grid.shape[0]
    whole = lax.dynamic_slice_in_dim(whole, 3 - shift, count, 0)
    col = lax.dynamic_slice_in_dim(col, 3 - shift, count, 0)
    return jnp.concatenate([whole[:, 1:], col], axis=1)


def line(*values):
    values = jnp.concatenate([value.reshape(-1) for value in values])
    return jnp.pad(values, (0, 512 - values.shape[0])).reshape(1, 512)


def shards(
    latent,
    surface,
    table,
    shifts,
    gain_one,
    inward_one,
    outward_one,
    gain_ffn,
    ffn_up,
    ffn_down,
    gain_merge,
    merge_proj,
    gain_two,
    inward_two,
    outward_two,
):
    lat, lon = lax.axis_index("lat"), lax.axis_index("lon")
    shift = jnp.where(shifts[0] <= 3, shifts[0], shifts[0] - 6)
    x, y, z, core = (lon // 2) % 4, lat % 4, (lat // 4) * 4 + lon // 8, lon % 2
    place = jnp.stack([x, y, z, core, lat, shift, jnp.where(core == 0, y, x)]).astype(jnp.int32)

    classes = surface.astype(BF)

    def message(part):
        return jnp.concatenate([latent[part].reshape(-1, 512), line(classes[part])])

    above = to_cell(message(slice(9, 12)), 1, 0)
    below = to_cell(message(slice(0, 3)), -1, 0)

    keep, send = pack(place, merge_proj, inward_two, outward_two)
    shard = jnp.stack([keep, to_core(send)])
    near = jnp.stack([along_z(shard, 1), shard, along_z(shard, -1)])
    near, above, below = lax.optimization_barrier((near, above, below))
    far_low, far_high = along_z(near, 3), along_z(near[:2], -3)

    cls = jnp.concatenate(
        [above[144, :144].reshape(3, 48), classes, below[144, :144].reshape(3, 48)]
    )
    left = to_cell(
        jnp.concatenate([above[47:144:48], latent[:, -1], below[47:144:48], line(cls[:, -1])]), 0, 1
    )
    cls = jnp.concatenate([left[18, :18, None], cls[:, :-1]], axis=1)
    cls = jnp.pad(moved_rows(cls, 3 + shift).astype(F32).T, ((0, 0), (0, 4)))
    frame, top, bottom, first, last = level_one(
        place, above, latent, below, left, cls, table,
        gain_one.reshape(1, -1), gain_ffn.reshape(1, -1),
        inward_one, outward_one, ffn_up, ffn_down,
    )

    above, below = edges(top, bottom)

    far_low, far_high = lax.optimization_barrier((far_low, far_high, top))[:2]
    block = assemble_z(place, far_low, near, far_high)
    from_left, from_right = along(block, False, 1), along(block, False, -1)
    block = assemble(
        place, block, from_left, from_right,
        along(from_left[:4], False, 1), along(from_right[4:], False, -1),
    )

    above, below = lax.optimization_barrier((above, below, block))[:2]
    left = column(above[:, :, None], last, below[:, :, None], 47, 1)
    right = column(above[:, :, None], first, below[:, :, None], 0, -1)
    out_one = moved_back(shift, above, frame, below, right)

    from_left, from_right = along(block, True, 1), along(block, True, -1)
    mine = [
        block, from_left, from_right,
        along(from_left[:2], True, 1), along(from_right[2:], True, -1),
    ]
    others = [to_core(piece) for piece in mine]
    frame, top, bottom, first = level_two(
        place, above, frame, below, left,
        gain_merge.reshape(1, -1), gain_two.reshape(1, -1), mine, others,
    )
    above, below = edges(top, bottom)
    right = jnp.concatenate(
        [to_cell(first[3:], 1, -1), to_cell(first, 0, -1), to_cell(first[:3], -1, -1)]
    )
    return out_one, moved_back(shift, above, frame, below, right)


def solution(mesh):
    placed = (
        P("lat", "lon", None),
        P("lat", "lon"),
        P(),
        P(),
        P(),
        P(),
        P(),
        P(),
        P(),
        P(),
        P(),
        P("lat", "lon"),
        P(),
        P("lat", "lon"),
        P("lat", "lon"),
    )
    return jax.shard_map(
        shards,
        mesh=mesh,
        in_specs=placed,
        out_specs=(P("lat", "lon", None), P("lat", "lon", None)),
        check_vma=False,
    )
```

```python
import jax
import jax.numpy as jnp
from jax import lax
from jax.experimental import pallas as pl
from jax.experimental.pallas import tpu as pltpu
from jax.sharding import PartitionSpec as P

EPS = 1e-05
BF = jnp.bfloat16
F32 = jnp.float32
AXES = ("lat", "lon")
VMEM = pl.BlockSpec(memory_space=pltpu.VMEM)
SMEM = pl.BlockSpec(memory_space=pltpu.SMEM)
ANY = pl.BlockSpec(memory_space=pl.ANY)
HBM = pl.BlockSpec(memory_space=pltpu.HBM)
MIB = 1024 * 1024

PLACES = [(x, y, z, c) for z in range(8) for y in range(4) for x in range(4) for c in range(2)]


def number(x, y, z, c):
    x, y, z, c = x % 4, y % 4, z % 8, c % 2
    return ((z // 4) * 4 + y) * 32 + ((z % 4) * 4 + x) * 2 + c


def move(array, steps):
    pairs = []
    for x, y, z, c in PLACES:
        dx, dy, dz, dc = steps[c]
        pairs.append((number(x, y, z, c), number(x + dx, y + dy, z + dz, c + dc)))
    return lax.ppermute(array, AXES, pairs)


def along_z(array, step):
    return move(array, ((0, 0, step, 0),) * 2)


def to_core(array):
    return move(array, ((0, 0, 0, 1),) * 2)


def along(array, last, step):
    by_x, by_y = (step, 0, 0, 0), (0, step, 0, 0)
    return move(array, (by_x, by_y) if last else (by_y, by_x))


def to_cell(array, dlat, dlon):
    pairs = [
        (i * 32 + j, ((i + dlat) % 8) * 32 + (j + dlon) % 32) for i in range(8) for j in range(32)
    ]
    return lax.ppermute(array, AXES, pairs)


def after(value, *others):
    return lax.optimization_barrier((value,) + others)[0]


def pack_kernel(place_ref, merge_ref, inward_ref, outward_ref, keep_ref, send_ref, sem):
    def copies(first, second):
        parts = (
            (merge_ref.at[:, 0:128], first.at[0:32]),
            (merge_ref.at[:, 128:256], first.at[32:64]),
            (outward_ref, first.at[64:96]),
            (inward_ref, second),
        )
        return [
            pltpu.make_async_copy(source, target, sem.at[index])
            for index, (source, target) in enumerate(parts)
        ]

    @pl.when(place_ref[3] == 0)
    def _():
        for copy in copies(keep_ref, send_ref):
            copy.start()

    @pl.when(place_ref[3] == 1)
    def _():
        for copy in copies(send_ref, keep_ref):
            copy.start()

    for copy in copies(keep_ref, send_ref):
        copy.wait()


def pack(place, merge, inward, outward):
    return pl.pallas_call(
        pack_kernel,
        out_shape=[jax.ShapeDtypeStruct((96, 128), BF)] * 2,
        in_specs=[SMEM] + [HBM] * 3,
        out_specs=[VMEM] * 2,
        scratch_shapes=[pltpu.SemaphoreType.DMA((4,))],
        compiler_params=pltpu.CompilerParams(vmem_limit_bytes=56 * MIB),
        name="pack",
    )(place, merge.T, inward.T, outward.T)


def assemble_z_kernel(place_ref, low_ref, near_ref, high_ref, out_ref, sem):
    z, core = place_ref[2], place_ref[3]
    copies = []
    for step in range(8):
        ref, first = ((low_ref, 0), (near_ref, 3), (high_ref, 6))[step // 3]
        to = lax.rem(z + 4 + step, 8)
        for other in range(2):
            target = out_ref.at[to, lax.rem(core + other, 2)]
            copies.append(
                pltpu.make_async_copy(ref.at[step - first, other], target, sem.at[len(copies)])
            )
    for copy in copies:
        copy.start()
    for copy in copies:
        copy.wait()


def assemble_z(place, low, near, high):
    return pl.pallas_call(
        assemble_z_kernel,
        out_shape=jax.ShapeDtypeStruct((8, 2, 96, 128), BF),
        in_specs=[SMEM] + [ANY] * 3,
        out_specs=VMEM,
        scratch_shapes=[pltpu.SemaphoreType.DMA((16,))],
        compiler_params=pltpu.CompilerParams(vmem_limit_bytes=6 * MIB),
        name="assemble_z",
    )(place, low, near, high)


def assemble_kernel(place_ref, own, left, right, half0, half1, out_ref, sem):
    at = place_ref[6]
    copies = [
        pltpu.make_async_copy(piece, out_ref.at[lax.rem(at + step, 4), lo:hi], sem.at[index])
        for index, (piece, step, lo, hi) in enumerate(
            ((own, 0, 0, 8), (left, 3, 0, 8), (right, 1, 0, 8), (half0, 2, 0, 4), (half1, 2, 4, 8))
        )
    ]
    for copy in copies:
        copy.start()
    for copy in copies:
        copy.wait()


def assemble(place, *pieces):
    return pl.pallas_call(
        assemble_kernel,
        out_shape=jax.ShapeDtypeStruct((4, 8, 2, 96, 128), BF),
        in_specs=[SMEM] + [ANY] * 5,
        out_specs=VMEM,
        scratch_shapes=[pltpu.SemaphoreType.DMA((5,))],
        compiler_params=pltpu.CompilerParams(vmem_limit_bytes=6 * MIB),
        name="assemble",
    )(place, *pieces)


def normed(hidden, gain):
    centre = jnp.mean(hidden, axis=-1, keepdims=True)
    centred = hidden - centre
    variance = jnp.mean(centred * centred, axis=-1, keepdims=True)
    return centred * lax.rsqrt(variance + EPS) * gain


def dot(a, b):
    return jnp.dot(a, b, preferred_element_type=F32)


def dot_nt(a, b):
    return lax.dot_general(a, b, (((1,), (1,)), ((), ())), preferred_element_type=F32)


def window_mask(split, edge):
    def code(axis):
        token = lax.broadcasted_iota(jnp.int32, (144, 144), axis)
        row = (token * 2731) >> 16
        col = token - 24 * row
        return jnp.where(col >= 12, 1, 0) + jnp.where(row >= split, 2, 0) * edge

    return code(0) == code(1)


def attend_pair(queries, keys, values, mask):
    low = lax.broadcasted_iota(jnp.int32, (144, 128), 1) < 64
    zero = jnp.zeros_like(queries)
    both = jnp.concatenate([jnp.where(low, queries, zero), jnp.where(low, zero, queries)], axis=0)
    scores = jnp.where(mask, dot_nt(both, keys), -1e9)
    weights = jnp.exp(scores - jnp.max(scores, axis=-1, keepdims=True))
    total = jnp.sum(weights, axis=-1, keepdims=True)
    mixed = dot(weights.astype(BF), values) * (1.0 / total)
    return jnp.where(low, mixed[:144], mixed[144:])


def level_one_kernel(
    place_ref,
    above_ref,
    x_ref,
    below_ref,
    col_ref,
    cls_ref,
    table_ref,
    gain1_ref,
    gain2_ref,
    inward_hbm,
    outward_hbm,
    up_hbm,
    down_hbm,
    out_ref,
    top_ref,
    bottom_ref,
    first_ref,
    last_ref,
    inward,
    outward,
    up,
    down,
    rim,
    residual,
    attended,
    ext,
    cols,
    sem,
):
    copies = [
        pltpu.make_async_copy(source, target, sem.at[index])
        for index, (source, target) in enumerate(
            ((inward_hbm, inward), (outward_hbm, outward), (up_hbm, up), (down_hbm, down))
        )
    ]
    for copy in copies:
        copy.start()
    lat, shift = place_ref[4], place_ref[5]
    split = jnp.where(shift > 0, 6 - shift, -shift)
    for row in range(3):
        ext[row] = above_ref[row * 48 : row * 48 + 48]
        ext[15 + row] = below_ref[row * 48 : row * 48 + 48]
    for row in range(12):
        ext[3 + row] = x_ref[row]
    for row in range(18):
        cols[row] = col_ref[row : row + 1].astype(F32)
    for band in range(2):
        for row in range(6):
            frame = band * 6 + row
            rim[row, 8:56] = ext[3 + shift + frame].astype(F32)
            rim[row, 7:8] = cols[3 + shift + frame]
            cls = cls_ref[:, frame : frame + 1]
            embedded = jnp.where(
                cls == 0.0, table_ref[0:1], jnp.where(cls == 1.0, table_ref[1:2], table_ref[2:3])
            )
            residual[row * 48 : (row + 1) * 48] = rim[row, 7:55] + embedded
        normal = normed(residual[...], gain1_ref[...]).astype(BF)
        if band == 1:
            edge = jnp.where((lat == 7) & (shift > 0), 1, 0)
        else:
            edge = jnp.where((lat == 0) & (shift < 0), 1, 0)
        mask = window_mask(split, edge)
        mask = jnp.concatenate([mask, mask], axis=0)
        if band == 0:
            copies[0].wait()
        for quarter in range(2):
            at = quarter * 256
            parts = [
                dot(normal, inward[:, part * 512 + at : part * 512 + at + 256]).reshape(6, 48, 256)
                for part in range(3)
            ]
            for pair in range(2):
                lanes = slice(pair * 128, pair * 128 + 128)
                for block in range(2):
                    span = slice(block * 24, block * 24 + 24)
                    queries, keys, values = (
                        part[:, span, lanes].reshape(144, 128).astype(BF) for part in parts
                    )
                    mixed = attend_pair(queries * BF(0.125), keys, values, mask)
                    attended[:, span, at + pair * 128 : at + pair * 128 + 128] = mixed.reshape(
                        6, 24, 128
                    )
        if band == 0:
            copies[1].wait()
        mid = residual[...] + dot(attended[...].reshape(288, 512).astype(BF), outward[...])
        residual[...] = mid
        normal = normed(mid, gain2_ref[...]).astype(BF)
        if band == 0:
            copies[2].wait()
            copies[3].wait()
        for chunk in range(4):
            part = slice(chunk * 512, chunk * 512 + 512)
            hidden = jax.nn.gelu(dot(normal, up[:, part])).astype(BF)
            residual[...] += dot(hidden, down[part])
        result = residual[...].astype(BF).reshape(6, 48, 512)
        out_ref[band * 6 : band * 6 + 6] = result
        if band == 0:
            top_ref[...] = result[:3]
        else:
            bottom_ref[...] = result[3:]
        for row in range(6):
            first_ref[band * 6 + row] = residual[row * 48 : row * 48 + 1].astype(BF)
            last_ref[band * 6 + row] = residual[row * 48 + 47 : row * 48 + 48].astype(BF)


def level_one(place, above, x, below, col, cls, table, gain1, gain2, inward, outward, up, down):
    return pl.pallas_call(
        level_one_kernel,
        out_shape=[
            jax.ShapeDtypeStruct((12, 48, 512), BF),
            jax.ShapeDtypeStruct((3, 48, 512), BF),
            jax.ShapeDtypeStruct((3, 48, 512), BF),
            jax.ShapeDtypeStruct((12, 1, 512), BF),
            jax.ShapeDtypeStruct((12, 1, 512), BF),
        ],
        in_specs=[SMEM] + [VMEM] * 8 + [HBM] * 4,
        out_specs=[VMEM] * 5,
        scratch_shapes=[
            pltpu.VMEM((512, 1536), BF),
            pltpu.VMEM((512, 512), BF),
            pltpu.VMEM((512, 2048), BF),
            pltpu.VMEM((2048, 512), BF),
            pltpu.VMEM((6, 56, 512), F32),
            pltpu.VMEM((288, 512), F32),
            pltpu.VMEM((6, 48, 512), F32),
            pltpu.VMEM((18, 48, 512), BF),
            pltpu.VMEM((18, 1, 512), F32),
            pltpu.SemaphoreType.DMA((4,)),
        ],
        compiler_params=pltpu.CompilerParams(vmem_limit_bytes=50 * MIB),
        cost_estimate=pl.CostEstimate(
            flops=13_000_000_000, bytes_accessed=8_000_000, transcendentals=3_000_000
        ),
        name="level_one",
    )(place, above, x, below, col, cls, table, gain1, gain2, inward, outward, up, down)


def level_two_kernel(place_ref, above_ref, f_ref, below_ref, col_ref, gain1_ref, gain2_ref, *refs):
    mine, others = refs[0:5], refs[5:10]
    (out_ref, top_ref, bottom_ref, first_ref) = refs[10:14]
    merge, outward, inward, rim, merged, total, packed, attended, ext, sem = refs[14:]
    x, y, core = place_ref[0], place_ref[1], place_ref[3]
    lat, shift = place_ref[4], place_ref[5]

    def jobs(first, second):
        lists = {"merge": [], "inward": [], "outward": []}
        count = 0
        for piece, step, lo, hi in zip(
            range(5), (0, 3, 1, 2, 2), (0, 0, 0, 0, 2), (4, 4, 4, 2, 4)
        ):
            to_x, to_y = lax.rem(x + step, 4), lax.rem(y + step, 4)
            for section in range(3):
                rows = slice(section * 32, section * 32 + 32)
                target = (merge.at[0], merge.at[1], outward)[section]
                lists["outward" if section == 2 else "merge"].append(
                    pltpu.make_async_copy(
                        first[piece].at[:, :, :, rows],
                        target.at[lo:hi, :, to_x],
                        sem.at[count],
                    )
                )
                count += 1
            for column in range(lo, hi):
                lists["inward"].append(
                    pltpu.make_async_copy(
                        second[piece].at[column - lo], inward.at[to_y, :, column], sem.at[count]
                    )
                )
                count += 1
        return lists

    @pl.when(core == 0)
    def _():
        for copies in jobs(mine, others).values():
            for copy in copies:
                copy.start()

    @pl.when(core == 1)
    def _():
        for copies in jobs(others, mine).values():
            for copy in copies:
                copy.start()

    waits = jobs(mine, others)
    for row in range(3):
        ext[row] = above_ref[row]
        ext[15 + row] = below_ref[row]
    for row in range(12):
        ext[3 + row] = f_ref[row]
    for row in range(12):
        values = ext[3 + shift + row].astype(F32)
        left = col_ref[3 + shift + row].astype(F32)
        for quarter in range(4):
            lanes = slice(quarter * 128, quarter * 128 + 128)
            rim[quarter, row, 8:56] = values[:, lanes]
            rim[quarter, row, 7:8] = left[:, lanes]
    for row in range(6):
        for part in range(4):
            for quarter in range(4):
                at = part * 512 + quarter * 128
                merged[row * 24 : row * 24 + 24, at : at + 128] = rim[
                    quarter, 2 * row + part % 2, pl.ds(7 + part // 2, 24, stride=2), :
                ]
    normal = normed(merged[...], gain1_ref[...]).astype(BF)
    for copy in waits["merge"]:
        copy.wait()
    reduced = None
    for z_hi in range(2):
        for y_at in range(4):
            block = jnp.concatenate(
                [
                    merge[half, y_at, z_hi * 4 : z_hi * 4 + 4].reshape(1024, 128)
                    for half in range(2)
                ],
                axis=1,
            )
            at = (z_hi * 4 + y_at) * 256
            part = dot_nt(normal[:, at : at + 256], block)
            reduced = part if reduced is None else reduced + part
    reduced = reduced.astype(BF).astype(F32)
    total[...] = reduced
    normal = normed(reduced, gain2_ref[...]).astype(BF)
    for copy in waits["inward"]:
        copy.wait()
    for third in range(3):
        for z_hi in range(2):
            for y_at in range(0, 4, 2):
                block = jnp.concatenate(
                    [
                        inward[y_at + half, z_hi * 4 : z_hi * 4 + 4].reshape(3072, 128)[
                            third * 1024 : third * 1024 + 1024
                        ]
                        for half in range(2)
                    ],
                    axis=1,
                )
                at = (z_hi * 4 + y_at) * 128
                part = dot_nt(normal[:, at : at + 256], block)
                if z_hi + y_at == 0:
                    sums = part
                else:
                    sums = sums + part
        if third == 0:
            sums = sums * 0.125
        packed[:, third * 1024 : third * 1024 + 1024] = sums.astype(BF)

    split = jnp.where(shift > 0, 6 - shift, -shift)
    edge = jnp.where(((lat == 7) & (shift > 0)) | ((lat == 0) & (shift < 0)), 1, 0)
    mask = window_mask(split, edge)
    mask = jnp.concatenate([mask, mask], axis=0)
    for pair in range(8):
        at = pair * 128
        mixed = attend_pair(
            packed[:, at : at + 128],
            packed[:, 1024 + at : 1024 + at + 128],
            packed[:, 2048 + at : 2048 + at + 128],
            mask,
        )
        attended[:, at : at + 128] = mixed.astype(BF)
    for copy in waits["outward"]:
        copy.wait()
    sums = total[...]
    for z_hi in range(2):
        for y_at in range(0, 4, 2):
            block = jnp.concatenate(
                [
                    outward[y_at + half, z_hi * 4 : z_hi * 4 + 4].reshape(1024, 128)
                    for half in range(2)
                ],
                axis=1,
            )
            at = (z_hi * 4 + y_at) * 128
            sums = sums + dot_nt(attended[:, at : at + 256], block)
    total[...] = sums
    for row in range(6):
        result = total[row * 24 : row * 24 + 24].astype(BF)
        out_ref[row] = result
        if row < 3:
            top_ref[row] = result
        else:
            bottom_ref[row - 3] = result
        first_ref[row] = total[row * 24 : row * 24 + 1].astype(BF)


def level_two(place, above, f, below, col, gain1, gain2, mine, others):
    return pl.pallas_call(
        level_two_kernel,
        out_shape=[
            jax.ShapeDtypeStruct((6, 24, 1024), BF),
            jax.ShapeDtypeStruct((3, 24, 1024), BF),
            jax.ShapeDtypeStruct((3, 24, 1024), BF),
            jax.ShapeDtypeStruct((6, 1, 1024), BF),
        ],
        in_specs=[SMEM] + [VMEM] * 6 + [ANY] * 10,
        out_specs=[VMEM] * 4,
        scratch_shapes=[
            pltpu.VMEM((2, 4, 8, 4, 2, 32, 128), BF),
            pltpu.VMEM((4, 8, 4, 2, 32, 128), BF),
            pltpu.VMEM((4, 8, 4, 2, 96, 128), BF),
            pltpu.VMEM((4, 12, 56, 128), F32),
            pltpu.VMEM((144, 2048), F32),
            pltpu.VMEM((144, 1024), F32),
            pltpu.VMEM((144, 3072), BF),
            pltpu.VMEM((144, 1024), BF),
            pltpu.VMEM((18, 48, 512), BF),
            pltpu.SemaphoreType.DMA((31,)),
        ],
        compiler_params=pltpu.CompilerParams(vmem_limit_bytes=32 * MIB),
        cost_estimate=pl.CostEstimate(
            flops=11_000_000_000, bytes_accessed=14_000_000, transcendentals=1_000_000
        ),
        name="level_two",
    )(place, above, f, below, col, gain1, gain2, *mine, *others)


def edges(top, bottom):
    return to_cell(bottom, 1, 0), to_cell(top, -1, 0)


def column(above, col, below, index, direction):
    part = jnp.concatenate([above[:, index], col, below[:, index]], axis=0)
    return to_cell(part, 0, direction)


def moved_rows(col, start):
    return lax.dynamic_slice_in_dim(col, start, 12, 0)


def moved_back(shift, above, grid, below, col):
    whole = jnp.concatenate([above, grid, below], axis=0)
    count = grid.shape[0]
    whole = lax.dynamic_slice_in_dim(whole, 3 - shift, count, 0)
    col = lax.dynamic_slice_in_dim(col, 3 - shift, count, 0)
    return jnp.concatenate([whole[:, 1:], col], axis=1)


def line(*values):
    values = jnp.concatenate([value.reshape(-1) for value in values])
    return jnp.pad(values, (0, 512 - values.shape[0])).reshape(1, 512)


def shards(
    latent,
    surface,
    table,
    shifts,
    gain_one,
    inward_one,
    outward_one,
    gain_ffn,
    ffn_up,
    ffn_down,
    gain_merge,
    merge_proj,
    gain_two,
    inward_two,
    outward_two,
):
    lat, lon = lax.axis_index("lat"), lax.axis_index("lon")
    shift = jnp.where(shifts[0] <= 3, shifts[0], shifts[0] - 6)
    x, y, z, core = (lon // 2) % 4, lat % 4, (lat // 4) * 4 + lon // 8, lon % 2
    place = jnp.stack([x, y, z, core, lat, shift, jnp.where(core == 0, y, x)]).astype(jnp.int32)

    classes = surface.astype(BF)

    def message(part):
        return jnp.concatenate([latent[part].reshape(-1, 512), line(classes[part])])

    above = to_cell(message(slice(9, 12)), 1, 0)
    below = to_cell(message(slice(0, 3)), -1, 0)

    keep, send = pack(place, merge_proj, inward_two, outward_two)
    shard = jnp.stack([keep, to_core(send)])
    near = jnp.stack([along_z(shard, 1), shard, along_z(shard, -1)])
    far_low, far_high = along_z(near, 3), along_z(near[:2], -3)

    cls = jnp.concatenate(
        [above[144, :144].reshape(3, 48), classes, below[144, :144].reshape(3, 48)]
    )
    left = to_cell(
        jnp.concatenate([above[47:144:48], latent[:, -1], below[47:144:48], line(cls[:, -1])]), 0, 1
    )
    cls = jnp.concatenate([left[18, :18, None], cls[:, :-1]], axis=1)
    cls = jnp.pad(moved_rows(cls, 3 + shift).astype(F32).T, ((0, 0), (0, 4)))
    far_low, far_high, left = lax.optimization_barrier((far_low, far_high, left))
    block = assemble_z(place, far_low, near, far_high)
    from_left, from_right = along(block, False, 1), along(block, False, -1)
    block = assemble(
        place, block, from_left, from_right,
        along(from_left[:4], False, 1), along(from_right[4:], False, -1),
    )
    from_left, from_right = along(block, True, 1), along(block, True, -1)
    frame, top, bottom, first, last = level_one(
        place, above, latent, below, after(left, block), cls, table,
        gain_one.reshape(1, -1), gain_ffn.reshape(1, -1),
        inward_one, outward_one, ffn_up, ffn_down,
    )
    from_left, from_right = lax.optimization_barrier((from_left, from_right, top))[:2]
    half0, half1 = from_left[:2], from_right[2:]
    mine = [block, from_left, from_right, along(half0, True, 1), along(half1, True, -1)]
    others = [to_core(after(block, half0, half1)), to_core(from_left), to_core(from_right)]

    above, below = edges(top, bottom)
    above, below = lax.optimization_barrier((above, below, others[0]))[:2]
    left = column(above[:, :, None], last, below[:, :, None], 47, 1)
    others += [to_core(after(piece, left)) for piece in mine[3:]]
    right = column(after(above, *others)[:, :, None], first, below[:, :, None], 0, -1)
    out_one = moved_back(shift, above, frame, below, right)
    frame, top, bottom, first = level_two(
        place, above, frame, below, left,
        gain_merge.reshape(1, -1), gain_two.reshape(1, -1), mine, others,
    )
    above, below = edges(top, bottom)
    right = column(above[:, :, None], first, below[:, :, None], 0, -1)
    return out_one, moved_back(shift, above, frame, below, right)


def solution(mesh):
    placed = (
        P("lat", "lon", None),
        P("lat", "lon"),
        P(),
        P(),
        P(),
        P(),
        P(),
        P(),
        P(),
        P(),
        P(),
        P("lat", "lon"),
        P(),
        P("lat", "lon"),
        P("lat", "lon"),
    )
    return jax.shard_map(
        shards,
        mesh=mesh,
        in_specs=placed,
        out_specs=(P("lat", "lon", None), P("lat", "lon", None)),
        check_vma=False,
    )
```

```python
import jax
import jax.numpy as jnp
from jax import lax
from jax.experimental import pallas as pl
from jax.experimental.pallas import tpu as pltpu
from jax.sharding import PartitionSpec as P

EPS = 1e-05
BF = jnp.bfloat16
F32 = jnp.float32
AXES = ("lat", "lon")
VMEM = pl.BlockSpec(memory_space=pltpu.VMEM)
SMEM = pl.BlockSpec(memory_space=pltpu.SMEM)
ANY = pl.BlockSpec(memory_space=pl.ANY)
HBM = pl.BlockSpec(memory_space=pltpu.HBM)
MIB = 1024 * 1024

PLACES = [(x, y, z, c) for z in range(8) for y in range(4) for x in range(4) for c in range(2)]


def number(x, y, z, c):
    x, y, z, c = x % 4, y % 4, z % 8, c % 2
    return ((z // 4) * 4 + y) * 32 + ((z % 4) * 4 + x) * 2 + c


def move(array, steps):
    pairs = []
    for x, y, z, c in PLACES:
        dx, dy, dz, dc = steps[c]
        pairs.append((number(x, y, z, c), number(x + dx, y + dy, z + dz, c + dc)))
    return lax.ppermute(array, AXES, pairs)


def along_z(array, step):
    return move(array, ((0, 0, step, 0),) * 2)


def to_core(array):
    return move(array, ((0, 0, 0, 1),) * 2)


def along(array, last, step):
    by_x, by_y = (step, 0, 0, 0), (0, step, 0, 0)
    return move(array, (by_x, by_y) if last else (by_y, by_x))


def to_cell(array, dlat, dlon):
    pairs = [
        (i * 32 + j, ((i + dlat) % 8) * 32 + (j + dlon) % 32) for i in range(8) for j in range(32)
    ]
    return lax.ppermute(array, AXES, pairs)


def after(value, *others):
    return lax.optimization_barrier((value,) + others)[0]


def pack_kernel(place_ref, merge_ref, inward_ref, outward_ref, keep_ref, send_ref):
    def store(first, second):
        first[0:32] = merge_ref[:, :128]
        first[32:64] = merge_ref[:, 128:]
        first[64:96] = outward_ref[...]
        second[...] = inward_ref[...]

    @pl.when(place_ref[3] == 0)
    def _():
        store(keep_ref, send_ref)

    @pl.when(place_ref[3] == 1)
    def _():
        store(send_ref, keep_ref)


def pack(place, merge, inward, outward):
    return pl.pallas_call(
        pack_kernel,
        out_shape=[jax.ShapeDtypeStruct((96, 128), BF)] * 2,
        in_specs=[SMEM] + [VMEM] * 3,
        out_specs=[VMEM] * 2,
        compiler_params=pltpu.CompilerParams(vmem_limit_bytes=56 * MIB),
        name="pack",
    )(place, merge.T, inward.T, outward.T)


def assemble_z_kernel(place_ref, low_ref, near_ref, high_ref, out_ref, sem):
    z, core = place_ref[2], place_ref[3]
    copies = []
    for step in range(8):
        ref, first = ((low_ref, 0), (near_ref, 3), (high_ref, 6))[step // 3]
        to = lax.rem(z + 4 + step, 8)
        for other in range(2):
            target = out_ref.at[to, lax.rem(core + other, 2)]
            copies.append(
                pltpu.make_async_copy(ref.at[step - first, other], target, sem.at[len(copies)])
            )
    for copy in copies:
        copy.start()
    for copy in copies:
        copy.wait()


def assemble_z(place, low, near, high):
    return pl.pallas_call(
        assemble_z_kernel,
        out_shape=jax.ShapeDtypeStruct((8, 2, 96, 128), BF),
        in_specs=[SMEM] + [ANY] * 3,
        out_specs=VMEM,
        scratch_shapes=[pltpu.SemaphoreType.DMA((16,))],
        compiler_params=pltpu.CompilerParams(vmem_limit_bytes=6 * MIB),
        name="assemble_z",
    )(place, low, near, high)


def assemble_kernel(place_ref, own, left, right, half0, half1, out_ref, sem):
    at = place_ref[6]
    copies = [
        pltpu.make_async_copy(piece, out_ref.at[lax.rem(at + step, 4), lo:hi], sem.at[index])
        for index, (piece, step, lo, hi) in enumerate(
            ((own, 0, 0, 8), (left, 3, 0, 8), (right, 1, 0, 8), (half0, 2, 0, 4), (half1, 2, 4, 8))
        )
    ]
    for copy in copies:
        copy.start()
    for copy in copies:
        copy.wait()


def assemble(place, *pieces):
    return pl.pallas_call(
        assemble_kernel,
        out_shape=jax.ShapeDtypeStruct((4, 8, 2, 96, 128), BF),
        in_specs=[SMEM] + [ANY] * 5,
        out_specs=VMEM,
        scratch_shapes=[pltpu.SemaphoreType.DMA((5,))],
        compiler_params=pltpu.CompilerParams(vmem_limit_bytes=6 * MIB),
        name="assemble",
    )(place, *pieces)


def normed(hidden, gain):
    centre = jnp.mean(hidden, axis=-1, keepdims=True)
    centred = hidden - centre
    variance = jnp.mean(centred * centred, axis=-1, keepdims=True)
    return centred * lax.rsqrt(variance + EPS) * gain


def dot(a, b):
    return jnp.dot(a, b, preferred_element_type=F32)


def dot_nt(a, b):
    return lax.dot_general(a, b, (((1,), (1,)), ((), ())), preferred_element_type=F32)


def window_mask(split, edge):
    def code(axis):
        token = lax.broadcasted_iota(jnp.int32, (144, 144), axis)
        row = (token * 2731) >> 16
        col = token - 24 * row
        return jnp.where(col >= 12, 1, 0) + jnp.where(row >= split, 2, 0) * edge

    return code(0) == code(1)


def attend_pair(queries, keys, values, mask):
    low = lax.broadcasted_iota(jnp.int32, (144, 128), 1) < 64
    zero = jnp.zeros_like(queries)
    both = jnp.concatenate([jnp.where(low, queries, zero), jnp.where(low, zero, queries)], axis=0)
    scores = jnp.where(mask, dot_nt(both, keys), -1e9)
    weights = jnp.exp(scores - jnp.max(scores, axis=-1, keepdims=True))
    total = jnp.sum(weights, axis=-1, keepdims=True)
    mixed = dot(weights.astype(BF), values) * (1.0 / total)
    return jnp.where(low, mixed[:144], mixed[144:])


def fill(ext, at, part0, part1):
    ext[at] = part0[0:48]
    ext[at + 1, 0:32] = part0[48:80]
    ext[at + 1, 32:48] = part1[0:16]
    ext[at + 2] = part1[16:64]


def level_one_kernel(
    place_ref,
    above0_ref,
    above1_ref,
    x_ref,
    below0_ref,
    below1_ref,
    col_ref,
    cls_ref,
    table_ref,
    gain1_ref,
    gain2_ref,
    inward_hbm,
    outward_hbm,
    up_hbm,
    down_hbm,
    out_ref,
    top0_ref,
    top1_ref,
    bottom0_ref,
    bottom1_ref,
    first_ref,
    last_ref,
    inward,
    outward,
    up,
    down,
    rim,
    residual,
    attended,
    ext,
    cols,
    sem,
):
    copies = [
        pltpu.make_async_copy(source, target, sem.at[index])
        for index, (source, target) in enumerate(
            ((inward_hbm, inward), (outward_hbm, outward), (up_hbm, up), (down_hbm, down))
        )
    ]
    for copy in copies:
        copy.start()
    lat, shift = place_ref[4], place_ref[5]
    split = jnp.where(shift > 0, 6 - shift, -shift)
    for at, part0, part1 in ((0, above0_ref, above1_ref), (15, below0_ref, below1_ref)):
        fill(ext, at, part0, part1)
        for row in range(3):
            cols[at + row] = part1[64 + row : 65 + row].astype(F32)
    for row in range(12):
        ext[3 + row] = x_ref[row]
        cols[3 + row] = col_ref[row : row + 1].astype(F32)
    for band in range(2):
        for row in range(6):
            frame = band * 6 + row
            rim[row, 8:56] = ext[3 + shift + frame].astype(F32)
            rim[row, 7:8] = cols[3 + shift + frame]
            cls = cls_ref[:, frame : frame + 1]
            embedded = jnp.where(
                cls == 0.0, table_ref[0:1], jnp.where(cls == 1.0, table_ref[1:2], table_ref[2:3])
            )
            residual[row * 48 : (row + 1) * 48] = rim[row, 7:55] + embedded
        normal = normed(residual[...], gain1_ref[...]).astype(BF)
        if band == 1:
            edge = jnp.where((lat == 7) & (shift > 0), 1, 0)
        else:
            edge = jnp.where((lat == 0) & (shift < 0), 1, 0)
        mask = window_mask(split, edge)
        mask = jnp.concatenate([mask, mask], axis=0)
        if band == 0:
            copies[0].wait()
        for quarter in range(2):
            at = quarter * 256
            parts = [
                dot(normal, inward[:, part * 512 + at : part * 512 + at + 256]).reshape(6, 48, 256)
                for part in range(3)
            ]
            for pair in range(2):
                lanes = slice(pair * 128, pair * 128 + 128)
                for block in range(2):
                    span = slice(block * 24, block * 24 + 24)
                    queries, keys, values = (
                        part[:, span, lanes].reshape(144, 128).astype(BF) for part in parts
                    )
                    mixed = attend_pair(queries * BF(0.125), keys, values, mask)
                    attended[:, span, at + pair * 128 : at + pair * 128 + 128] = mixed.reshape(
                        6, 24, 128
                    )
        if band == 0:
            copies[1].wait()
        mid = residual[...] + dot(attended[...].reshape(288, 512).astype(BF), outward[...])
        residual[...] = mid
        normal = normed(mid, gain2_ref[...]).astype(BF)
        if band == 0:
            copies[2].wait()
            copies[3].wait()
        for chunk in range(4):
            part = slice(chunk * 512, chunk * 512 + 512)
            hidden = jax.nn.gelu(dot(normal, up[:, part])).astype(BF)
            residual[...] += dot(hidden, down[part])
        result = residual[...].astype(BF)
        out_ref[band * 6 : band * 6 + 6] = result.reshape(6, 48, 512)
        if band == 0:
            top0_ref[...] = result[0:80]
            top1_ref[...] = result[80:144]
        else:
            bottom0_ref[...] = result[144:224]
            bottom1_ref[...] = result[224:288]
        for row in range(6):
            first_ref[band * 6 + row] = residual[row * 48 : row * 48 + 1].astype(BF)
            last_ref[band * 6 + row] = residual[row * 48 + 47 : row * 48 + 48].astype(BF)


def level_one(place, above, x, below, col, cls, table, gain1, gain2, *weights):
    return pl.pallas_call(
        level_one_kernel,
        out_shape=[
            jax.ShapeDtypeStruct((12, 48, 512), BF),
            jax.ShapeDtypeStruct((80, 512), BF),
            jax.ShapeDtypeStruct((64, 512), BF),
            jax.ShapeDtypeStruct((80, 512), BF),
            jax.ShapeDtypeStruct((64, 512), BF),
            jax.ShapeDtypeStruct((12, 1, 512), BF),
            jax.ShapeDtypeStruct((12, 1, 512), BF),
        ],
        in_specs=[SMEM] + [VMEM] * 10 + [HBM] * 4,
        out_specs=[VMEM] * 7,
        scratch_shapes=[
            pltpu.VMEM((512, 1536), BF),
            pltpu.VMEM((512, 512), BF),
            pltpu.VMEM((512, 2048), BF),
            pltpu.VMEM((2048, 512), BF),
            pltpu.VMEM((6, 56, 512), F32),
            pltpu.VMEM((288, 512), F32),
            pltpu.VMEM((6, 48, 512), F32),
            pltpu.VMEM((18, 48, 512), BF),
            pltpu.VMEM((18, 1, 512), F32),
            pltpu.SemaphoreType.DMA((4,)),
        ],
        compiler_params=pltpu.CompilerParams(vmem_limit_bytes=50 * MIB),
        cost_estimate=pl.CostEstimate(
            flops=13_000_000_000, bytes_accessed=8_000_000, transcendentals=3_000_000
        ),
        name="level_one",
    )(place, *above, x, *below, col, cls, table, gain1, gain2, *weights)


def level_two_kernel(place_ref, f_ref, col_ref, gain1_ref, gain2_ref, *refs):
    above, below, refs = refs[0:2], refs[2:4], refs[4:]
    mine, others = refs[0:5], refs[5:10]
    (out_ref, top_ref, bottom_ref, first_ref) = refs[10:14]
    merge, outward, inward, rim, merged, total, packed, attended, ext, sem = refs[14:]
    x, y, core = place_ref[0], place_ref[1], place_ref[3]
    lat, shift = place_ref[4], place_ref[5]

    def jobs(first, second):
        lists = {"merge": [], "inward": [], "outward": []}
        count = 0
        for piece, step, lo, hi in zip(
            range(5), (0, 3, 1, 2, 2), (0, 0, 0, 0, 2), (4, 4, 4, 2, 4)
        ):
            to_x, to_y = lax.rem(x + step, 4), lax.rem(y + step, 4)
            for section in range(3):
                rows = slice(section * 32, section * 32 + 32)
                target = (merge.at[0], merge.at[1], outward)[section]
                lists["outward" if section == 2 else "merge"].append(
                    pltpu.make_async_copy(
                        first[piece].at[:, :, :, rows],
                        target.at[lo:hi, :, to_x],
                        sem.at[count],
                    )
                )
                count += 1
            for column in range(lo, hi):
                lists["inward"].append(
                    pltpu.make_async_copy(
                        second[piece].at[column - lo], inward.at[to_y, :, column], sem.at[count]
                    )
                )
                count += 1
        return lists

    @pl.when(core == 0)
    def _():
        for copies in jobs(mine, others).values():
            for copy in copies:
                copy.start()

    @pl.when(core == 1)
    def _():
        for copies in jobs(others, mine).values():
            for copy in copies:
                copy.start()

    waits = jobs(mine, others)
    fill(ext, 0, *above)
    fill(ext, 15, *below)
    for row in range(12):
        ext[3 + row] = f_ref[row]
    for row in range(12):
        values = ext[3 + shift + row].astype(F32)
        left = col_ref[3 + shift + row].astype(F32)
        for quarter in range(4):
            lanes = slice(quarter * 128, quarter * 128 + 128)
            rim[quarter, row, 8:56] = values[:, lanes]
            rim[quarter, row, 7:8] = left[:, lanes]
    for row in range(6):
        for part in range(4):
            for quarter in range(4):
                at = part * 512 + quarter * 128
                merged[row * 24 : row * 24 + 24, at : at + 128] = rim[
                    quarter, 2 * row + part % 2, pl.ds(7 + part // 2, 24, stride=2), :
                ]
    normal = normed(merged[...], gain1_ref[...]).astype(BF)
    for copy in waits["merge"]:
        copy.wait()
    reduced = None
    for z_hi in range(2):
        for y_at in range(4):
            block = jnp.concatenate(
                [
                    merge[half, y_at, z_hi * 4 : z_hi * 4 + 4].reshape(1024, 128)
                    for half in range(2)
                ],
                axis=1,
            )
            at = (z_hi * 4 + y_at) * 256
            part = dot_nt(normal[:, at : at + 256], block)
            reduced = part if reduced is None else reduced + part
    reduced = reduced.astype(BF).astype(F32)
    total[...] = reduced
    normal = normed(reduced, gain2_ref[...]).astype(BF)
    for copy in waits["inward"]:
        copy.wait()
    for third in range(3):
        for z_hi in range(2):
            for y_at in range(0, 4, 2):
                block = jnp.concatenate(
                    [
                        inward[y_at + half, z_hi * 4 : z_hi * 4 + 4].reshape(3072, 128)[
                            third * 1024 : third * 1024 + 1024
                        ]
                        for half in range(2)
                    ],
                    axis=1,
                )
                at = (z_hi * 4 + y_at) * 128
                part = dot_nt(normal[:, at : at + 256], block)
                if z_hi + y_at == 0:
                    sums = part
                else:
                    sums = sums + part
        if third == 0:
            sums = sums * 0.125
        packed[:, third * 1024 : third * 1024 + 1024] = sums.astype(BF)

    split = jnp.where(shift > 0, 6 - shift, -shift)
    edge = jnp.where(((lat == 7) & (shift > 0)) | ((lat == 0) & (shift < 0)), 1, 0)
    mask = window_mask(split, edge)
    mask = jnp.concatenate([mask, mask], axis=0)
    for pair in range(8):
        at = pair * 128
        mixed = attend_pair(
            packed[:, at : at + 128],
            packed[:, 1024 + at : 1024 + at + 128],
            packed[:, 2048 + at : 2048 + at + 128],
            mask,
        )
        attended[:, at : at + 128] = mixed.astype(BF)
    for copy in waits["outward"]:
        copy.wait()
    sums = total[...]
    for z_hi in range(2):
        for y_at in range(0, 4, 2):
            block = jnp.concatenate(
                [
                    outward[y_at + half, z_hi * 4 : z_hi * 4 + 4].reshape(1024, 128)
                    for half in range(2)
                ],
                axis=1,
            )
            at = (z_hi * 4 + y_at) * 128
            sums = sums + dot_nt(attended[:, at : at + 256], block)
    total[...] = sums
    for row in range(6):
        result = total[row * 24 : row * 24 + 24].astype(BF)
        out_ref[row] = result
        if row < 3:
            top_ref[row] = result
        else:
            bottom_ref[row - 3] = result
        first_ref[row] = total[row * 24 : row * 24 + 1].astype(BF)


def level_two(place, above, f, below, col, gain1, gain2, mine, others):
    return pl.pallas_call(
        level_two_kernel,
        out_shape=[
            jax.ShapeDtypeStruct((6, 24, 1024), BF),
            jax.ShapeDtypeStruct((3, 24, 1024), BF),
            jax.ShapeDtypeStruct((3, 24, 1024), BF),
            jax.ShapeDtypeStruct((6, 1, 1024), BF),
        ],
        in_specs=[SMEM] + [VMEM] * 8 + [ANY] * 10,
        out_specs=[VMEM] * 4,
        scratch_shapes=[
            pltpu.VMEM((2, 4, 8, 4, 2, 32, 128), BF),
            pltpu.VMEM((4, 8, 4, 2, 32, 128), BF),
            pltpu.VMEM((4, 8, 4, 2, 96, 128), BF),
            pltpu.VMEM((4, 12, 56, 128), F32),
            pltpu.VMEM((144, 2048), F32),
            pltpu.VMEM((144, 1024), F32),
            pltpu.VMEM((144, 3072), BF),
            pltpu.VMEM((144, 1024), BF),
            pltpu.VMEM((18, 48, 512), BF),
            pltpu.SemaphoreType.DMA((31,)),
        ],
        compiler_params=pltpu.CompilerParams(vmem_limit_bytes=32 * MIB),
        cost_estimate=pl.CostEstimate(
            flops=11_000_000_000, bytes_accessed=14_000_000, transcendentals=1_000_000
        ),
        name="level_two",
    )(place, f, col, gain1, gain2, *above, *below, *mine, *others)


def edges(top, bottom):
    return to_cell(bottom, 1, 0), to_cell(top, -1, 0)


def column(above, col, below, index, direction):
    part = jnp.concatenate([above[:, index], col, below[:, index]], axis=0)
    return to_cell(part, 0, direction)


def moved_rows(col, start):
    return lax.dynamic_slice_in_dim(col, start, 12, 0)


def moved_back(shift, above, grid, below, col):
    whole = jnp.concatenate([above, grid, below], axis=0)
    count = grid.shape[0]
    whole = lax.dynamic_slice_in_dim(whole, 3 - shift, count, 0)
    col = lax.dynamic_slice_in_dim(col, 3 - shift, count, 0)
    return jnp.concatenate([whole[:, 1:], col], axis=1)


def line(*values):
    values = jnp.concatenate([value.reshape(-1) for value in values])
    return jnp.pad(values, (0, 512 - values.shape[0])).reshape(1, 512)


def shards(
    latent,
    surface,
    table,
    shifts,
    gain_one,
    inward_one,
    outward_one,
    gain_ffn,
    ffn_up,
    ffn_down,
    gain_merge,
    merge_proj,
    gain_two,
    inward_two,
    outward_two,
):
    lat, lon = lax.axis_index("lat"), lax.axis_index("lon")
    shift = jnp.where(shifts[0] <= 3, shifts[0], shifts[0] - 6)
    x, y, z, core = (lon // 2) % 4, lat % 4, (lat // 4) * 4 + lon // 8, lon % 2
    place = jnp.stack([x, y, z, core, lat, shift, jnp.where(core == 0, y, x)]).astype(jnp.int32)

    keep, send = pack(place, merge_proj, inward_two, outward_two)
    shard = jnp.stack([keep, to_core(send)])
    near = jnp.stack([along_z(shard, 1), shard, along_z(shard, -1)])
    far_low, far_high = along_z(near, 3), along_z(near[:2], -3)

    classes = surface.astype(BF)
    left = to_cell(jnp.concatenate([latent[:, -1], line(classes[:, -1])]), 0, 1)

    far_low, far_high, left = lax.optimization_barrier((far_low, far_high, left))
    left_cls = left[12, :12]

    def message(part):
        values = latent[part].reshape(-1, 512)
        extra = line(classes[part], left_cls[part])
        return values[:80], jnp.concatenate([values[80:], left[:12][part], extra])

    above0, above1 = message(slice(9, 12))
    below0, below1 = message(slice(0, 3))
    above0, below0 = after((above0, below0), far_low, far_high)
    above0, below0 = to_cell(above0, 1, 0), to_cell(below0, -1, 0)
    block = assemble_z(place, far_low, near, far_high)

    from_left, from_right = along(block, False, 1), along(block, False, -1)
    half0, half1, above0, below0 = lax.optimization_barrier(
        (from_left[:4], from_right[4:], above0, below0)
    )
    above1, below1 = after((above1, below1), half0, half1)
    above1, below1 = to_cell(above1, 1, 0), to_cell(below1, -1, 0)
    block = assemble(
        place, block, from_left, from_right, along(half0, False, 1), along(half1, False, -1)
    )
    block, above1, below1 = lax.optimization_barrier((block, above1, below1))

    from_left, from_right = along(block, True, 1), along(block, True, -1)
    cls = jnp.concatenate(
        [above1[67, :144].reshape(3, 48), classes, below1[67, :144].reshape(3, 48)]
    )
    left_cls = jnp.concatenate([above1[67, 144:147], left_cls, below1[67, 144:147]])
    cls = jnp.concatenate([left_cls[:, None], cls[:, :-1]], axis=1)
    cls = jnp.pad(moved_rows(cls, 3 + shift).astype(F32).T, ((0, 0), (0, 4)))
    frame, top0, top1, bottom0, bottom1, first, last = level_one(
        place, (above0, above1), latent, (below0, below1), left, cls, table,
        gain_one.reshape(1, -1), gain_ffn.reshape(1, -1),
        inward_one, outward_one, ffn_up, ffn_down,
    )
    above0, below0 = edges(top0, bottom0)
    from_left, from_right = lax.optimization_barrier((from_left, from_right, top0))[:2]
    half0, half1, above0, below0 = lax.optimization_barrier(
        (from_left[:2], from_right[2:], above0, below0)
    )
    mine = [block, from_left, from_right, along(half0, True, 1), along(half1, True, -1)]
    others = [to_core(after(block, half0, half1)), to_core(from_left), to_core(from_right)]

    above1, below1 = edges(*after((top1, bottom1), half0, half1))
    above1, below1 = lax.optimization_barrier((above1, below1, others[0]))[:2]
    left = to_cell(
        jnp.concatenate(
            [
                above0[47:48, None], above1[15:64:48, None], last,
                below0[47:48, None], below1[15:64:48, None],
            ]
        ),
        0, 1,
    )
    others += [to_core(after(piece, left)) for piece in mine[3:]]
    right = to_cell(
        jnp.concatenate(
            [
                after(above0, *others)[0:80:48, None], above1[16:17, None], first,
                below0[0:80:48, None], below1[16:17, None],
            ]
        ),
        0, -1,
    )
    out_one = moved_back(
        shift,
        jnp.concatenate([above0, above1]).reshape(3, 48, 512),
        frame,
        jnp.concatenate([below0, below1]).reshape(3, 48, 512),
        right,
    )
    frame, top, bottom, first = level_two(
        place, (above0, above1), frame, (below0, below1), left,
        gain_merge.reshape(1, -1), gain_two.reshape(1, -1), mine, others,
    )
    above, below = edges(top, bottom)
    right = column(above[:, :, None], first, below[:, :, None], 0, -1)
    return out_one, moved_back(shift, above, frame, below, right)


def solution(mesh):
    placed = (
        P("lat", "lon", None),
        P("lat", "lon"),
        P(),
        P(),
        P(),
        P(),
        P(),
        P(),
        P(),
        P(),
        P(),
        P("lat", "lon"),
        P(),
        P("lat", "lon"),
        P("lat", "lon"),
    )
    return jax.shard_map(
        shards,
        mesh=mesh,
        in_specs=placed,
        out_specs=(P("lat", "lon", None), P("lat", "lon", None)),
        check_vma=False,
    )
```

```python
import jax
import jax.numpy as jnp
from jax import lax
from jax.experimental import pallas as pl
from jax.experimental.pallas import tpu as pltpu
from jax.sharding import PartitionSpec as P

EPS = 1e-05
BF = jnp.bfloat16
F32 = jnp.float32
AXES = ("lat", "lon")
VMEM = pl.BlockSpec(memory_space=pltpu.VMEM)
SMEM = pl.BlockSpec(memory_space=pltpu.SMEM)
ANY = pl.BlockSpec(memory_space=pl.ANY)
HBM = pl.BlockSpec(memory_space=pltpu.HBM)
MIB = 1024 * 1024

PLACES = [(x, y, z, c) for z in range(8) for y in range(4) for x in range(4) for c in range(2)]


def number(x, y, z, c):
    x, y, z, c = x % 4, y % 4, z % 8, c % 2
    return ((z // 4) * 4 + y) * 32 + ((z % 4) * 4 + x) * 2 + c


def move(array, steps):
    pairs = []
    for x, y, z, c in PLACES:
        dx, dy, dz, dc = steps[c]
        pairs.append((number(x, y, z, c), number(x + dx, y + dy, z + dz, c + dc)))
    return lax.ppermute(array, AXES, pairs)


def along_z(array, step):
    return move(array, ((0, 0, step, 0),) * 2)


def to_core(array):
    return move(array, ((0, 0, 0, 1),) * 2)


def along(array, last, step):
    by_x, by_y = (step, 0, 0, 0), (0, step, 0, 0)
    return move(array, (by_x, by_y) if last else (by_y, by_x))


def to_cell(array, dlat, dlon):
    pairs = [
        (i * 32 + j, ((i + dlat) % 8) * 32 + (j + dlon) % 32) for i in range(8) for j in range(32)
    ]
    return lax.ppermute(array, AXES, pairs)


def after(value, *others):
    return lax.optimization_barrier((value,) + others)[0]


def pack_kernel(place_ref, merge_ref, inward_ref, outward_ref, keep_ref, send_ref):
    def store(first, second):
        first[0:32] = merge_ref[:, :128]
        first[32:64] = merge_ref[:, 128:]
        first[64:96] = outward_ref[...]
        second[...] = inward_ref[...]

    @pl.when(place_ref[3] == 0)
    def _():
        store(keep_ref, send_ref)

    @pl.when(place_ref[3] == 1)
    def _():
        store(send_ref, keep_ref)


def pack(place, merge, inward, outward):
    return pl.pallas_call(
        pack_kernel,
        out_shape=[jax.ShapeDtypeStruct((96, 128), BF)] * 2,
        in_specs=[SMEM] + [VMEM] * 3,
        out_specs=[VMEM] * 2,
        compiler_params=pltpu.CompilerParams(vmem_limit_bytes=56 * MIB),
        name="pack",
    )(place, merge.T, inward.T, outward.T)


def assemble_z_kernel(place_ref, low_ref, near_ref, high_ref, out_ref, sem):
    z, core = place_ref[2], place_ref[3]
    copies = []
    for step in range(8):
        ref, first = ((low_ref, 0), (near_ref, 3), (high_ref, 6))[step // 3]
        to = lax.rem(z + 4 + step, 8)
        for other in range(2):
            target = out_ref.at[to, lax.rem(core + other, 2)]
            copies.append(
                pltpu.make_async_copy(ref.at[step - first, other], target, sem.at[len(copies)])
            )
    for copy in copies:
        copy.start()
    for copy in copies:
        copy.wait()


def assemble_z(place, low, near, high):
    return pl.pallas_call(
        assemble_z_kernel,
        out_shape=jax.ShapeDtypeStruct((8, 2, 96, 128), BF),
        in_specs=[SMEM] + [ANY] * 3,
        out_specs=VMEM,
        scratch_shapes=[pltpu.SemaphoreType.DMA((16,))],
        compiler_params=pltpu.CompilerParams(vmem_limit_bytes=6 * MIB),
        name="assemble_z",
    )(place, low, near, high)


def assemble_kernel(place_ref, own, left, right, half0, half1, whole_ref, out0_ref, out1_ref, sem):
    at = place_ref[6]
    pieces = ((own, 0, 0, 8), (left, 3, 0, 8), (right, 1, 0, 8), (half0, 2, 0, 4), (half1, 2, 4, 8))
    copies = []
    for index, (piece, step, lo, hi) in enumerate(pieces):
        to = lax.rem(at + step, 4)
        copies.append(pltpu.make_async_copy(piece, whole_ref.at[to, lo:hi], sem.at[0, index]))
    for copy in copies:
        copy.start()
    for index, (piece, step, lo, hi) in enumerate(pieces):
        to = lax.rem(at + step, 4)
        for part, out_ref in enumerate((out0_ref, out1_ref)):
            inner = jnp.clip(to - 2 * part, 0, 1)

            @pl.when((to >= 2 * part) & (to < 2 * part + 2))
            def _(piece=piece, target=out_ref.at[inner, lo:hi], index=index):
                pltpu.make_async_copy(piece, target, sem.at[1, index]).start()

        copies.append(pltpu.make_async_copy(piece, out0_ref.at[0, lo:hi], sem.at[1, index]))
    for copy in copies:
        copy.wait()


def assemble(place, *pieces):
    return pl.pallas_call(
        assemble_kernel,
        out_shape=[
            jax.ShapeDtypeStruct((count, 8, 2, 96, 128), BF) for count in (4, 2, 2)
        ],
        in_specs=[SMEM] + [ANY] * 5,
        out_specs=[VMEM] * 3,
        scratch_shapes=[pltpu.SemaphoreType.DMA((2, 5))],
        compiler_params=pltpu.CompilerParams(vmem_limit_bytes=8 * MIB),
        name="assemble",
    )(place, *pieces)


def normed(hidden, gain):
    centre = jnp.mean(hidden, axis=-1, keepdims=True)
    centred = hidden - centre
    variance = jnp.mean(centred * centred, axis=-1, keepdims=True)
    return centred * lax.rsqrt(variance + EPS) * gain


def dot(a, b):
    return jnp.dot(a, b, preferred_element_type=F32)


def dot_nt(a, b):
    return lax.dot_general(a, b, (((1,), (1,)), ((), ())), preferred_element_type=F32)


def window_mask(split, edge):
    def code(axis):
        token = lax.broadcasted_iota(jnp.int32, (144, 144), axis)
        row = (token * 2731) >> 16
        col = token - 24 * row
        return jnp.where(col >= 12, 1, 0) + jnp.where(row >= split, 2, 0) * edge

    return code(0) == code(1)


def attend_pair(queries, keys, values, mask):
    low = lax.broadcasted_iota(jnp.int32, (144, 128), 1) < 64
    zero = jnp.zeros_like(queries)
    both = jnp.concatenate([jnp.where(low, queries, zero), jnp.where(low, zero, queries)], axis=0)
    scores = jnp.where(mask, dot_nt(both, keys), -1e9)
    weights = jnp.exp(scores - jnp.max(scores, axis=-1, keepdims=True))
    total = jnp.sum(weights, axis=-1, keepdims=True)
    mixed = dot(weights.astype(BF), values) * (1.0 / total)
    return jnp.where(low, mixed[:144], mixed[144:])


def level_one_kernel(
    place_ref,
    above_ref,
    x_ref,
    below_ref,
    col_ref,
    cls_ref,
    table_ref,
    gain1_ref,
    gain2_ref,
    inward_hbm,
    outward_hbm,
    up_hbm,
    down_hbm,
    out_ref,
    top_ref,
    bottom_ref,
    first_ref,
    last_ref,
    inward,
    outward,
    up,
    down,
    rim,
    residual,
    attended,
    ext,
    cols,
    sem,
):
    copies = [
        pltpu.make_async_copy(source, target, sem.at[index])
        for index, (source, target) in enumerate(
            ((inward_hbm, inward), (outward_hbm, outward), (up_hbm, up), (down_hbm, down))
        )
    ]
    for copy in copies:
        copy.start()
    lat, shift = place_ref[4], place_ref[5]
    split = jnp.where(shift > 0, 6 - shift, -shift)
    for row in range(3):
        ext[row] = above_ref[row * 48 : row * 48 + 48]
        ext[15 + row] = below_ref[row * 48 : row * 48 + 48]
    for row in range(12):
        ext[3 + row] = x_ref[row]
    for row in range(18):
        cols[row] = col_ref[row : row + 1].astype(F32)
    for band in range(2):
        for row in range(6):
            frame = band * 6 + row
            rim[row, 8:56] = ext[3 + shift + frame].astype(F32)
            rim[row, 7:8] = cols[3 + shift + frame]
            cls = cls_ref[:, frame : frame + 1]
            embedded = jnp.where(
                cls == 0.0, table_ref[0:1], jnp.where(cls == 1.0, table_ref[1:2], table_ref[2:3])
            )
            residual[row * 48 : (row + 1) * 48] = rim[row, 7:55] + embedded
        normal = normed(residual[...], gain1_ref[...]).astype(BF)
        if band == 1:
            edge = jnp.where((lat == 7) & (shift > 0), 1, 0)
        else:
            edge = jnp.where((lat == 0) & (shift < 0), 1, 0)
        mask = window_mask(split, edge)
        mask = jnp.concatenate([mask, mask], axis=0)
        if band == 0:
            copies[0].wait()
        for quarter in range(2):
            at = quarter * 256
            parts = [
                dot(normal, inward[:, part * 512 + at : part * 512 + at + 256]).reshape(6, 48, 256)
                for part in range(3)
            ]
            for pair in range(2):
                lanes = slice(pair * 128, pair * 128 + 128)
                for block in range(2):
                    span = slice(block * 24, block * 24 + 24)
                    queries, keys, values = (
                        part[:, span, lanes].reshape(144, 128).astype(BF) for part in parts
                    )
                    mixed = attend_pair(queries * BF(0.125), keys, values, mask)
                    attended[:, span, at + pair * 128 : at + pair * 128 + 128] = mixed.reshape(
                        6, 24, 128
                    )
        if band == 0:
            copies[1].wait()
        mid = residual[...] + dot(attended[...].reshape(288, 512).astype(BF), outward[...])
        residual[...] = mid
        normal = normed(mid, gain2_ref[...]).astype(BF)
        if band == 0:
            copies[2].wait()
            copies[3].wait()
        for chunk in range(4):
            part = slice(chunk * 512, chunk * 512 + 512)
            hidden = jax.nn.gelu(dot(normal, up[:, part])).astype(BF)
            residual[...] += dot(hidden, down[part])
        result = residual[...].astype(BF).reshape(6, 48, 512)
        out_ref[band * 6 : band * 6 + 6] = result
        if band == 0:
            top_ref[...] = result[:3]
        else:
            bottom_ref[...] = result[3:]
        for row in range(6):
            first_ref[band * 6 + row] = residual[row * 48 : row * 48 + 1].astype(BF)
            last_ref[band * 6 + row] = residual[row * 48 + 47 : row * 48 + 48].astype(BF)


def level_one(place, above, x, below, col, cls, table, gain1, gain2, inward, outward, up, down):
    return pl.pallas_call(
        level_one_kernel,
        out_shape=[
            jax.ShapeDtypeStruct((12, 48, 512), BF),
            jax.ShapeDtypeStruct((3, 48, 512), BF),
            jax.ShapeDtypeStruct((3, 48, 512), BF),
            jax.ShapeDtypeStruct((12, 1, 512), BF),
            jax.ShapeDtypeStruct((12, 1, 512), BF),
        ],
        in_specs=[SMEM] + [VMEM] * 8 + [HBM] * 4,
        out_specs=[VMEM] * 5,
        scratch_shapes=[
            pltpu.VMEM((512, 1536), BF),
            pltpu.VMEM((512, 512), BF),
            pltpu.VMEM((512, 2048), BF),
            pltpu.VMEM((2048, 512), BF),
            pltpu.VMEM((6, 56, 512), F32),
            pltpu.VMEM((288, 512), F32),
            pltpu.VMEM((6, 48, 512), F32),
            pltpu.VMEM((18, 48, 512), BF),
            pltpu.VMEM((18, 1, 512), F32),
            pltpu.SemaphoreType.DMA((4,)),
        ],
        compiler_params=pltpu.CompilerParams(vmem_limit_bytes=50 * MIB),
        cost_estimate=pl.CostEstimate(
            flops=13_000_000_000, bytes_accessed=8_000_000, transcendentals=3_000_000
        ),
        name="level_one",
    )(place, above, x, below, col, cls, table, gain1, gain2, inward, outward, up, down)


def level_two_kernel(place_ref, above_ref, f_ref, below_ref, col_ref, gain1_ref, gain2_ref, *refs):
    mine, others = refs[0:7], refs[7:14]
    (out_ref, top_ref, bottom_ref, first_ref) = refs[14:18]
    merge, outward, inward, rim, merged, total, packed, attended, ext, sem = refs[18:]
    x, y, core = place_ref[0], place_ref[1], place_ref[3]
    lat, shift = place_ref[4], place_ref[5]

    def jobs(first, second):
        lists = {"merge": [], "inward": [], "outward": []}
        count = 0
        for piece, step, lo, hi in zip(
            range(7), (0, 3, 3, 1, 1, 2, 2), (0, 0, 2, 0, 2, 0, 2), (4, 2, 4, 2, 4, 2, 4)
        ):
            to_x, to_y = lax.rem(x + step, 4), lax.rem(y + step, 4)
            for section in range(3):
                rows = slice(section * 32, section * 32 + 32)
                target = (merge.at[0], merge.at[1], outward)[section]
                lists["outward" if section == 2 else "merge"].append(
                    pltpu.make_async_copy(
                        first[piece].at[:, :, :, rows],
                        target.at[lo:hi, :, to_x],
                        sem.at[count],
                    )
                )
                count += 1
            for column in range(lo, hi):
                lists["inward"].append(
                    pltpu.make_async_copy(
                        second[piece].at[column - lo], inward.at[to_y, :, column], sem.at[count]
                    )
                )
                count += 1
        return lists

    @pl.when(core == 0)
    def _():
        for copies in jobs(mine, others).values():
            for copy in copies:
                copy.start()

    @pl.when(core == 1)
    def _():
        for copies in jobs(others, mine).values():
            for copy in copies:
                copy.start()

    waits = jobs(mine, others)
    for row in range(3):
        ext[row] = above_ref[row]
        ext[15 + row] = below_ref[row]
    for row in range(12):
        ext[3 + row] = f_ref[row]
    for row in range(12):
        values = ext[3 + shift + row].astype(F32)
        left = col_ref[3 + shift + row].astype(F32)
        for quarter in range(4):
            lanes = slice(quarter * 128, quarter * 128 + 128)
            rim[quarter, row, 8:56] = values[:, lanes]
            rim[quarter, row, 7:8] = left[:, lanes]
    for row in range(6):
        for part in range(4):
            for quarter in range(4):
                at = part * 512 + quarter * 128
                merged[row * 24 : row * 24 + 24, at : at + 128] = rim[
                    quarter, 2 * row + part % 2, pl.ds(7 + part // 2, 24, stride=2), :
                ]
    normal = normed(merged[...], gain1_ref[...]).astype(BF)
    for copy in waits["merge"]:
        copy.wait()
    reduced = None
    for z_hi in range(2):
        for y_at in range(4):
            block = jnp.concatenate(
                [
                    merge[half, y_at, z_hi * 4 : z_hi * 4 + 4].reshape(1024, 128)
                    for half in range(2)
                ],
                axis=1,
            )
            at = (z_hi * 4 + y_at) * 256
            part = dot_nt(normal[:, at : at + 256], block)
            reduced = part if reduced is None else reduced + part
    reduced = reduced.astype(BF).astype(F32)
    total[...] = reduced
    normal = normed(reduced, gain2_ref[...]).astype(BF)
    for copy in waits["inward"]:
        copy.wait()
    for third in range(3):
        for z_hi in range(2):
            for y_at in range(0, 4, 2):
                block = jnp.concatenate(
                    [
                        inward[y_at + half, z_hi * 4 : z_hi * 4 + 4].reshape(3072, 128)[
                            third * 1024 : third * 1024 + 1024
                        ]
                        for half in range(2)
                    ],
                    axis=1,
                )
                at = (z_hi * 4 + y_at) * 128
                part = dot_nt(normal[:, at : at + 256], block)
                if z_hi + y_at == 0:
                    sums = part
                else:
                    sums = sums + part
        if third == 0:
            sums = sums * 0.125
        packed[:, third * 1024 : third * 1024 + 1024] = sums.astype(BF)

    split = jnp.where(shift > 0, 6 - shift, -shift)
    edge = jnp.where(((lat == 7) & (shift > 0)) | ((lat == 0) & (shift < 0)), 1, 0)
    mask = window_mask(split, edge)
    mask = jnp.concatenate([mask, mask], axis=0)
    for pair in range(8):
        at = pair * 128
        mixed = attend_pair(
            packed[:, at : at + 128],
            packed[:, 1024 + at : 1024 + at + 128],
            packed[:, 2048 + at : 2048 + at + 128],
            mask,
        )
        attended[:, at : at + 128] = mixed.astype(BF)
    for copy in waits["outward"]:
        copy.wait()
    sums = total[...]
    for z_hi in range(2):
        for y_at in range(0, 4, 2):
            block = jnp.concatenate(
                [
                    outward[y_at + half, z_hi * 4 : z_hi * 4 + 4].reshape(1024, 128)
                    for half in range(2)
                ],
                axis=1,
            )
            at = (z_hi * 4 + y_at) * 128
            sums = sums + dot_nt(attended[:, at : at + 256], block)
    total[...] = sums
    for row in range(6):
        result = total[row * 24 : row * 24 + 24].astype(BF)
        out_ref[row] = result
        if row < 3:
            top_ref[row] = result
        else:
            bottom_ref[row - 3] = result
        first_ref[row] = total[row * 24 : row * 24 + 1].astype(BF)


def level_two(place, above, f, below, col, gain1, gain2, mine, others):
    return pl.pallas_call(
        level_two_kernel,
        out_shape=[
            jax.ShapeDtypeStruct((6, 24, 1024), BF),
            jax.ShapeDtypeStruct((3, 24, 1024), BF),
            jax.ShapeDtypeStruct((3, 24, 1024), BF),
            jax.ShapeDtypeStruct((6, 1, 1024), BF),
        ],
        in_specs=[SMEM] + [VMEM] * 6 + [ANY] * 14,
        out_specs=[VMEM] * 4,
        scratch_shapes=[
            pltpu.VMEM((2, 4, 8, 4, 2, 32, 128), BF),
            pltpu.VMEM((4, 8, 4, 2, 32, 128), BF),
            pltpu.VMEM((4, 8, 4, 2, 96, 128), BF),
            pltpu.VMEM((4, 12, 56, 128), F32),
            pltpu.VMEM((144, 2048), F32),
            pltpu.VMEM((144, 1024), F32),
            pltpu.VMEM((144, 3072), BF),
            pltpu.VMEM((144, 1024), BF),
            pltpu.VMEM((18, 48, 512), BF),
            pltpu.SemaphoreType.DMA((37,)),
        ],
        compiler_params=pltpu.CompilerParams(vmem_limit_bytes=32 * MIB),
        cost_estimate=pl.CostEstimate(
            flops=11_000_000_000, bytes_accessed=14_000_000, transcendentals=1_000_000
        ),
        name="level_two",
    )(place, above, f, below, col, gain1, gain2, *mine, *others)


def edges(top, bottom):
    return to_cell(bottom, 1, 0), to_cell(top, -1, 0)


def column(above, col, below, index, direction):
    part = jnp.concatenate([above[:, index], col, below[:, index]], axis=0)
    return to_cell(part, 0, direction)


def moved_rows(col, start):
    return lax.dynamic_slice_in_dim(col, start, 12, 0)


def moved_back(shift, above, grid, below, col):
    whole = jnp.concatenate([above, grid, below], axis=0)
    count = grid.shape[0]
    whole = lax.dynamic_slice_in_dim(whole, 3 - shift, count, 0)
    col = lax.dynamic_slice_in_dim(col, 3 - shift, count, 0)
    return jnp.concatenate([whole[:, 1:], col], axis=1)


def line(*values):
    values = jnp.concatenate([value.reshape(-1) for value in values])
    return jnp.pad(values, (0, 512 - values.shape[0])).reshape(1, 512)


def shards(
    latent,
    surface,
    table,
    shifts,
    gain_one,
    inward_one,
    outward_one,
    gain_ffn,
    ffn_up,
    ffn_down,
    gain_merge,
    merge_proj,
    gain_two,
    inward_two,
    outward_two,
):
    lat, lon = lax.axis_index("lat"), lax.axis_index("lon")
    shift = jnp.where(shifts[0] <= 3, shifts[0], shifts[0] - 6)
    x, y, z, core = (lon // 2) % 4, lat % 4, (lat // 4) * 4 + lon // 8, lon % 2
    place = jnp.stack([x, y, z, core, lat, shift, jnp.where(core == 0, y, x)]).astype(jnp.int32)

    classes = surface.astype(BF)

    def message(part):
        return jnp.concatenate([latent[part].reshape(-1, 512), line(classes[part])])

    above = to_cell(message(slice(9, 12)), 1, 0)
    below = to_cell(message(slice(0, 3)), -1, 0)

    keep, send = pack(place, merge_proj, inward_two, outward_two)
    shard = jnp.stack([keep, to_core(send)])
    near = jnp.stack([along_z(shard, 1), shard, along_z(shard, -1)])
    far_low, far_high = along_z(near, 3), along_z(near[:2], -3)

    cls = jnp.concatenate(
        [above[144, :144].reshape(3, 48), classes, below[144, :144].reshape(3, 48)]
    )
    left = to_cell(
        jnp.concatenate([above[47:144:48], latent[:, -1], below[47:144:48], line(cls[:, -1])]), 0, 1
    )
    cls = jnp.concatenate([left[18, :18, None], cls[:, :-1]], axis=1)
    cls = jnp.pad(moved_rows(cls, 3 + shift).astype(F32).T, ((0, 0), (0, 4)))
    far_low, far_high, left = lax.optimization_barrier((far_low, far_high, left))
    block = assemble_z(place, far_low, near, far_high)
    from_left, from_right = along(block, False, 1), along(block, False, -1)
    block, part0, part1 = assemble(
        place, block, from_left, from_right,
        along(from_left[:4], False, 1), along(from_right[4:], False, -1),
    )
    left0, right1 = along(part0, True, 1), along(part1, True, -1)
    left1, right0 = along(part1, True, 1), along(part0, True, -1)
    frame, top, bottom, first, last = level_one(
        place, above, latent, below, after(left, block), cls, table,
        gain_one.reshape(1, -1), gain_ffn.reshape(1, -1),
        inward_one, outward_one, ffn_up, ffn_down,
    )
    own, left0, right1, top, bottom = lax.optimization_barrier(
        (to_core(block), left0, right1, top, bottom)
    )
    above, below = edges(top, bottom)
    mine = [
        block, left0, left1, right0, right1, along(left0, True, 1), along(right1, True, -1)
    ]
    above, below, left1, right0 = lax.optimization_barrier((above, below, left1, right0))
    left0, right1 = after((left0, right1), above)
    others = [own] + [to_core(piece) for piece in (left0, left1, right0, right1)]
    left = column(above[:, :, None], last, below[:, :, None], 47, 1)
    others += [to_core(piece) for piece in after(tuple(mine[5:]), left)]
    right = column(after(above, *others)[:, :, None], first, below[:, :, None], 0, -1)
    out_one = moved_back(shift, above, frame, below, right)
    frame, top, bottom, first = level_two(
        place, above, frame, below, left,
        gain_merge.reshape(1, -1), gain_two.reshape(1, -1), mine, others,
    )
    above, below = edges(top, bottom)
    right = column(above[:, :, None], first, below[:, :, None], 0, -1)
    return out_one, moved_back(shift, above, frame, below, right)


def solution(mesh):
    placed = (
        P("lat", "lon", None),
        P("lat", "lon"),
        P(),
        P(),
        P(),
        P(),
        P(),
        P(),
        P(),
        P(),
        P(),
        P("lat", "lon"),
        P(),
        P("lat", "lon"),
        P("lat", "lon"),
    )
    return jax.shard_map(
        shards,
        mesh=mesh,
        in_specs=placed,
        out_specs=(P("lat", "lon", None), P("lat", "lon", None)),
        check_vma=False,
    )
```

```python
import jax
import jax.numpy as jnp
from jax import lax
from jax.experimental import pallas as pl
from jax.experimental.pallas import tpu as pltpu
from jax.sharding import PartitionSpec as P

EPS = 1e-05
BF = jnp.bfloat16
F32 = jnp.float32
AXES = ("lat", "lon")
VMEM = pl.BlockSpec(memory_space=pltpu.VMEM)
SMEM = pl.BlockSpec(memory_space=pltpu.SMEM)
ANY = pl.BlockSpec(memory_space=pl.ANY)
HBM = pl.BlockSpec(memory_space=pltpu.HBM)
MIB = 1024 * 1024

PLACES = [(x, y, z, c) for z in range(8) for y in range(4) for x in range(4) for c in range(2)]


def number(x, y, z, c):
    x, y, z, c = x % 4, y % 4, z % 8, c % 2
    return ((z // 4) * 4 + y) * 32 + ((z % 4) * 4 + x) * 2 + c


def move(array, steps):
    pairs = []
    for x, y, z, c in PLACES:
        dx, dy, dz, dc = steps[c]
        pairs.append((number(x, y, z, c), number(x + dx, y + dy, z + dz, c + dc)))
    return lax.ppermute(array, AXES, pairs)


def along_z(array, step):
    return move(array, ((0, 0, step, 0),) * 2)


def to_core(array):
    return move(array, ((0, 0, 0, 1),) * 2)


def along(array, last, step):
    by_x, by_y = (step, 0, 0, 0), (0, step, 0, 0)
    return move(array, (by_x, by_y) if last else (by_y, by_x))


def to_cell(array, dlat, dlon):
    pairs = [
        (i * 32 + j, ((i + dlat) % 8) * 32 + (j + dlon) % 32) for i in range(8) for j in range(32)
    ]
    return lax.ppermute(array, AXES, pairs)


def after(value, *others):
    return lax.optimization_barrier((value,) + others)[0]


def pack_kernel(place_ref, merge_ref, inward_ref, outward_ref, keep_ref, send_ref):
    def store(first, second):
        first[0:32] = merge_ref[:, :128]
        first[32:64] = merge_ref[:, 128:]
        first[64:96] = outward_ref[...]
        second[...] = inward_ref[...]

    @pl.when(place_ref[3] == 0)
    def _():
        store(keep_ref, send_ref)

    @pl.when(place_ref[3] == 1)
    def _():
        store(send_ref, keep_ref)


def pack(place, merge, inward, outward):
    return pl.pallas_call(
        pack_kernel,
        out_shape=[jax.ShapeDtypeStruct((96, 128), BF)] * 2,
        in_specs=[SMEM] + [VMEM] * 3,
        out_specs=[VMEM] * 2,
        compiler_params=pltpu.CompilerParams(vmem_limit_bytes=56 * MIB),
        name="pack",
    )(place, merge.T, inward.T, outward.T)


def assemble_z_kernel(place_ref, low_ref, near_ref, high_ref, out_ref, sem):
    z, core = place_ref[2], place_ref[3]
    copies = []
    for step in range(8):
        ref, first = ((low_ref, 0), (near_ref, 3), (high_ref, 6))[step // 3]
        to = lax.rem(z + 4 + step, 8)
        for other in range(2):
            target = out_ref.at[to, lax.rem(core + other, 2)]
            copies.append(
                pltpu.make_async_copy(ref.at[step - first, other], target, sem.at[len(copies)])
            )
    for copy in copies:
        copy.start()
    for copy in copies:
        copy.wait()


def assemble_z(place, low, near, high):
    return pl.pallas_call(
        assemble_z_kernel,
        out_shape=jax.ShapeDtypeStruct((8, 2, 96, 128), BF),
        in_specs=[SMEM] + [ANY] * 3,
        out_specs=VMEM,
        scratch_shapes=[pltpu.SemaphoreType.DMA((16,))],
        compiler_params=pltpu.CompilerParams(vmem_limit_bytes=6 * MIB),
        name="assemble_z",
    )(place, low, near, high)


def assemble_kernel(place_ref, own, left, right, half0, half1, out_ref, sem):
    at = place_ref[6]
    copies = [
        pltpu.make_async_copy(piece, out_ref.at[lax.rem(at + step, 4), lo:hi], sem.at[index])
        for index, (piece, step, lo, hi) in enumerate(
            ((own, 0, 0, 8), (left, 3, 0, 8), (right, 1, 0, 8), (half0, 2, 0, 4), (half1, 2, 4, 8))
        )
    ]
    for copy in copies:
        copy.start()
    for copy in copies:
        copy.wait()


def assemble(place, *pieces):
    return pl.pallas_call(
        assemble_kernel,
        out_shape=jax.ShapeDtypeStruct((4, 8, 2, 96, 128), BF),
        in_specs=[SMEM] + [ANY] * 5,
        out_specs=VMEM,
        scratch_shapes=[pltpu.SemaphoreType.DMA((5,))],
        compiler_params=pltpu.CompilerParams(vmem_limit_bytes=6 * MIB),
        name="assemble",
    )(place, *pieces)


def normed(hidden, gain):
    centre = jnp.mean(hidden, axis=-1, keepdims=True)
    centred = hidden - centre
    variance = jnp.mean(centred * centred, axis=-1, keepdims=True)
    return centred * lax.rsqrt(variance + EPS) * gain


def dot(a, b):
    return jnp.dot(a, b, preferred_element_type=F32)


def dot_nt(a, b):
    return lax.dot_general(a, b, (((1,), (1,)), ((), ())), preferred_element_type=F32)


def window_mask(split, edge):
    def code(axis):
        token = lax.broadcasted_iota(jnp.int32, (144, 144), axis)
        row = (token * 2731) >> 16
        col = token - 24 * row
        return jnp.where(col >= 12, 1, 0) + jnp.where(row >= split, 2, 0) * edge

    return code(0) == code(1)


def attend_pair(queries, keys, values, mask):
    low = lax.broadcasted_iota(jnp.int32, (144, 128), 1) < 64
    zero = jnp.zeros_like(queries)
    both = jnp.concatenate([jnp.where(low, queries, zero), jnp.where(low, zero, queries)], axis=0)
    scores = jnp.where(mask, dot_nt(both, keys), -1e9)
    weights = jnp.exp(scores - jnp.max(scores, axis=-1, keepdims=True))
    total = jnp.sum(weights, axis=-1, keepdims=True)
    mixed = dot(weights.astype(BF), values) * (1.0 / total)
    return jnp.where(low, mixed[:144], mixed[144:])


def level_one_kernel(
    place_ref,
    above_ref,
    x_ref,
    below_ref,
    col_ref,
    cls_ref,
    table_ref,
    gain1_ref,
    gain2_ref,
    inward_hbm,
    outward_hbm,
    up_hbm,
    down_hbm,
    out_ref,
    top_ref,
    bottom_ref,
    first_ref,
    last_ref,
    inward,
    outward,
    up,
    down,
    rim,
    residual,
    attended,
    ext,
    cols,
    sem,
):
    copies = [
        pltpu.make_async_copy(source, target, sem.at[index])
        for index, (source, target) in enumerate(
            ((inward_hbm, inward), (outward_hbm, outward), (up_hbm, up), (down_hbm, down))
        )
    ]
    for copy in copies:
        copy.start()
    lat, shift = place_ref[4], place_ref[5]
    split = jnp.where(shift > 0, 6 - shift, -shift)
    for row in range(3):
        ext[row] = above_ref[row * 48 : row * 48 + 48]
        ext[15 + row] = below_ref[row * 48 : row * 48 + 48]
    for row in range(12):
        ext[3 + row] = x_ref[row]
    for row in range(18):
        cols[row] = col_ref[row : row + 1].astype(F32)
    for band in range(2):
        for row in range(6):
            frame = band * 6 + row
            rim[row, 8:56] = ext[3 + shift + frame].astype(F32)
            rim[row, 7:8] = cols[3 + shift + frame]
            cls = cls_ref[:, frame : frame + 1]
            embedded = jnp.where(
                cls == 0.0, table_ref[0:1], jnp.where(cls == 1.0, table_ref[1:2], table_ref[2:3])
            )
            residual[row * 48 : (row + 1) * 48] = rim[row, 7:55] + embedded
        normal = normed(residual[...], gain1_ref[...]).astype(BF)
        if band == 1:
            edge = jnp.where((lat == 7) & (shift > 0), 1, 0)
        else:
            edge = jnp.where((lat == 0) & (shift < 0), 1, 0)
        mask = window_mask(split, edge)
        mask = jnp.concatenate([mask, mask], axis=0)
        if band == 0:
            copies[0].wait()
        for quarter in range(2):
            at = quarter * 256
            parts = [
                dot(normal, inward[:, part * 512 + at : part * 512 + at + 256]).reshape(6, 48, 256)
                for part in range(3)
            ]
            for pair in range(2):
                lanes = slice(pair * 128, pair * 128 + 128)
                for block in range(2):
                    span = slice(block * 24, block * 24 + 24)
                    queries, keys, values = (
                        part[:, span, lanes].reshape(144, 128).astype(BF) for part in parts
                    )
                    mixed = attend_pair(queries * BF(0.125), keys, values, mask)
                    attended[:, span, at + pair * 128 : at + pair * 128 + 128] = mixed.reshape(
                        6, 24, 128
                    )
        if band == 0:
            copies[1].wait()
        mid = residual[...] + dot(attended[...].reshape(288, 512).astype(BF), outward[...])
        residual[...] = mid
        normal = normed(mid, gain2_ref[...]).astype(BF)
        if band == 0:
            copies[2].wait()
            copies[3].wait()
        for chunk in range(4):
            part = slice(chunk * 512, chunk * 512 + 512)
            hidden = jax.nn.gelu(dot(normal, up[:, part])).astype(BF)
            residual[...] += dot(hidden, down[part])
        result = residual[...].astype(BF).reshape(6, 48, 512)
        out_ref[band * 6 : band * 6 + 6] = result
        if band == 0:
            top_ref[...] = result[:3]
        else:
            bottom_ref[...] = result[3:]
        for row in range(6):
            first_ref[band * 6 + row] = residual[row * 48 : row * 48 + 1].astype(BF)
            last_ref[band * 6 + row] = residual[row * 48 + 47 : row * 48 + 48].astype(BF)


def level_one(place, above, x, below, col, cls, table, gain1, gain2, inward, outward, up, down):
    return pl.pallas_call(
        level_one_kernel,
        out_shape=[
            jax.ShapeDtypeStruct((12, 48, 512), BF),
            jax.ShapeDtypeStruct((3, 48, 512), BF),
            jax.ShapeDtypeStruct((3, 48, 512), BF),
            jax.ShapeDtypeStruct((12, 1, 512), BF),
            jax.ShapeDtypeStruct((12, 1, 512), BF),
        ],
        in_specs=[SMEM] + [VMEM] * 8 + [HBM] * 4,
        out_specs=[VMEM] * 5,
        scratch_shapes=[
            pltpu.VMEM((512, 1536), BF),
            pltpu.VMEM((512, 512), BF),
            pltpu.VMEM((512, 2048), BF),
            pltpu.VMEM((2048, 512), BF),
            pltpu.VMEM((6, 56, 512), F32),
            pltpu.VMEM((288, 512), F32),
            pltpu.VMEM((6, 48, 512), F32),
            pltpu.VMEM((18, 48, 512), BF),
            pltpu.VMEM((18, 1, 512), F32),
            pltpu.SemaphoreType.DMA((4,)),
        ],
        compiler_params=pltpu.CompilerParams(vmem_limit_bytes=50 * MIB),
        cost_estimate=pl.CostEstimate(
            flops=13_000_000_000, bytes_accessed=8_000_000, transcendentals=3_000_000
        ),
        name="level_one",
    )(place, above, x, below, col, cls, table, gain1, gain2, inward, outward, up, down)


def level_two_kernel(place_ref, above_ref, f_ref, below_ref, col_ref, gain1_ref, gain2_ref, *refs):
    mine, others = refs[0:5], refs[5:10]
    (out_ref, top_ref, bottom_ref, first_ref) = refs[10:14]
    merge, outward, inward, rim, merged, total, packed, attended, ext, sem = refs[14:]
    x, y, core = place_ref[0], place_ref[1], place_ref[3]
    lat, shift = place_ref[4], place_ref[5]

    def jobs(first, second):
        lists = {"merge": [], "inward": [], "outward": []}
        count = 0
        for piece, step, lo, hi in zip(
            range(5), (0, 3, 1, 2, 2), (0, 0, 0, 0, 2), (4, 4, 4, 2, 4)
        ):
            to_x, to_y = lax.rem(x + step, 4), lax.rem(y + step, 4)
            for section in range(3):
                rows = slice(section * 32, section * 32 + 32)
                target = (merge.at[0], merge.at[1], outward)[section]
                lists["outward" if section == 2 else "merge"].append(
                    pltpu.make_async_copy(
                        first[piece].at[:, :, :, rows],
                        target.at[lo:hi, :, to_x],
                        sem.at[count],
                    )
                )
                count += 1
            for column in range(lo, hi):
                lists["inward"].append(
                    pltpu.make_async_copy(
                        second[piece].at[column - lo], inward.at[to_y, :, column], sem.at[count]
                    )
                )
                count += 1
        return lists

    @pl.when(core == 0)
    def _():
        for copies in jobs(mine, others).values():
            for copy in copies:
                copy.start()

    @pl.when(core == 1)
    def _():
        for copies in jobs(others, mine).values():
            for copy in copies:
                copy.start()

    waits = jobs(mine, others)
    for row in range(3):
        ext[row] = above_ref[row]
        ext[15 + row] = below_ref[row]
    for row in range(12):
        ext[3 + row] = f_ref[row]
    for row in range(12):
        values = ext[3 + shift + row].astype(F32)
        left = col_ref[3 + shift + row].astype(F32)
        for quarter in range(4):
            lanes = slice(quarter * 128, quarter * 128 + 128)
            rim[quarter, row, 8:56] = values[:, lanes]
            rim[quarter, row, 7:8] = left[:, lanes]
    for row in range(6):
        for part in range(4):
            for quarter in range(4):
                at = part * 512 + quarter * 128
                merged[row * 24 : row * 24 + 24, at : at + 128] = rim[
                    quarter, 2 * row + part % 2, pl.ds(7 + part // 2, 24, stride=2), :
                ]
    normal = normed(merged[...], gain1_ref[...]).astype(BF)
    for copy in waits["merge"]:
        copy.wait()
    reduced = None
    for z_hi in range(2):
        for y_at in range(4):
            block = jnp.concatenate(
                [
                    merge[half, y_at, z_hi * 4 : z_hi * 4 + 4].reshape(1024, 128)
                    for half in range(2)
                ],
                axis=1,
            )
            at = (z_hi * 4 + y_at) * 256
            part = dot_nt(normal[:, at : at + 256], block)
            reduced = part if reduced is None else reduced + part
    reduced = reduced.astype(BF).astype(F32)
    total[...] = reduced
    normal = normed(reduced, gain2_ref[...]).astype(BF)
    for copy in waits["inward"]:
        copy.wait()
    for third in range(3):
        for z_hi in range(2):
            for y_at in range(0, 4, 2):
                block = jnp.concatenate(
                    [
                        inward[y_at + half, z_hi * 4 : z_hi * 4 + 4].reshape(3072, 128)[
                            third * 1024 : third * 1024 + 1024
                        ]
                        for half in range(2)
                    ],
                    axis=1,
                )
                at = (z_hi * 4 + y_at) * 128
                part = dot_nt(normal[:, at : at + 256], block)
                if z_hi + y_at == 0:
                    sums = part
                else:
                    sums = sums + part
        if third == 0:
            sums = sums * 0.125
        packed[:, third * 1024 : third * 1024 + 1024] = sums.astype(BF)

    split = jnp.where(shift > 0, 6 - shift, -shift)
    edge = jnp.where(((lat == 7) & (shift > 0)) | ((lat == 0) & (shift < 0)), 1, 0)
    mask = window_mask(split, edge)
    mask = jnp.concatenate([mask, mask], axis=0)
    for pair in range(8):
        at = pair * 128
        mixed = attend_pair(
            packed[:, at : at + 128],
            packed[:, 1024 + at : 1024 + at + 128],
            packed[:, 2048 + at : 2048 + at + 128],
            mask,
        )
        attended[:, at : at + 128] = mixed.astype(BF)
    for copy in waits["outward"]:
        copy.wait()
    sums = total[...]
    for z_hi in range(2):
        for y_at in range(0, 4, 2):
            block = jnp.concatenate(
                [
                    outward[y_at + half, z_hi * 4 : z_hi * 4 + 4].reshape(1024, 128)
                    for half in range(2)
                ],
                axis=1,
            )
            at = (z_hi * 4 + y_at) * 128
            sums = sums + dot_nt(attended[:, at : at + 256], block)
    total[...] = sums
    for row in range(6):
        result = total[row * 24 : row * 24 + 24].astype(BF)
        out_ref[row] = result
        if row < 3:
            top_ref[row] = result
        else:
            bottom_ref[row - 3] = result
        first_ref[row] = total[row * 24 : row * 24 + 1].astype(BF)


def level_two(place, above, f, below, col, gain1, gain2, mine, others):
    return pl.pallas_call(
        level_two_kernel,
        out_shape=[
            jax.ShapeDtypeStruct((6, 24, 1024), BF),
            jax.ShapeDtypeStruct((3, 24, 1024), BF),
            jax.ShapeDtypeStruct((3, 24, 1024), BF),
            jax.ShapeDtypeStruct((6, 1, 1024), BF),
        ],
        in_specs=[SMEM] + [VMEM] * 6 + [ANY] * 10,
        out_specs=[VMEM] * 4,
        scratch_shapes=[
            pltpu.VMEM((2, 4, 8, 4, 2, 32, 128), BF),
            pltpu.VMEM((4, 8, 4, 2, 32, 128), BF),
            pltpu.VMEM((4, 8, 4, 2, 96, 128), BF),
            pltpu.VMEM((4, 12, 56, 128), F32),
            pltpu.VMEM((144, 2048), F32),
            pltpu.VMEM((144, 1024), F32),
            pltpu.VMEM((144, 3072), BF),
            pltpu.VMEM((144, 1024), BF),
            pltpu.VMEM((18, 48, 512), BF),
            pltpu.SemaphoreType.DMA((31,)),
        ],
        compiler_params=pltpu.CompilerParams(vmem_limit_bytes=32 * MIB),
        cost_estimate=pl.CostEstimate(
            flops=11_000_000_000, bytes_accessed=14_000_000, transcendentals=1_000_000
        ),
        name="level_two",
    )(place, above, f, below, col, gain1, gain2, *mine, *others)


def edges(top, bottom):
    return to_cell(bottom, 1, 0), to_cell(top, -1, 0)


def column(above, col, below, index, direction):
    part = jnp.concatenate([above[:, index], col, below[:, index]], axis=0)
    return to_cell(part, 0, direction)


def moved_rows(col, start):
    return lax.dynamic_slice_in_dim(col, start, 12, 0)


def moved_back(shift, above, grid, below, col):
    whole = jnp.concatenate([above, grid, below], axis=0)
    count = grid.shape[0]
    whole = lax.dynamic_slice_in_dim(whole, 3 - shift, count, 0)
    col = lax.dynamic_slice_in_dim(col, 3 - shift, count, 0)
    return jnp.concatenate([whole[:, 1:], col], axis=1)


def line(*values):
    values = jnp.concatenate([value.reshape(-1) for value in values])
    return jnp.pad(values, (0, 512 - values.shape[0])).reshape(1, 512)


def shards(
    latent,
    surface,
    table,
    shifts,
    gain_one,
    inward_one,
    outward_one,
    gain_ffn,
    ffn_up,
    ffn_down,
    gain_merge,
    merge_proj,
    gain_two,
    inward_two,
    outward_two,
):
    lat, lon = lax.axis_index("lat"), lax.axis_index("lon")
    shift = jnp.where(shifts[0] <= 3, shifts[0], shifts[0] - 6)
    x, y, z, core = (lon // 2) % 4, lat % 4, (lat // 4) * 4 + lon // 8, lon % 2
    place = jnp.stack([x, y, z, core, lat, shift, jnp.where(core == 0, y, x)]).astype(jnp.int32)

    classes = surface.astype(BF)

    def message(part):
        return jnp.concatenate([latent[part].reshape(-1, 512), line(classes[part])])

    above = to_cell(message(slice(9, 12)), 1, 0)
    below = to_cell(message(slice(0, 3)), -1, 0)

    keep, send = pack(place, merge_proj, inward_two, outward_two)
    shard = jnp.stack([keep, to_core(send)])
    near = jnp.stack([along_z(shard, 1), shard, along_z(shard, -1)])
    far_low, far_high = along_z(near, 3), along_z(near[:2], -3)

    cls = jnp.concatenate(
        [above[144, :144].reshape(3, 48), classes, below[144, :144].reshape(3, 48)]
    )
    left = to_cell(
        jnp.concatenate([above[47:144:48], latent[:, -1], below[47:144:48], line(cls[:, -1])]), 0, 1
    )
    cls = jnp.concatenate([left[18, :18, None], cls[:, :-1]], axis=1)
    cls = jnp.pad(moved_rows(cls, 3 + shift).astype(F32).T, ((0, 0), (0, 4)))
    block = assemble_z(place, far_low, near, far_high)
    from_left, from_right = along(block, False, 1), along(block, False, -1)
    far0, far1, left = lax.optimization_barrier(
        (along(from_left[:4], False, 1), along(from_right[4:], False, -1), left)
    )
    block = assemble(place, block, from_left, from_right, far0, far1)
    from_left, from_right = along(block, True, 1), along(block, True, -1)
    frame, top, bottom, first, last = level_one(
        place, above, latent, below, after(left, block), cls, table,
        gain_one.reshape(1, -1), gain_ffn.reshape(1, -1),
        inward_one, outward_one, ffn_up, ffn_down,
    )
    above, below = edges(top, bottom)
    from_left, from_right = lax.optimization_barrier((from_left, from_right, top))[:2]
    half0, half1, above, below = lax.optimization_barrier(
        (from_left[:2], from_right[2:], above, below)
    )
    mine = [block, from_left, from_right, along(half0, True, 1), along(half1, True, -1)]
    left = column(above[:, :, None], last, below[:, :, None], 47, 1)
    others = [to_core(piece) for piece in after(tuple(mine[:3]), above)]
    others += [to_core(piece) for piece in after(tuple(mine[3:]), left)]
    right = column(after(above, *others)[:, :, None], first, below[:, :, None], 0, -1)
    out_one = moved_back(shift, above, frame, below, right)
    frame, top, bottom, first = level_two(
        place, above, frame, below, left,
        gain_merge.reshape(1, -1), gain_two.reshape(1, -1), mine, others,
    )
    above, below = edges(top, bottom)
    right = column(above[:, :, None], first, below[:, :, None], 0, -1)
    return out_one, moved_back(shift, above, frame, below, right)


def solution(mesh):
    placed = (
        P("lat", "lon", None),
        P("lat", "lon"),
        P(),
        P(),
        P(),
        P(),
        P(),
        P(),
        P(),
        P(),
        P(),
        P("lat", "lon"),
        P(),
        P("lat", "lon"),
        P("lat", "lon"),
    )
    return jax.shard_map(
        shards,
        mesh=mesh,
        in_specs=placed,
        out_specs=(P("lat", "lon", None), P("lat", "lon", None)),
        check_vma=False,
    )
```

```python
import jax
import jax.numpy as jnp
from jax import lax
from jax.experimental import pallas as pl
from jax.experimental.pallas import tpu as pltpu
from jax.sharding import PartitionSpec as P

EPS = 1e-05
BF = jnp.bfloat16
F32 = jnp.float32
AXES = ("lat", "lon")
VMEM = pl.BlockSpec(memory_space=pltpu.VMEM)
SMEM = pl.BlockSpec(memory_space=pltpu.SMEM)
ANY = pl.BlockSpec(memory_space=pl.ANY)
HBM = pl.BlockSpec(memory_space=pltpu.HBM)
MIB = 1024 * 1024

PLACES = [(x, y, z, c) for z in range(8) for y in range(4) for x in range(4) for c in range(2)]


def number(x, y, z, c):
    x, y, z, c = x % 4, y % 4, z % 8, c % 2
    return ((z // 4) * 4 + y) * 32 + ((z % 4) * 4 + x) * 2 + c


def move(array, steps):
    pairs = []
    for x, y, z, c in PLACES:
        dx, dy, dz, dc = steps[c]
        pairs.append((number(x, y, z, c), number(x + dx, y + dy, z + dz, c + dc)))
    return lax.ppermute(array, AXES, pairs)


def along_z(array, step):
    return move(array, ((0, 0, step, 0),) * 2)


def to_core(array):
    return move(array, ((0, 0, 0, 1),) * 2)


def along(array, last, step):
    by_x, by_y = (step, 0, 0, 0), (0, step, 0, 0)
    return move(array, (by_x, by_y) if last else (by_y, by_x))


def to_cell(array, dlat, dlon):
    pairs = [
        (i * 32 + j, ((i + dlat) % 8) * 32 + (j + dlon) % 32) for i in range(8) for j in range(32)
    ]
    return lax.ppermute(array, AXES, pairs)


def after(value, *others):
    return lax.optimization_barrier((value,) + others)[0]


def pack_kernel(place_ref, merge_ref, inward_ref, outward_ref, keep_ref, send_ref):
    def store(first, second):
        first[0:32] = merge_ref[:, :128]
        first[32:64] = merge_ref[:, 128:]
        first[64:96] = outward_ref[...]
        second[...] = inward_ref[...]

    @pl.when(place_ref[3] == 0)
    def _():
        store(keep_ref, send_ref)

    @pl.when(place_ref[3] == 1)
    def _():
        store(send_ref, keep_ref)


def pack(place, merge, inward, outward):
    return pl.pallas_call(
        pack_kernel,
        out_shape=[jax.ShapeDtypeStruct((96, 128), BF)] * 2,
        in_specs=[SMEM] + [VMEM] * 3,
        out_specs=[VMEM] * 2,
        compiler_params=pltpu.CompilerParams(vmem_limit_bytes=56 * MIB),
        name="pack",
    )(place, merge.T, inward.T, outward.T)


def assemble_z_kernel(place_ref, low_ref, near_ref, high_ref, out_ref, sem):
    z, core = place_ref[2], place_ref[3]
    copies = []
    for step in range(8):
        ref, first = ((low_ref, 0), (near_ref, 3), (high_ref, 6))[step // 3]
        to = lax.rem(z + 4 + step, 8)
        for other in range(2):
            target = out_ref.at[to, lax.rem(core + other, 2)]
            copies.append(
                pltpu.make_async_copy(ref.at[step - first, other], target, sem.at[len(copies)])
            )
    for copy in copies:
        copy.start()
    for copy in copies:
        copy.wait()


def assemble_z(place, low, near, high):
    return pl.pallas_call(
        assemble_z_kernel,
        out_shape=jax.ShapeDtypeStruct((8, 2, 96, 128), BF),
        in_specs=[SMEM] + [ANY] * 3,
        out_specs=VMEM,
        scratch_shapes=[pltpu.SemaphoreType.DMA((16,))],
        compiler_params=pltpu.CompilerParams(vmem_limit_bytes=6 * MIB),
        name="assemble_z",
    )(place, low, near, high)


def assemble_kernel(place_ref, own, left, right, half0, half1, out_ref, sem):
    at = place_ref[6]
    copies = [
        pltpu.make_async_copy(piece, out_ref.at[lax.rem(at + step, 4), lo:hi], sem.at[index])
        for index, (piece, step, lo, hi) in enumerate(
            ((own, 0, 0, 8), (left, 3, 0, 8), (right, 1, 0, 8), (half0, 2, 0, 4), (half1, 2, 4, 8))
        )
    ]
    for copy in copies:
        copy.start()
    for copy in copies:
        copy.wait()


def assemble(place, *pieces):
    return pl.pallas_call(
        assemble_kernel,
        out_shape=jax.ShapeDtypeStruct((4, 8, 2, 96, 128), BF),
        in_specs=[SMEM] + [ANY] * 5,
        out_specs=VMEM,
        scratch_shapes=[pltpu.SemaphoreType.DMA((5,))],
        compiler_params=pltpu.CompilerParams(vmem_limit_bytes=6 * MIB),
        name="assemble",
    )(place, *pieces)


def normed(hidden, gain):
    centre = jnp.mean(hidden, axis=-1, keepdims=True)
    centred = hidden - centre
    variance = jnp.mean(centred * centred, axis=-1, keepdims=True)
    return centred * lax.rsqrt(variance + EPS) * gain


def dot(a, b):
    return jnp.dot(a, b, preferred_element_type=F32)


def dot_nt(a, b):
    return lax.dot_general(a, b, (((1,), (1,)), ((), ())), preferred_element_type=F32)


def window_mask(split, edge):
    def code(axis):
        token = lax.broadcasted_iota(jnp.int32, (144, 144), axis)
        row = (token * 2731) >> 16
        col = token - 24 * row
        return jnp.where(col >= 12, 1, 0) + jnp.where(row >= split, 2, 0) * edge

    return code(0) == code(1)


def attend_pair(queries, keys, values, mask):
    low = lax.broadcasted_iota(jnp.int32, (144, 128), 1) < 64
    zero = jnp.zeros_like(queries)
    both = jnp.concatenate([jnp.where(low, queries, zero), jnp.where(low, zero, queries)], axis=0)
    scores = jnp.where(mask, dot_nt(both, keys), -1e9)
    weights = jnp.exp(scores - jnp.max(scores, axis=-1, keepdims=True))
    total = jnp.sum(weights, axis=-1, keepdims=True)
    mixed = dot(weights.astype(BF), values) * (1.0 / total)
    return jnp.where(low, mixed[:144], mixed[144:])


def level_one_kernel(
    place_ref,
    above_ref,
    x_ref,
    below_ref,
    col_ref,
    cls_ref,
    table_ref,
    gain1_ref,
    gain2_ref,
    inward_hbm,
    outward_hbm,
    up_hbm,
    down_hbm,
    out_ref,
    top_ref,
    bottom_ref,
    first_ref,
    last_ref,
    inward,
    outward,
    up,
    down,
    rim,
    residual,
    attended,
    ext,
    cols,
    sem,
):
    copies = [
        pltpu.make_async_copy(source, target, sem.at[index])
        for index, (source, target) in enumerate(
            ((inward_hbm, inward), (outward_hbm, outward), (up_hbm, up), (down_hbm, down))
        )
    ]
    for copy in copies:
        copy.start()
    lat, shift = place_ref[4], place_ref[5]
    split = jnp.where(shift > 0, 6 - shift, -shift)
    for row in range(3):
        ext[row] = above_ref[row * 48 : row * 48 + 48]
        ext[15 + row] = below_ref[row * 48 : row * 48 + 48]
    for row in range(12):
        ext[3 + row] = x_ref[row]
    for row in range(18):
        cols[row] = col_ref[row : row + 1].astype(F32)
    for band in range(2):
        for row in range(6):
            frame = band * 6 + row
            rim[row, 8:56] = ext[3 + shift + frame].astype(F32)
            rim[row, 7:8] = cols[3 + shift + frame]
            cls = cls_ref[:, frame : frame + 1]
            embedded = jnp.where(
                cls == 0.0, table_ref[0:1], jnp.where(cls == 1.0, table_ref[1:2], table_ref[2:3])
            )
            residual[row * 48 : (row + 1) * 48] = rim[row, 7:55] + embedded
        normal = normed(residual[...], gain1_ref[...]).astype(BF)
        if band == 1:
            edge = jnp.where((lat == 7) & (shift > 0), 1, 0)
        else:
            edge = jnp.where((lat == 0) & (shift < 0), 1, 0)
        mask = window_mask(split, edge)
        mask = jnp.concatenate([mask, mask], axis=0)
        if band == 0:
            copies[0].wait()
        for quarter in range(2):
            at = quarter * 256
            parts = [
                dot(normal, inward[:, part * 512 + at : part * 512 + at + 256]).reshape(6, 48, 256)
                for part in range(3)
            ]
            for pair in range(2):
                lanes = slice(pair * 128, pair * 128 + 128)
                for block in range(2):
                    span = slice(block * 24, block * 24 + 24)
                    queries, keys, values = (
                        part[:, span, lanes].reshape(144, 128).astype(BF) for part in parts
                    )
                    mixed = attend_pair(queries * BF(0.125), keys, values, mask)
                    attended[:, span, at + pair * 128 : at + pair * 128 + 128] = mixed.reshape(
                        6, 24, 128
                    )
        if band == 0:
            copies[1].wait()
        mid = residual[...] + dot(attended[...].reshape(288, 512).astype(BF), outward[...])
        residual[...] = mid
        normal = normed(mid, gain2_ref[...]).astype(BF)
        if band == 0:
            copies[2].wait()
            copies[3].wait()
        for chunk in range(4):
            part = slice(chunk * 512, chunk * 512 + 512)
            hidden = jax.nn.gelu(dot(normal, up[:, part])).astype(BF)
            residual[...] += dot(hidden, down[part])
        result = residual[...].astype(BF).reshape(6, 48, 512)
        out_ref[band * 6 : band * 6 + 6] = result
        if band == 0:
            top_ref[...] = result[:3]
        else:
            bottom_ref[...] = result[3:]
        for row in range(6):
            first_ref[band * 6 + row] = residual[row * 48 : row * 48 + 1].astype(BF)
            last_ref[band * 6 + row] = residual[row * 48 + 47 : row * 48 + 48].astype(BF)


def level_one(place, above, x, below, col, cls, table, gain1, gain2, inward, outward, up, down):
    return pl.pallas_call(
        level_one_kernel,
        out_shape=[
            jax.ShapeDtypeStruct((12, 48, 512), BF),
            jax.ShapeDtypeStruct((3, 48, 512), BF),
            jax.ShapeDtypeStruct((3, 48, 512), BF),
            jax.ShapeDtypeStruct((12, 1, 512), BF),
            jax.ShapeDtypeStruct((12, 1, 512), BF),
        ],
        in_specs=[SMEM] + [VMEM] * 8 + [HBM] * 4,
        out_specs=[VMEM] * 5,
        scratch_shapes=[
            pltpu.VMEM((512, 1536), BF),
            pltpu.VMEM((512, 512), BF),
            pltpu.VMEM((512, 2048), BF),
            pltpu.VMEM((2048, 512), BF),
            pltpu.VMEM((6, 56, 512), F32),
            pltpu.VMEM((288, 512), F32),
            pltpu.VMEM((6, 48, 512), F32),
            pltpu.VMEM((18, 48, 512), BF),
            pltpu.VMEM((18, 1, 512), F32),
            pltpu.SemaphoreType.DMA((4,)),
        ],
        compiler_params=pltpu.CompilerParams(vmem_limit_bytes=50 * MIB),
        cost_estimate=pl.CostEstimate(
            flops=13_000_000_000, bytes_accessed=8_000_000, transcendentals=3_000_000
        ),
        name="level_one",
    )(place, above, x, below, col, cls, table, gain1, gain2, inward, outward, up, down)


def level_two_kernel(place_ref, above_ref, f_ref, below_ref, col_ref, gain1_ref, gain2_ref, *refs):
    mine, others = refs[0:5], refs[5:10]
    (out_ref, top_ref, bottom_ref, first_ref) = refs[10:14]
    merge, outward, inward, rim, merged, total, packed, attended, ext, sem = refs[14:]
    x, y, core = place_ref[0], place_ref[1], place_ref[3]
    lat, shift = place_ref[4], place_ref[5]

    def jobs(first, second):
        lists = {"merge": [], "inward": [], "outward": []}
        count = 0
        for piece, step, lo, hi in zip(
            range(5), (0, 3, 1, 2, 2), (0, 0, 0, 0, 2), (4, 4, 4, 2, 4)
        ):
            to_x, to_y = lax.rem(x + step, 4), lax.rem(y + step, 4)
            for section in range(3):
                rows = slice(section * 32, section * 32 + 32)
                target = (merge.at[0], merge.at[1], outward)[section]
                lists["outward" if section == 2 else "merge"].append(
                    pltpu.make_async_copy(
                        first[piece].at[:, :, :, rows],
                        target.at[lo:hi, :, to_x],
                        sem.at[count],
                    )
                )
                count += 1
            for column in range(lo, hi):
                lists["inward"].append(
                    pltpu.make_async_copy(
                        second[piece].at[column - lo], inward.at[to_y, :, column], sem.at[count]
                    )
                )
                count += 1
        return lists

    @pl.when(core == 0)
    def _():
        for copies in jobs(mine, others).values():
            for copy in copies:
                copy.start()

    @pl.when(core == 1)
    def _():
        for copies in jobs(others, mine).values():
            for copy in copies:
                copy.start()

    waits = jobs(mine, others)
    for row in range(3):
        ext[row] = above_ref[row]
        ext[15 + row] = below_ref[row]
    for row in range(12):
        ext[3 + row] = f_ref[row]
    for row in range(12):
        values = ext[3 + shift + row].astype(F32)
        left = col_ref[3 + shift + row].astype(F32)
        for quarter in range(4):
            lanes = slice(quarter * 128, quarter * 128 + 128)
            rim[quarter, row, 8:56] = values[:, lanes]
            rim[quarter, row, 7:8] = left[:, lanes]
    for row in range(6):
        for part in range(4):
            for quarter in range(4):
                at = part * 512 + quarter * 128
                merged[row * 24 : row * 24 + 24, at : at + 128] = rim[
                    quarter, 2 * row + part % 2, pl.ds(7 + part // 2, 24, stride=2), :
                ]
    normal = normed(merged[...], gain1_ref[...]).astype(BF)
    for copy in waits["merge"]:
        copy.wait()
    reduced = None
    for z_hi in range(2):
        for y_at in range(4):
            block = jnp.concatenate(
                [
                    merge[half, y_at, z_hi * 4 : z_hi * 4 + 4].reshape(1024, 128)
                    for half in range(2)
                ],
                axis=1,
            )
            at = (z_hi * 4 + y_at) * 256
            part = dot_nt(normal[:, at : at + 256], block)
            reduced = part if reduced is None else reduced + part
    reduced = reduced.astype(BF).astype(F32)
    total[...] = reduced
    normal = normed(reduced, gain2_ref[...]).astype(BF)
    for copy in waits["inward"]:
        copy.wait()
    for third in range(3):
        for z_hi in range(2):
            for y_at in range(0, 4, 2):
                block = jnp.concatenate(
                    [
                        inward[y_at + half, z_hi * 4 : z_hi * 4 + 4].reshape(3072, 128)[
                            third * 1024 : third * 1024 + 1024
                        ]
                        for half in range(2)
                    ],
                    axis=1,
                )
                at = (z_hi * 4 + y_at) * 128
                part = dot_nt(normal[:, at : at + 256], block)
                if z_hi + y_at == 0:
                    sums = part
                else:
                    sums = sums + part
        if third == 0:
            sums = sums * 0.125
        packed[:, third * 1024 : third * 1024 + 1024] = sums.astype(BF)

    split = jnp.where(shift > 0, 6 - shift, -shift)
    edge = jnp.where(((lat == 7) & (shift > 0)) | ((lat == 0) & (shift < 0)), 1, 0)
    mask = window_mask(split, edge)
    mask = jnp.concatenate([mask, mask], axis=0)
    for pair in range(8):
        at = pair * 128
        mixed = attend_pair(
            packed[:, at : at + 128],
            packed[:, 1024 + at : 1024 + at + 128],
            packed[:, 2048 + at : 2048 + at + 128],
            mask,
        )
        attended[:, at : at + 128] = mixed.astype(BF)
    for copy in waits["outward"]:
        copy.wait()
    sums = total[...]
    for z_hi in range(2):
        for y_at in range(0, 4, 2):
            block = jnp.concatenate(
                [
                    outward[y_at + half, z_hi * 4 : z_hi * 4 + 4].reshape(1024, 128)
                    for half in range(2)
                ],
                axis=1,
            )
            at = (z_hi * 4 + y_at) * 128
            sums = sums + dot_nt(attended[:, at : at + 256], block)
    total[...] = sums
    for row in range(6):
        result = total[row * 24 : row * 24 + 24].astype(BF)
        out_ref[row] = result
        if row < 3:
            top_ref[row] = result
        else:
            bottom_ref[row - 3] = result
        first_ref[row] = total[row * 24 : row * 24 + 1].astype(BF)


def level_two(place, above, f, below, col, gain1, gain2, mine, others):
    return pl.pallas_call(
        level_two_kernel,
        out_shape=[
            jax.ShapeDtypeStruct((6, 24, 1024), BF),
            jax.ShapeDtypeStruct((3, 24, 1024), BF),
            jax.ShapeDtypeStruct((3, 24, 1024), BF),
            jax.ShapeDtypeStruct((6, 1, 1024), BF),
        ],
        in_specs=[SMEM] + [VMEM] * 6 + [ANY] * 10,
        out_specs=[VMEM] * 4,
        scratch_shapes=[
            pltpu.VMEM((2, 4, 8, 4, 2, 32, 128), BF),
            pltpu.VMEM((4, 8, 4, 2, 32, 128), BF),
            pltpu.VMEM((4, 8, 4, 2, 96, 128), BF),
            pltpu.VMEM((4, 12, 56, 128), F32),
            pltpu.VMEM((144, 2048), F32),
            pltpu.VMEM((144, 1024), F32),
            pltpu.VMEM((144, 3072), BF),
            pltpu.VMEM((144, 1024), BF),
            pltpu.VMEM((18, 48, 512), BF),
            pltpu.SemaphoreType.DMA((31,)),
        ],
        compiler_params=pltpu.CompilerParams(vmem_limit_bytes=32 * MIB),
        cost_estimate=pl.CostEstimate(
            flops=11_000_000_000, bytes_accessed=14_000_000, transcendentals=1_000_000
        ),
        name="level_two",
    )(place, above, f, below, col, gain1, gain2, *mine, *others)


def edges(top, bottom):
    return to_cell(bottom, 1, 0), to_cell(top, -1, 0)


def column(above, col, below, index, direction):
    part = jnp.concatenate([above[:, index], col, below[:, index]], axis=0)
    return to_cell(part, 0, direction)


def moved_rows(col, start):
    return lax.dynamic_slice_in_dim(col, start, 12, 0)


def moved_back(shift, above, grid, below, col):
    whole = jnp.concatenate([above, grid, below], axis=0)
    count = grid.shape[0]
    whole = lax.dynamic_slice_in_dim(whole, 3 - shift, count, 0)
    col = lax.dynamic_slice_in_dim(col, 3 - shift, count, 0)
    return jnp.concatenate([whole[:, 1:], col], axis=1)


def line(*values):
    values = jnp.concatenate([value.reshape(-1) for value in values])
    return jnp.pad(values, (0, 512 - values.shape[0])).reshape(1, 512)


def shards(
    latent,
    surface,
    table,
    shifts,
    gain_one,
    inward_one,
    outward_one,
    gain_ffn,
    ffn_up,
    ffn_down,
    gain_merge,
    merge_proj,
    gain_two,
    inward_two,
    outward_two,
):
    lat, lon = lax.axis_index("lat"), lax.axis_index("lon")
    shift = jnp.where(shifts[0] <= 3, shifts[0], shifts[0] - 6)
    x, y, z, core = (lon // 2) % 4, lat % 4, (lat // 4) * 4 + lon // 8, lon % 2
    place = jnp.stack([x, y, z, core, lat, shift, jnp.where(core == 0, y, x)]).astype(jnp.int32)

    classes = surface.astype(BF)

    def message(part):
        return jnp.concatenate([latent[part].reshape(-1, 512), line(classes[part])])

    above = to_cell(message(slice(9, 12)), 1, 0)
    below = to_cell(message(slice(0, 3)), -1, 0)

    keep, send = pack(place, merge_proj, inward_two, outward_two)
    shard = jnp.stack([keep, to_core(send)])
    near = jnp.stack([along_z(shard, 1), shard, along_z(shard, -1)])
    far_low, far_high = along_z(near, 3), along_z(near[:2], -3)

    cls = jnp.concatenate(
        [above[144, :144].reshape(3, 48), classes, below[144, :144].reshape(3, 48)]
    )
    left = to_cell(
        jnp.concatenate([above[47:144:48], latent[:, -1], below[47:144:48], line(cls[:, -1])]), 0, 1
    )
    cls = jnp.concatenate([left[18, :18, None], cls[:, :-1]], axis=1)
    cls = jnp.pad(moved_rows(cls, 3 + shift).astype(F32).T, ((0, 0), (0, 4)))
    block = assemble_z(place, far_low, near, far_high)
    from_left, from_right = along(block, False, 1), along(block, False, -1)
    far0, far1, left = lax.optimization_barrier(
        (along(from_left[:4], False, 1), along(from_right[4:], False, -1), left)
    )
    block = assemble(place, block, from_left, from_right, far0, far1)
    from_left, from_right = along(block, True, 1), along(block, True, -1)
    frame, top, bottom, first, last = level_one(
        place, above, latent, below, after(left, block), cls, table,
        gain_one.reshape(1, -1), gain_ffn.reshape(1, -1),
        inward_one, outward_one, ffn_up, ffn_down,
    )
    above, below = edges(top, bottom)
    from_left, from_right = lax.optimization_barrier((from_left, from_right, top))[:2]
    half0, half1, above, below = lax.optimization_barrier(
        (from_left[:2], from_right[2:], above, below)
    )
    mine = [block, from_left, from_right, along(half0, True, 1), along(half1, True, -1)]
    others = [to_core(piece) for piece in after(tuple(mine[:3]), above)]
    left = column(after(above, mine[3])[:, :, None], last, below[:, :, None], 47, 1)
    others += [to_core(piece) for piece in after(tuple(mine[3:]), others[0])]
    level, top, bottom, ends = level_two(
        place, above, frame, below, left,
        gain_merge.reshape(1, -1), gain_two.reshape(1, -1), mine, others,
    )
    right = column(after(above, top)[:, :, None], first, below[:, :, None], 0, -1)
    out_one = moved_back(shift, above, frame, below, right)
    above, below = edges(top, bottom)
    right = column(above[:, :, None], ends, below[:, :, None], 0, -1)
    return out_one, moved_back(shift, above, level, below, right)


def solution(mesh):
    placed = (
        P("lat", "lon", None),
        P("lat", "lon"),
        P(),
        P(),
        P(),
        P(),
        P(),
        P(),
        P(),
        P(),
        P(),
        P("lat", "lon"),
        P(),
        P("lat", "lon"),
        P("lat", "lon"),
    )
    return jax.shard_map(
        shards,
        mesh=mesh,
        in_specs=placed,
        out_specs=(P("lat", "lon", None), P("lat", "lon", None)),
        check_vma=False,
    )
```

```python
import jax
import jax.numpy as jnp
from jax import lax
from jax.experimental import pallas as pl
from jax.experimental.pallas import tpu as pltpu
from jax.sharding import PartitionSpec as P

EPS = 1e-05
BF = jnp.bfloat16
F32 = jnp.float32
AXES = ("lat", "lon")
VMEM = pl.BlockSpec(memory_space=pltpu.VMEM)
SMEM = pl.BlockSpec(memory_space=pltpu.SMEM)
ANY = pl.BlockSpec(memory_space=pl.ANY)
HBM = pl.BlockSpec(memory_space=pltpu.HBM)
MIB = 1024 * 1024

PLACES = [(x, y, z, c) for z in range(8) for y in range(4) for x in range(4) for c in range(2)]


def number(x, y, z, c):
    x, y, z, c = x % 4, y % 4, z % 8, c % 2
    return ((z // 4) * 4 + y) * 32 + ((z % 4) * 4 + x) * 2 + c


def move(array, steps):
    pairs = []
    for x, y, z, c in PLACES:
        dx, dy, dz, dc = steps[c]
        pairs.append((number(x, y, z, c), number(x + dx, y + dy, z + dz, c + dc)))
    return lax.ppermute(array, AXES, pairs)


def along_z(array, step):
    return move(array, ((0, 0, step, 0),) * 2)


def to_core(array):
    return move(array, ((0, 0, 0, 1),) * 2)


def along(array, last, step):
    by_x, by_y = (step, 0, 0, 0), (0, step, 0, 0)
    return move(array, (by_x, by_y) if last else (by_y, by_x))


def to_cell(array, dlat, dlon):
    pairs = [
        (i * 32 + j, ((i + dlat) % 8) * 32 + (j + dlon) % 32) for i in range(8) for j in range(32)
    ]
    return lax.ppermute(array, AXES, pairs)


def after(value, *others):
    return lax.optimization_barrier((value,) + others)[0]


def pack_kernel(place_ref, merge_ref, inward_ref, outward_ref, keep_ref, send_ref):
    def store(first, second):
        first[0:32] = merge_ref[:, :128]
        first[32:64] = merge_ref[:, 128:]
        first[64:96] = outward_ref[...]
        second[...] = inward_ref[...]

    @pl.when(place_ref[3] == 0)
    def _():
        store(keep_ref, send_ref)

    @pl.when(place_ref[3] == 1)
    def _():
        store(send_ref, keep_ref)


def pack(place, merge, inward, outward):
    return pl.pallas_call(
        pack_kernel,
        out_shape=[jax.ShapeDtypeStruct((96, 128), BF)] * 2,
        in_specs=[SMEM] + [VMEM] * 3,
        out_specs=[VMEM] * 2,
        compiler_params=pltpu.CompilerParams(vmem_limit_bytes=56 * MIB),
        name="pack",
    )(place, merge.T, inward.T, outward.T)


def assemble_z_kernel(place_ref, low_ref, near_ref, high_ref, out_ref, sem):
    z, core = place_ref[2], place_ref[3]
    copies = []
    for step in range(8):
        ref, first = ((low_ref, 0), (near_ref, 3), (high_ref, 6))[step // 3]
        to = lax.rem(z + 4 + step, 8)
        for other in range(2):
            target = out_ref.at[to, lax.rem(core + other, 2)]
            copies.append(
                pltpu.make_async_copy(ref.at[step - first, other], target, sem.at[len(copies)])
            )
    for copy in copies:
        copy.start()
    for copy in copies:
        copy.wait()


def assemble_z(place, low, near, high):
    return pl.pallas_call(
        assemble_z_kernel,
        out_shape=jax.ShapeDtypeStruct((8, 2, 96, 128), BF),
        in_specs=[SMEM] + [ANY] * 3,
        out_specs=VMEM,
        scratch_shapes=[pltpu.SemaphoreType.DMA((16,))],
        compiler_params=pltpu.CompilerParams(vmem_limit_bytes=6 * MIB),
        name="assemble_z",
    )(place, low, near, high)


def assemble_kernel(place_ref, own, left, right, half0, half1, out_ref, sem):
    at = place_ref[6]
    copies = [
        pltpu.make_async_copy(piece, out_ref.at[lax.rem(at + step, 4), lo:hi], sem.at[index])
        for index, (piece, step, lo, hi) in enumerate(
            ((own, 0, 0, 8), (left, 3, 0, 8), (right, 1, 0, 8), (half0, 2, 0, 4), (half1, 2, 4, 8))
        )
    ]
    for copy in copies:
        copy.start()
    for copy in copies:
        copy.wait()


def assemble(place, *pieces):
    return pl.pallas_call(
        assemble_kernel,
        out_shape=jax.ShapeDtypeStruct((4, 8, 2, 96, 128), BF),
        in_specs=[SMEM] + [ANY] * 5,
        out_specs=VMEM,
        scratch_shapes=[pltpu.SemaphoreType.DMA((5,))],
        compiler_params=pltpu.CompilerParams(vmem_limit_bytes=6 * MIB),
        name="assemble",
    )(place, *pieces)


def normed(hidden, gain):
    centre = jnp.mean(hidden, axis=-1, keepdims=True)
    centred = hidden - centre
    variance = jnp.mean(centred * centred, axis=-1, keepdims=True)
    return centred * lax.rsqrt(variance + EPS) * gain


def dot(a, b):
    return jnp.dot(a, b, preferred_element_type=F32)


def dot_nt(a, b):
    return lax.dot_general(a, b, (((1,), (1,)), ((), ())), preferred_element_type=F32)


def window_mask(split, edge):
    def code(axis):
        token = lax.broadcasted_iota(jnp.int32, (144, 144), axis)
        row = (token * 2731) >> 16
        col = token - 24 * row
        return jnp.where(col >= 12, 1, 0) + jnp.where(row >= split, 2, 0) * edge

    return code(0) == code(1)


def attend_pair(queries, keys, values, mask):
    low = lax.broadcasted_iota(jnp.int32, (144, 128), 1) < 64
    zero = jnp.zeros_like(queries)
    both = jnp.concatenate([jnp.where(low, queries, zero), jnp.where(low, zero, queries)], axis=0)
    scores = jnp.where(mask, dot_nt(both, keys), -1e9)
    weights = jnp.exp(scores - jnp.max(scores, axis=-1, keepdims=True))
    total = jnp.sum(weights, axis=-1, keepdims=True)
    mixed = dot(weights.astype(BF), values) * (1.0 / total)
    return jnp.where(low, mixed[:144], mixed[144:])


def level_one_kernel(
    place_ref,
    above_ref,
    x_ref,
    below_ref,
    col_ref,
    cls_ref,
    table_ref,
    gain1_ref,
    gain2_ref,
    inward_hbm,
    outward_hbm,
    up_hbm,
    down_hbm,
    out_ref,
    top_ref,
    bottom_ref,
    first_ref,
    last_ref,
    inward,
    outward,
    up,
    down,
    rim,
    residual,
    attended,
    ext,
    cols,
    sem,
):
    copies = [
        pltpu.make_async_copy(source, target, sem.at[index])
        for index, (source, target) in enumerate(
            ((inward_hbm, inward), (outward_hbm, outward), (up_hbm, up), (down_hbm, down))
        )
    ]
    for copy in copies:
        copy.start()
    lat, shift = place_ref[4], place_ref[5]
    split = jnp.where(shift > 0, 6 - shift, -shift)
    for row in range(3):
        ext[row] = above_ref[row * 48 : row * 48 + 48]
        ext[15 + row] = below_ref[row * 48 : row * 48 + 48]
    for row in range(12):
        ext[3 + row] = x_ref[row]
    for row in range(18):
        cols[row] = col_ref[row : row + 1].astype(F32)
    for band in range(2):
        for row in range(6):
            frame = band * 6 + row
            rim[row, 8:56] = ext[3 + shift + frame].astype(F32)
            rim[row, 7:8] = cols[3 + shift + frame]
            cls = cls_ref[:, frame : frame + 1]
            embedded = jnp.where(
                cls == 0.0, table_ref[0:1], jnp.where(cls == 1.0, table_ref[1:2], table_ref[2:3])
            )
            residual[row * 48 : (row + 1) * 48] = rim[row, 7:55] + embedded
        normal = normed(residual[...], gain1_ref[...]).astype(BF)
        if band == 1:
            edge = jnp.where((lat == 7) & (shift > 0), 1, 0)
        else:
            edge = jnp.where((lat == 0) & (shift < 0), 1, 0)
        mask = window_mask(split, edge)
        mask = jnp.concatenate([mask, mask], axis=0)
        if band == 0:
            copies[0].wait()
        for quarter in range(2):
            at = quarter * 256
            parts = [
                dot(normal, inward[:, part * 512 + at : part * 512 + at + 256]).reshape(6, 48, 256)
                for part in range(3)
            ]
            for pair in range(2):
                lanes = slice(pair * 128, pair * 128 + 128)
                for block in range(2):
                    span = slice(block * 24, block * 24 + 24)
                    queries, keys, values = (
                        part[:, span, lanes].reshape(144, 128).astype(BF) for part in parts
                    )
                    mixed = attend_pair(queries * BF(0.125), keys, values, mask)
                    attended[:, span, at + pair * 128 : at + pair * 128 + 128] = mixed.reshape(
                        6, 24, 128
                    )
        if band == 0:
            copies[1].wait()
        mid = residual[...] + dot(attended[...].reshape(288, 512).astype(BF), outward[...])
        residual[...] = mid
        normal = normed(mid, gain2_ref[...]).astype(BF)
        if band == 0:
            copies[2].wait()
            copies[3].wait()
        for chunk in range(4):
            part = slice(chunk * 512, chunk * 512 + 512)
            hidden = jax.nn.gelu(dot(normal, up[:, part])).astype(BF)
            residual[...] += dot(hidden, down[part])
        result = residual[...].astype(BF).reshape(6, 48, 512)
        out_ref[band * 6 : band * 6 + 6] = result
        if band == 0:
            top_ref[...] = result[:3]
        else:
            bottom_ref[...] = result[3:]
        for row in range(6):
            first_ref[band * 6 + row] = residual[row * 48 : row * 48 + 1].astype(BF)
            last_ref[band * 6 + row] = residual[row * 48 + 47 : row * 48 + 48].astype(BF)


def level_one(place, above, x, below, col, cls, table, gain1, gain2, inward, outward, up, down):
    return pl.pallas_call(
        level_one_kernel,
        out_shape=[
            jax.ShapeDtypeStruct((12, 48, 512), BF),
            jax.ShapeDtypeStruct((3, 48, 512), BF),
            jax.ShapeDtypeStruct((3, 48, 512), BF),
            jax.ShapeDtypeStruct((12, 1, 512), BF),
            jax.ShapeDtypeStruct((12, 1, 512), BF),
        ],
        in_specs=[SMEM] + [VMEM] * 8 + [HBM] * 4,
        out_specs=[VMEM] * 5,
        scratch_shapes=[
            pltpu.VMEM((512, 1536), BF),
            pltpu.VMEM((512, 512), BF),
            pltpu.VMEM((512, 2048), BF),
            pltpu.VMEM((2048, 512), BF),
            pltpu.VMEM((6, 56, 512), F32),
            pltpu.VMEM((288, 512), F32),
            pltpu.VMEM((6, 48, 512), F32),
            pltpu.VMEM((18, 48, 512), BF),
            pltpu.VMEM((18, 1, 512), F32),
            pltpu.SemaphoreType.DMA((4,)),
        ],
        compiler_params=pltpu.CompilerParams(vmem_limit_bytes=50 * MIB),
        cost_estimate=pl.CostEstimate(
            flops=13_000_000_000, bytes_accessed=8_000_000, transcendentals=3_000_000
        ),
        name="level_one",
    )(place, above, x, below, col, cls, table, gain1, gain2, inward, outward, up, down)


def level_two_kernel(place_ref, above_ref, f_ref, below_ref, col_ref, gain1_ref, gain2_ref, *refs):
    mine, others = refs[0:5], refs[5:10]
    (out_ref, top_ref, bottom_ref, first_ref) = refs[10:14]
    merge, outward, inward, rim, merged, total, packed, attended, ext, sem = refs[14:]
    x, y, core = place_ref[0], place_ref[1], place_ref[3]
    lat, shift = place_ref[4], place_ref[5]

    def jobs(first, second):
        lists = {"merge": [], "inward": [], "outward": []}
        count = 0
        for piece, step, lo, hi in zip(
            range(5), (0, 3, 1, 2, 2), (0, 0, 0, 0, 2), (4, 4, 4, 2, 4)
        ):
            to_x, to_y = lax.rem(x + step, 4), lax.rem(y + step, 4)
            for section in range(3):
                rows = slice(section * 32, section * 32 + 32)
                target = (merge.at[0], merge.at[1], outward)[section]
                lists["outward" if section == 2 else "merge"].append(
                    pltpu.make_async_copy(
                        first[piece].at[:, :, :, rows],
                        target.at[lo:hi, :, to_x],
                        sem.at[count],
                    )
                )
                count += 1
            for column in range(lo, hi):
                lists["inward"].append(
                    pltpu.make_async_copy(
                        second[piece].at[column - lo], inward.at[to_y, :, column], sem.at[count]
                    )
                )
                count += 1
        return lists

    @pl.when(core == 0)
    def _():
        for copies in jobs(mine, others).values():
            for copy in copies:
                copy.start()

    @pl.when(core == 1)
    def _():
        for copies in jobs(others, mine).values():
            for copy in copies:
                copy.start()

    waits = jobs(mine, others)
    for row in range(3):
        ext[row] = above_ref[row]
        ext[15 + row] = below_ref[row]
    for row in range(12):
        ext[3 + row] = f_ref[row]
    for row in range(12):
        values = ext[3 + shift + row].astype(F32)
        left = col_ref[3 + shift + row].astype(F32)
        for quarter in range(4):
            lanes = slice(quarter * 128, quarter * 128 + 128)
            rim[quarter, row, 8:56] = values[:, lanes]
            rim[quarter, row, 7:8] = left[:, lanes]
    for row in range(6):
        for part in range(4):
            for quarter in range(4):
                at = part * 512 + quarter * 128
                merged[row * 24 : row * 24 + 24, at : at + 128] = rim[
                    quarter, 2 * row + part % 2, pl.ds(7 + part // 2, 24, stride=2), :
                ]
    normal = normed(merged[...], gain1_ref[...]).astype(BF)
    for copy in waits["merge"]:
        copy.wait()
    reduced = None
    for z_hi in range(2):
        for y_at in range(4):
            block = jnp.concatenate(
                [
                    merge[half, y_at, z_hi * 4 : z_hi * 4 + 4].reshape(1024, 128)
                    for half in range(2)
                ],
                axis=1,
            )
            at = (z_hi * 4 + y_at) * 256
            part = dot_nt(normal[:, at : at + 256], block)
            reduced = part if reduced is None else reduced + part
    reduced = reduced.astype(BF).astype(F32)
    total[...] = reduced
    normal = normed(reduced, gain2_ref[...]).astype(BF)
    for copy in waits["inward"]:
        copy.wait()
    for third in range(3):
        for z_hi in range(2):
            for y_at in range(0, 4, 2):
                block = jnp.concatenate(
                    [
                        inward[y_at + half, z_hi * 4 : z_hi * 4 + 4].reshape(3072, 128)[
                            third * 1024 : third * 1024 + 1024
                        ]
                        for half in range(2)
                    ],
                    axis=1,
                )
                at = (z_hi * 4 + y_at) * 128
                part = dot_nt(normal[:, at : at + 256], block)
                if z_hi + y_at == 0:
                    sums = part
                else:
                    sums = sums + part
        if third == 0:
            sums = sums * 0.125
        packed[:, third * 1024 : third * 1024 + 1024] = sums.astype(BF)

    split = jnp.where(shift > 0, 6 - shift, -shift)
    edge = jnp.where(((lat == 7) & (shift > 0)) | ((lat == 0) & (shift < 0)), 1, 0)
    mask = window_mask(split, edge)
    mask = jnp.concatenate([mask, mask], axis=0)
    for pair in range(8):
        at = pair * 128
        mixed = attend_pair(
            packed[:, at : at + 128],
            packed[:, 1024 + at : 1024 + at + 128],
            packed[:, 2048 + at : 2048 + at + 128],
            mask,
        )
        attended[:, at : at + 128] = mixed.astype(BF)
    for copy in waits["outward"]:
        copy.wait()
    sums = total[...]
    for z_hi in range(2):
        for y_at in range(0, 4, 2):
            block = jnp.concatenate(
                [
                    outward[y_at + half, z_hi * 4 : z_hi * 4 + 4].reshape(1024, 128)
                    for half in range(2)
                ],
                axis=1,
            )
            at = (z_hi * 4 + y_at) * 128
            sums = sums + dot_nt(attended[:, at : at + 256], block)
    total[...] = sums
    for row in range(6):
        result = total[row * 24 : row * 24 + 24].astype(BF)
        out_ref[row] = result
        if row < 3:
            top_ref[row] = result
        else:
            bottom_ref[row - 3] = result
        first_ref[row] = total[row * 24 : row * 24 + 1].astype(BF)


def level_two(place, above, f, below, col, gain1, gain2, mine, others):
    return pl.pallas_call(
        level_two_kernel,
        out_shape=[
            jax.ShapeDtypeStruct((6, 24, 1024), BF),
            jax.ShapeDtypeStruct((3, 24, 1024), BF),
            jax.ShapeDtypeStruct((3, 24, 1024), BF),
            jax.ShapeDtypeStruct((6, 1, 1024), BF),
        ],
        in_specs=[SMEM] + [VMEM] * 6 + [ANY] * 10,
        out_specs=[VMEM] * 4,
        scratch_shapes=[
            pltpu.VMEM((2, 4, 8, 4, 2, 32, 128), BF),
            pltpu.VMEM((4, 8, 4, 2, 32, 128), BF),
            pltpu.VMEM((4, 8, 4, 2, 96, 128), BF),
            pltpu.VMEM((4, 12, 56, 128), F32),
            pltpu.VMEM((144, 2048), F32),
            pltpu.VMEM((144, 1024), F32),
            pltpu.VMEM((144, 3072), BF),
            pltpu.VMEM((144, 1024), BF),
            pltpu.VMEM((18, 48, 512), BF),
            pltpu.SemaphoreType.DMA((31,)),
        ],
        compiler_params=pltpu.CompilerParams(vmem_limit_bytes=32 * MIB),
        cost_estimate=pl.CostEstimate(
            flops=11_000_000_000, bytes_accessed=14_000_000, transcendentals=1_000_000
        ),
        name="level_two",
    )(place, above, f, below, col, gain1, gain2, *mine, *others)


def edges(top, bottom):
    return to_cell(bottom, 1, 0), to_cell(top, -1, 0)


def column(above, col, below, index, direction):
    part = jnp.concatenate([above[:, index], col, below[:, index]], axis=0)
    return to_cell(part, 0, direction)


def moved_rows(col, start):
    return lax.dynamic_slice_in_dim(col, start, 12, 0)


def moved_back(shift, above, grid, below, col):
    whole = jnp.concatenate([above, grid, below], axis=0)
    count = grid.shape[0]
    whole = lax.dynamic_slice_in_dim(whole, 3 - shift, count, 0)
    col = lax.dynamic_slice_in_dim(col, 3 - shift, count, 0)
    return jnp.concatenate([whole[:, 1:], col], axis=1)


def line(*values):
    values = jnp.concatenate([value.reshape(-1) for value in values])
    return jnp.pad(values, (0, 512 - values.shape[0])).reshape(1, 512)


def shards(
    latent,
    surface,
    table,
    shifts,
    gain_one,
    inward_one,
    outward_one,
    gain_ffn,
    ffn_up,
    ffn_down,
    gain_merge,
    merge_proj,
    gain_two,
    inward_two,
    outward_two,
):
    lat, lon = lax.axis_index("lat"), lax.axis_index("lon")
    shift = jnp.where(shifts[0] <= 3, shifts[0], shifts[0] - 6)
    x, y, z, core = (lon // 2) % 4, lat % 4, (lat // 4) * 4 + lon // 8, lon % 2
    place = jnp.stack([x, y, z, core, lat, shift, jnp.where(core == 0, y, x)]).astype(jnp.int32)

    classes = surface.astype(BF)

    def message(part):
        return jnp.concatenate([latent[part].reshape(-1, 512), line(classes[part])])

    above = to_cell(message(slice(9, 12)), 1, 0)
    below = to_cell(message(slice(0, 3)), -1, 0)

    keep, send = pack(place, merge_proj, inward_two, outward_two)
    shard = jnp.stack([keep, to_core(send)])
    near = jnp.stack([along_z(shard, 1), shard, along_z(shard, -1)])
    far_low, far_high = along_z(near, 3), along_z(near[:2], -3)

    cls = jnp.concatenate(
        [above[144, :144].reshape(3, 48), classes, below[144, :144].reshape(3, 48)]
    )
    left = to_cell(
        jnp.concatenate([above[47:144:48], latent[:, -1], below[47:144:48], line(cls[:, -1])]), 0, 1
    )
    cls = jnp.concatenate([left[18, :18, None], cls[:, :-1]], axis=1)
    cls = jnp.pad(moved_rows(cls, 3 + shift).astype(F32).T, ((0, 0), (0, 4)))
    block = assemble_z(place, far_low, near, far_high)
    from_left, from_right = along(block, False, 1), along(block, False, -1)
    far0, far1, left = lax.optimization_barrier(
        (along(from_left[:4], False, 1), along(from_right[4:], False, -1), left)
    )
    block = assemble(place, block, from_left, from_right, far0, far1)
    from_left, from_right = along(block, True, 1), along(block, True, -1)
    frame, top, bottom, first, last = level_one(
        place, above, latent, below, after(left, block), cls, table,
        gain_one.reshape(1, -1), gain_ffn.reshape(1, -1),
        inward_one, outward_one, ffn_up, ffn_down,
    )
    above, below = edges(top, bottom)
    from_left, from_right = lax.optimization_barrier((from_left, from_right, top))[:2]
    half0, half1, above, below = lax.optimization_barrier(
        (from_left[:2], from_right[2:], above, below)
    )
    mine = [block, from_left, from_right, along(half0, True, 1), along(half1, True, -1)]
    others = [to_core(piece) for piece in after(tuple(mine[:3]), above)]
    left = column(after(above, mine[3])[:, :, None], last, below[:, :, None], 47, 1)
    others += [to_core(piece) for piece in mine[3:]]
    level, top, bottom, ends = level_two(
        place, above, frame, below, left,
        gain_merge.reshape(1, -1), gain_two.reshape(1, -1), mine, others,
    )
    level_above, level_below = edges(top, bottom)
    right = column(
        after(above, level_above, level_below)[:, :, None], first, below[:, :, None], 0, -1
    )
    out_one = moved_back(shift, above, frame, below, right)
    right = column(level_above[:, :, None], ends, level_below[:, :, None], 0, -1)
    return out_one, moved_back(shift, level_above, level, level_below, right)


def solution(mesh):
    placed = (
        P("lat", "lon", None),
        P("lat", "lon"),
        P(),
        P(),
        P(),
        P(),
        P(),
        P(),
        P(),
        P(),
        P(),
        P("lat", "lon"),
        P(),
        P("lat", "lon"),
        P("lat", "lon"),
    )
    return jax.shard_map(
        shards,
        mesh=mesh,
        in_specs=placed,
        out_specs=(P("lat", "lon", None), P("lat", "lon", None)),
        check_vma=False,
    )
```

```python
import jax
import jax.numpy as jnp
from jax import lax
from jax.experimental import pallas as pl
from jax.experimental.pallas import tpu as pltpu
from jax.sharding import PartitionSpec as P

EPS = 1e-05
BF = jnp.bfloat16
F32 = jnp.float32
AXES = ("lat", "lon")
VMEM = pl.BlockSpec(memory_space=pltpu.VMEM)
SMEM = pl.BlockSpec(memory_space=pltpu.SMEM)
ANY = pl.BlockSpec(memory_space=pl.ANY)
HBM = pl.BlockSpec(memory_space=pltpu.HBM)
MIB = 1024 * 1024

PLACES = [(x, y, z, c) for z in range(8) for y in range(4) for x in range(4) for c in range(2)]


def number(x, y, z, c):
    x, y, z, c = x % 4, y % 4, z % 8, c % 2
    return ((z // 4) * 4 + y) * 32 + ((z % 4) * 4 + x) * 2 + c


def move(array, steps):
    pairs = []
    for x, y, z, c in PLACES:
        dx, dy, dz, dc = steps[c]
        pairs.append((number(x, y, z, c), number(x + dx, y + dy, z + dz, c + dc)))
    return lax.ppermute(array, AXES, pairs)


def along_z(array, step):
    return move(array, ((0, 0, step, 0),) * 2)


def to_core(array):
    return move(array, ((0, 0, 0, 1),) * 2)


def along(array, last, step):
    by_x, by_y = (step, 0, 0, 0), (0, step, 0, 0)
    return move(array, (by_x, by_y) if last else (by_y, by_x))


def to_cell(array, dlat, dlon):
    pairs = [
        (i * 32 + j, ((i + dlat) % 8) * 32 + (j + dlon) % 32) for i in range(8) for j in range(32)
    ]
    return lax.ppermute(array, AXES, pairs)


def after(value, *others):
    return lax.optimization_barrier((value,) + others)[0]


def pack_kernel(place_ref, merge_ref, inward_ref, outward_ref, keep_ref, send_ref):
    def store(first, second):
        first[0:32] = merge_ref[:, :128]
        first[32:64] = merge_ref[:, 128:]
        first[64:96] = outward_ref[...]
        second[...] = inward_ref[...]

    @pl.when(place_ref[3] == 0)
    def _():
        store(keep_ref, send_ref)

    @pl.when(place_ref[3] == 1)
    def _():
        store(send_ref, keep_ref)


def pack(place, merge, inward, outward):
    return pl.pallas_call(
        pack_kernel,
        out_shape=[jax.ShapeDtypeStruct((96, 128), BF)] * 2,
        in_specs=[SMEM] + [VMEM] * 3,
        out_specs=[VMEM] * 2,
        compiler_params=pltpu.CompilerParams(vmem_limit_bytes=56 * MIB),
        name="pack",
    )(place, merge.T, inward.T, outward.T)


def assemble_z_kernel(place_ref, low_ref, near_ref, high_ref, out_ref, sem):
    z, core = place_ref[2], place_ref[3]
    copies = []
    for step in range(8):
        ref, first = ((low_ref, 0), (near_ref, 3), (high_ref, 6))[step // 3]
        to = lax.rem(z + 4 + step, 8)
        for other in range(2):
            target = out_ref.at[to, lax.rem(core + other, 2)]
            copies.append(
                pltpu.make_async_copy(ref.at[step - first, other], target, sem.at[len(copies)])
            )
    for copy in copies:
        copy.start()
    for copy in copies:
        copy.wait()


def assemble_z(place, low, near, high):
    return pl.pallas_call(
        assemble_z_kernel,
        out_shape=jax.ShapeDtypeStruct((8, 2, 96, 128), BF),
        in_specs=[SMEM] + [ANY] * 3,
        out_specs=VMEM,
        scratch_shapes=[pltpu.SemaphoreType.DMA((16,))],
        compiler_params=pltpu.CompilerParams(vmem_limit_bytes=6 * MIB),
        name="assemble_z",
    )(place, low, near, high)


def assemble_kernel(place_ref, own, left, right, half0, half1, out_ref, sem):
    at = place_ref[6]
    copies = [
        pltpu.make_async_copy(piece, out_ref.at[lax.rem(at + step, 4), lo:hi], sem.at[index])
        for index, (piece, step, lo, hi) in enumerate(
            ((own, 0, 0, 8), (left, 3, 0, 8), (right, 1, 0, 8), (half0, 2, 0, 4), (half1, 2, 4, 8))
        )
    ]
    for copy in copies:
        copy.start()
    for copy in copies:
        copy.wait()


def assemble(place, *pieces):
    return pl.pallas_call(
        assemble_kernel,
        out_shape=jax.ShapeDtypeStruct((4, 8, 2, 96, 128), BF),
        in_specs=[SMEM] + [ANY] * 5,
        out_specs=VMEM,
        scratch_shapes=[pltpu.SemaphoreType.DMA((5,))],
        compiler_params=pltpu.CompilerParams(vmem_limit_bytes=6 * MIB),
        name="assemble",
    )(place, *pieces)


def normed(hidden, gain):
    centre = jnp.mean(hidden, axis=-1, keepdims=True)
    centred = hidden - centre
    variance = jnp.mean(centred * centred, axis=-1, keepdims=True)
    return centred * lax.rsqrt(variance + EPS) * gain


def dot(a, b):
    return jnp.dot(a, b, preferred_element_type=F32)


def dot_nt(a, b):
    return lax.dot_general(a, b, (((1,), (1,)), ((), ())), preferred_element_type=F32)


def window_mask(split, edge):
    def code(axis):
        token = lax.broadcasted_iota(jnp.int32, (144, 144), axis)
        row = (token * 2731) >> 16
        col = token - 24 * row
        return jnp.where(col >= 12, 1, 0) + jnp.where(row >= split, 2, 0) * edge

    return code(0) == code(1)


def attend_pair(queries, keys, values, mask):
    low = lax.broadcasted_iota(jnp.int32, (144, 128), 1) < 64
    zero = jnp.zeros_like(queries)
    both = jnp.concatenate([jnp.where(low, queries, zero), jnp.where(low, zero, queries)], axis=0)
    scores = jnp.where(mask, dot_nt(both, keys), -1e9)
    weights = jnp.exp(scores - jnp.max(scores, axis=-1, keepdims=True))
    total = jnp.sum(weights, axis=-1, keepdims=True)
    mixed = dot(weights.astype(BF), values) * (1.0 / total)
    return jnp.where(low, mixed[:144], mixed[144:])


def level_one_kernel(
    place_ref,
    above_ref,
    x_ref,
    below_ref,
    col_ref,
    cls_ref,
    table_ref,
    gain1_ref,
    gain2_ref,
    inward_hbm,
    outward_hbm,
    up_hbm,
    down_hbm,
    out_ref,
    top_ref,
    bottom_ref,
    first_ref,
    last_ref,
    inward,
    outward,
    up,
    down,
    rim,
    residual,
    attended,
    ext,
    cols,
    sem,
):
    copies = [
        pltpu.make_async_copy(source, target, sem.at[index])
        for index, (source, target) in enumerate(
            ((inward_hbm, inward), (outward_hbm, outward), (up_hbm, up), (down_hbm, down))
        )
    ]
    for copy in copies:
        copy.start()
    lat, shift = place_ref[4], place_ref[5]
    split = jnp.where(shift > 0, 6 - shift, -shift)
    for row in range(3):
        ext[row] = above_ref[row * 48 : row * 48 + 48]
        ext[15 + row] = below_ref[row * 48 : row * 48 + 48]
    for row in range(12):
        ext[3 + row] = x_ref[row]
    for row in range(18):
        cols[row] = col_ref[row : row + 1].astype(F32)
    for band in range(2):
        for row in range(6):
            frame = band * 6 + row
            rim[row, 8:56] = ext[3 + shift + frame].astype(F32)
            rim[row, 7:8] = cols[3 + shift + frame]
            cls = cls_ref[:, frame : frame + 1]
            embedded = jnp.where(
                cls == 0.0, table_ref[0:1], jnp.where(cls == 1.0, table_ref[1:2], table_ref[2:3])
            )
            residual[row * 48 : (row + 1) * 48] = rim[row, 7:55] + embedded
        normal = normed(residual[...], gain1_ref[...]).astype(BF)
        if band == 1:
            edge = jnp.where((lat == 7) & (shift > 0), 1, 0)
        else:
            edge = jnp.where((lat == 0) & (shift < 0), 1, 0)
        mask = window_mask(split, edge)
        mask = jnp.concatenate([mask, mask], axis=0)
        if band == 0:
            copies[0].wait()
        for quarter in range(2):
            at = quarter * 256
            parts = [
                dot(normal, inward[:, part * 512 + at : part * 512 + at + 256]).reshape(6, 48, 256)
                for part in range(3)
            ]
            for pair in range(2):
                lanes = slice(pair * 128, pair * 128 + 128)
                for block in range(2):
                    span = slice(block * 24, block * 24 + 24)
                    queries, keys, values = (
                        part[:, span, lanes].reshape(144, 128).astype(BF) for part in parts
                    )
                    mixed = attend_pair(queries * BF(0.125), keys, values, mask)
                    attended[:, span, at + pair * 128 : at + pair * 128 + 128] = mixed.reshape(
                        6, 24, 128
                    )
        if band == 0:
            copies[1].wait()
        mid = residual[...] + dot(attended[...].reshape(288, 512).astype(BF), outward[...])
        residual[...] = mid
        normal = normed(mid, gain2_ref[...]).astype(BF)
        if band == 0:
            copies[2].wait()
            copies[3].wait()
        for chunk in range(4):
            part = slice(chunk * 512, chunk * 512 + 512)
            hidden = jax.nn.gelu(dot(normal, up[:, part])).astype(BF)
            residual[...] += dot(hidden, down[part])
        result = residual[...].astype(BF).reshape(6, 48, 512)
        out_ref[band * 6 : band * 6 + 6] = result
        if band == 0:
            top_ref[...] = result[:3]
        else:
            bottom_ref[...] = result[3:]
        for row in range(6):
            first_ref[band * 6 + row] = residual[row * 48 : row * 48 + 1].astype(BF)
            last_ref[band * 6 + row] = residual[row * 48 + 47 : row * 48 + 48].astype(BF)


def level_one(place, above, x, below, col, cls, table, gain1, gain2, inward, outward, up, down):
    return pl.pallas_call(
        level_one_kernel,
        out_shape=[
            jax.ShapeDtypeStruct((12, 48, 512), BF),
            jax.ShapeDtypeStruct((3, 48, 512), BF),
            jax.ShapeDtypeStruct((3, 48, 512), BF),
            jax.ShapeDtypeStruct((12, 1, 512), BF),
            jax.ShapeDtypeStruct((12, 1, 512), BF),
        ],
        in_specs=[SMEM] + [VMEM] * 8 + [HBM] * 4,
        out_specs=[VMEM] * 5,
        scratch_shapes=[
            pltpu.VMEM((512, 1536), BF),
            pltpu.VMEM((512, 512), BF),
            pltpu.VMEM((512, 2048), BF),
            pltpu.VMEM((2048, 512), BF),
            pltpu.VMEM((6, 56, 512), F32),
            pltpu.VMEM((288, 512), F32),
            pltpu.VMEM((6, 48, 512), F32),
            pltpu.VMEM((18, 48, 512), BF),
            pltpu.VMEM((18, 1, 512), F32),
            pltpu.SemaphoreType.DMA((4,)),
        ],
        compiler_params=pltpu.CompilerParams(vmem_limit_bytes=50 * MIB),
        cost_estimate=pl.CostEstimate(
            flops=13_000_000_000, bytes_accessed=8_000_000, transcendentals=3_000_000
        ),
        name="level_one",
    )(place, above, x, below, col, cls, table, gain1, gain2, inward, outward, up, down)


def level_two_kernel(place_ref, above_ref, f_ref, below_ref, col_ref, gain1_ref, gain2_ref, *refs):
    mine, others = refs[0:5], refs[5:10]
    (out_ref, top_ref, bottom_ref, first_ref) = refs[10:14]
    merge, outward, inward, rim, merged, total, packed, attended, ext, sem = refs[14:]
    x, y, core = place_ref[0], place_ref[1], place_ref[3]
    lat, shift = place_ref[4], place_ref[5]

    def jobs(first, second):
        lists = {"merge": [], "inward": [], "outward": []}
        count = 0
        for piece, step, lo, hi in zip(
            range(5), (0, 3, 1, 2, 2), (0, 0, 0, 0, 2), (4, 4, 4, 2, 4)
        ):
            to_x, to_y = lax.rem(x + step, 4), lax.rem(y + step, 4)
            for section in range(3):
                rows = slice(section * 32, section * 32 + 32)
                target = (merge.at[0], merge.at[1], outward)[section]
                lists["outward" if section == 2 else "merge"].append(
                    pltpu.make_async_copy(
                        first[piece].at[:, :, :, rows],
                        target.at[lo:hi, :, to_x],
                        sem.at[count],
                    )
                )
                count += 1
            for column in range(lo, hi):
                lists["inward"].append(
                    pltpu.make_async_copy(
                        second[piece].at[column - lo], inward.at[to_y, :, column], sem.at[count]
                    )
                )
                count += 1
        return lists

    @pl.when(core == 0)
    def _():
        for copies in jobs(mine, others).values():
            for copy in copies:
                copy.start()

    @pl.when(core == 1)
    def _():
        for copies in jobs(others, mine).values():
            for copy in copies:
                copy.start()

    waits = jobs(mine, others)
    for row in range(3):
        ext[row] = above_ref[row]
        ext[15 + row] = below_ref[row]
    for row in range(12):
        ext[3 + row] = f_ref[row]
    for row in range(12):
        values = ext[3 + shift + row].astype(F32)
        left = col_ref[3 + shift + row].astype(F32)
        for quarter in range(4):
            lanes = slice(quarter * 128, quarter * 128 + 128)
            rim[quarter, row, 8:56] = values[:, lanes]
            rim[quarter, row, 7:8] = left[:, lanes]
    for row in range(6):
        for part in range(4):
            for quarter in range(4):
                at = part * 512 + quarter * 128
                merged[row * 24 : row * 24 + 24, at : at + 128] = rim[
                    quarter, 2 * row + part % 2, pl.ds(7 + part // 2, 24, stride=2), :
                ]
    normal = normed(merged[...], gain1_ref[...]).astype(BF)
    for copy in waits["merge"]:
        copy.wait()
    reduced = None
    for z_hi in range(2):
        for y_at in range(4):
            block = jnp.concatenate(
                [
                    merge[half, y_at, z_hi * 4 : z_hi * 4 + 4].reshape(1024, 128)
                    for half in range(2)
                ],
                axis=1,
            )
            at = (z_hi * 4 + y_at) * 256
            part = dot_nt(normal[:, at : at + 256], block)
            reduced = part if reduced is None else reduced + part
    reduced = reduced.astype(BF).astype(F32)
    total[...] = reduced
    normal = normed(reduced, gain2_ref[...]).astype(BF)
    for copy in waits["inward"]:
        copy.wait()
    for third in range(3):
        for z_hi in range(2):
            for y_at in range(0, 4, 2):
                block = jnp.concatenate(
                    [
                        inward[y_at + half, z_hi * 4 : z_hi * 4 + 4].reshape(3072, 128)[
                            third * 1024 : third * 1024 + 1024
                        ]
                        for half in range(2)
                    ],
                    axis=1,
                )
                at = (z_hi * 4 + y_at) * 128
                part = dot_nt(normal[:, at : at + 256], block)
                if z_hi + y_at == 0:
                    sums = part
                else:
                    sums = sums + part
        if third == 0:
            sums = sums * 0.125
        packed[:, third * 1024 : third * 1024 + 1024] = sums.astype(BF)

    split = jnp.where(shift > 0, 6 - shift, -shift)
    edge = jnp.where(((lat == 7) & (shift > 0)) | ((lat == 0) & (shift < 0)), 1, 0)
    mask = window_mask(split, edge)
    mask = jnp.concatenate([mask, mask], axis=0)
    for pair in range(8):
        at = pair * 128
        mixed = attend_pair(
            packed[:, at : at + 128],
            packed[:, 1024 + at : 1024 + at + 128],
            packed[:, 2048 + at : 2048 + at + 128],
            mask,
        )
        attended[:, at : at + 128] = mixed.astype(BF)
    for copy in waits["outward"]:
        copy.wait()
    sums = total[...]
    for z_hi in range(2):
        for y_at in range(0, 4, 2):
            block = jnp.concatenate(
                [
                    outward[y_at + half, z_hi * 4 : z_hi * 4 + 4].reshape(1024, 128)
                    for half in range(2)
                ],
                axis=1,
            )
            at = (z_hi * 4 + y_at) * 128
            sums = sums + dot_nt(attended[:, at : at + 256], block)
    total[...] = sums
    for row in range(6):
        result = total[row * 24 : row * 24 + 24].astype(BF)
        out_ref[row] = result
        if row < 3:
            top_ref[row] = result
        else:
            bottom_ref[row - 3] = result
        first_ref[row] = total[row * 24 : row * 24 + 1].astype(BF)


def level_two(place, above, f, below, col, gain1, gain2, mine, others):
    return pl.pallas_call(
        level_two_kernel,
        out_shape=[
            jax.ShapeDtypeStruct((6, 24, 1024), BF),
            jax.ShapeDtypeStruct((3, 24, 1024), BF),
            jax.ShapeDtypeStruct((3, 24, 1024), BF),
            jax.ShapeDtypeStruct((6, 1, 1024), BF),
        ],
        in_specs=[SMEM] + [VMEM] * 6 + [ANY] * 10,
        out_specs=[VMEM] * 4,
        scratch_shapes=[
            pltpu.VMEM((2, 4, 8, 4, 2, 32, 128), BF),
            pltpu.VMEM((4, 8, 4, 2, 32, 128), BF),
            pltpu.VMEM((4, 8, 4, 2, 96, 128), BF),
            pltpu.VMEM((4, 12, 56, 128), F32),
            pltpu.VMEM((144, 2048), F32),
            pltpu.VMEM((144, 1024), F32),
            pltpu.VMEM((144, 3072), BF),
            pltpu.VMEM((144, 1024), BF),
            pltpu.VMEM((18, 48, 512), BF),
            pltpu.SemaphoreType.DMA((31,)),
        ],
        compiler_params=pltpu.CompilerParams(vmem_limit_bytes=32 * MIB),
        cost_estimate=pl.CostEstimate(
            flops=11_000_000_000, bytes_accessed=14_000_000, transcendentals=1_000_000
        ),
        name="level_two",
    )(place, above, f, below, col, gain1, gain2, *mine, *others)


def edges(top, bottom):
    return to_cell(bottom, 1, 0), to_cell(top, -1, 0)


def column(above, col, below, index, direction):
    part = jnp.concatenate([above[:, index], col, below[:, index]], axis=0)
    return to_cell(part, 0, direction)


def moved_rows(col, start):
    return lax.dynamic_slice_in_dim(col, start, 12, 0)


def moved_back(shift, above, grid, below, col):
    whole = jnp.concatenate([above, grid, below], axis=0)
    count = grid.shape[0]
    whole = lax.dynamic_slice_in_dim(whole, 3 - shift, count, 0)
    col = lax.dynamic_slice_in_dim(col, 3 - shift, count, 0)
    return jnp.concatenate([whole[:, 1:], col], axis=1)


def line(*values):
    values = jnp.concatenate([value.reshape(-1) for value in values])
    return jnp.pad(values, (0, 512 - values.shape[0])).reshape(1, 512)


def shards(
    latent,
    surface,
    table,
    shifts,
    gain_one,
    inward_one,
    outward_one,
    gain_ffn,
    ffn_up,
    ffn_down,
    gain_merge,
    merge_proj,
    gain_two,
    inward_two,
    outward_two,
):
    lat, lon = lax.axis_index("lat"), lax.axis_index("lon")
    shift = jnp.where(shifts[0] <= 3, shifts[0], shifts[0] - 6)
    x, y, z, core = (lon // 2) % 4, lat % 4, (lat // 4) * 4 + lon // 8, lon % 2
    place = jnp.stack([x, y, z, core, lat, shift, jnp.where(core == 0, y, x)]).astype(jnp.int32)

    classes = surface.astype(BF)

    def message(part):
        return jnp.concatenate([latent[part].reshape(-1, 512), line(classes[part])])

    above = to_cell(message(slice(9, 12)), 1, 0)

    keep, send = pack(place, merge_proj, inward_two, outward_two)
    shard = jnp.stack([keep, to_core(send)])
    near = jnp.stack([along_z(shard, 1), shard, along_z(shard, -1)])
    far_low, far_high = along_z(near, 3), along_z(near[:2], -3)
    below = to_cell(after(message(slice(0, 3)), near), -1, 0)

    cls = jnp.concatenate(
        [above[144, :144].reshape(3, 48), classes, below[144, :144].reshape(3, 48)]
    )
    left = to_cell(
        jnp.concatenate([above[47:144:48], latent[:, -1], below[47:144:48], line(cls[:, -1])]), 0, 1
    )
    cls = jnp.concatenate([left[18, :18, None], cls[:, :-1]], axis=1)
    cls = jnp.pad(moved_rows(cls, 3 + shift).astype(F32).T, ((0, 0), (0, 4)))
    block = assemble_z(place, far_low, near, far_high)
    from_left, from_right = along(block, False, 1), along(block, False, -1)
    far0, far1, left = lax.optimization_barrier(
        (along(from_left[:4], False, 1), along(from_right[4:], False, -1), left)
    )
    block = assemble(place, block, from_left, from_right, far0, far1)
    from_left, from_right = along(block, True, 1), along(block, True, -1)
    frame, top, bottom, first, last = level_one(
        place, above, latent, below, after(left, block), cls, table,
        gain_one.reshape(1, -1), gain_ffn.reshape(1, -1),
        inward_one, outward_one, ffn_up, ffn_down,
    )
    above, below = edges(top, bottom)
    from_left, from_right = lax.optimization_barrier((from_left, from_right, top))[:2]
    half0, half1, above, below = lax.optimization_barrier(
        (from_left[:2], from_right[2:], above, below)
    )
    mine = [block, from_left, from_right, along(half0, True, 1), along(half1, True, -1)]
    others = [to_core(piece) for piece in after(tuple(mine[:3]), above)]
    left = column(after(above, mine[3])[:, :, None], last, below[:, :, None], 47, 1)
    others += [to_core(piece) for piece in mine[3:]]
    level, top, bottom, ends = level_two(
        place, above, frame, below, left,
        gain_merge.reshape(1, -1), gain_two.reshape(1, -1), mine, others,
    )
    level_above, level_below = edges(top, bottom)
    right = column(
        after(above, level_above, level_below)[:, :, None], first, below[:, :, None], 0, -1
    )
    out_one = moved_back(shift, above, frame, below, right)
    right = column(level_above[:, :, None], ends, level_below[:, :, None], 0, -1)
    return out_one, moved_back(shift, level_above, level, level_below, right)


def solution(mesh):
    placed = (
        P("lat", "lon", None),
        P("lat", "lon"),
        P(),
        P(),
        P(),
        P(),
        P(),
        P(),
        P(),
        P(),
        P(),
        P("lat", "lon"),
        P(),
        P("lat", "lon"),
        P("lat", "lon"),
    )
    return jax.shard_map(
        shards,
        mesh=mesh,
        in_specs=placed,
        out_specs=(P("lat", "lon", None), P("lat", "lon", None)),
        check_vma=False,
    )
```
